32 devices in a mesh: dp: 8 (over z, y), tp: 2 (over core), wd: 2 (over x).
Axes of the slice: x: 2, y: 2, z: 4, core: 2. Of those that a mesh axis runs over, the one named last changes fastest.
Arguments:
- inputs: bfloat16 [4096, 1536], P('dp', 'wd'), may hold values from -6 to 6
- lengths: int32 [8], P('dp'), may hold values from 64 to 512
- gain_attn: float32 [1536], P('wd'), may hold values from 0.5 to 1.5
- attn_proj: bfloat16 [1536, 12, 512], P('wd', 'tp'), may hold values from -0.15625 to 0.15625
- beta_proj: bfloat16 [1536, 12], P('wd', 'tp'), may hold values from -0.15625 to 0.15625
- conv_kernel: float32 [4, 12, 128], P(None, ('tp', 'wd')), may hold values from -3 to 3
- out_proj: bfloat16 [12, 128, 1536], P('tp', None, 'wd'), may hold values from -0.625 to 0.625
- gain_ffn: float32 [1536], P('wd'), may hold values from 0.5 to 1.5
- gate_proj: bfloat16 [1536, 4096], P('wd', 'tp'), may hold values from -0.15625 to 0.15625
- up_proj: bfloat16 [1536, 4096], P('wd', 'tp'), may hold values from -0.15625 to 0.15625
- down_proj: bfloat16 [4096, 1536], P('tp', 'wd'), may hold values from -0.09375 to 0.09375
- cotangent: bfloat16 [4096, 1536], P('dp', 'wd'), may hold values from -6 to 6
Outputs:
- outputs: bfloat16 [4096, 1536], P('dp', 'wd')
- grad_inputs: bfloat16 [4096, 1536], P('dp', 'wd')
- grad_gain_attn: float32 [1536], P('wd')
- grad_attn_proj: float32 [1536, 12, 512], P('wd', 'tp')
- grad_beta_proj: float32 [1536, 12], P('wd', 'tp')
- grad_conv_kernel: float32 [4, 12, 128], P(None, ('tp', 'wd'))
- grad_out_proj: float32 [12, 128, 1536], P('tp', None, 'wd')
- grad_gain_ffn: float32 [1536], P('wd')
- grad_gate_proj: float32 [1536, 4096], P('wd', 'tp')
- grad_up_proj: float32 [1536, 4096], P('wd', 'tp')
- grad_down_proj: float32 [4096, 1536], P('tp', 'wd')
The draws below stay inside these ranges and needn't reach their ends.
All inputs are finite; a program needn't handle non-finite values.
Results may differ from the reference program's by a relative error of at most 0.023.
Values may be sent and summed in bfloat16 or wider, within the bound.
A program may use at most 192 MiB of HBM per device.

```python
import jax
import jax.numpy as jnp
from jax import lax

D = 1536
HEADS = 12
HEAD_DIM = 128
FF = 4096
KCONV = 4
LEN = 512
SEQS = 8
TOKENS = 4096


def touch_ends(values, stream_key, least, top_value):
    extent = values.shape
    index_at = [jax.random.randint(jax.random.fold_in(stream_key, axis), (), 0, extent[axis]) for axis in range(len(extent))]
    values = values.at[tuple(index_at)].set(least)
    longest = extent.index(max(extent))
    index_at[longest] = (index_at[longest] + 1) % extent[longest]
    return values.at[tuple(index_at)].set(top_value)


def steps_of(rng, extent, pieces, low, top_value):
    def one(position, blocks):
        draws = jax.random.uniform(jax.random.fold_in(jax.random.fold_in(rng, 6), position), (blocks,), jnp.float32, low / len(pieces), top_value / len(pieces))
        return jnp.repeat(jnp.exp(draws), extent[position] // blocks).reshape((-1,) + (1,) * (len(extent) - position - 1))

    level = one(*pieces[0])
    for cut in pieces[1:]:
        level = level * one(*cut)
    return level


def gaussian(rng, extent, spread, limit, cuts=(), kind=jnp.bfloat16):
    drawn = jax.random.normal(rng, extent, jnp.float32) * spread
    if len(cuts) > 0:
        drawn = steps_of(rng, extent, cuts, -0.22, 0.18) * drawn
    return jnp.clip(drawn, min=-limit, max=limit).astype(kind)


def setup_inputs(seed: int = 0) -> dict:
    streams_of = jax.random.split(jax.random.key(seed), 13)
    return {
        "inputs": gaussian(streams_of[0], (TOKENS, D), 1.0, 6.0, ((0, 8), (1, 2))),
        "lengths": touch_ends(jax.random.randint(streams_of[1], (SEQS,), LEN // 8, LEN + 1), jax.random.fold_in(streams_of[1], 1), LEN // 8, LEN).astype(jnp.int32),
        "gain_attn": jnp.clip(1.0 + 0.1 * jax.random.normal(streams_of[2], (D,), jnp.float32), 0.5, 1.5),
        "attn_proj": gaussian(streams_of[3], (D, HEADS, 4 * HEAD_DIM), D ** -0.5, 0.15625, ((0, 2), (1, 2))),
        "beta_proj": gaussian(streams_of[4], (D, HEADS), D ** -0.5, 0.15625, ((0, 2), (1, 2))),
        "conv_kernel": gaussian(streams_of[5], (KCONV, HEADS, HEAD_DIM), 0.5, 3.0, ((1, 4),), jnp.float32),
        "out_proj": gaussian(streams_of[6], (HEADS, HEAD_DIM, D), (HEADS * HEAD_DIM // 16) ** -0.5, 0.625, ((0, 2), (2, 2))),
        "gain_ffn": jnp.clip(1.0 + 0.1 * jax.random.normal(streams_of[7], (D,), jnp.float32), 0.5, 1.5),
        "gate_proj": gaussian(streams_of[8], (D, FF), D ** -0.5, 0.15625, ((0, 2), (1, 2))),
        "up_proj": gaussian(streams_of[9], (D, FF), D ** -0.5, 0.15625, ((0, 2), (1, 2))),
        "down_proj": gaussian(streams_of[10], (FF, D), FF ** -0.5, 0.09375, ((0, 2), (1, 2))),
        "cotangent": gaussian(streams_of[11], (TOKENS, D), 1.0, 6.0, ((0, 8), (1, 2))),
    }


@jax.custom_vjp
def low(v):
    return lax.optimization_barrier(v.astype(jnp.bfloat16)).astype(jnp.float32)

@jax.custom_vjp
def low_back(v):
    return v

def low_keep(v):
    return (low(v), None)

def low_pass(kept, grad):
    return (grad,)

def back_keep(v):
    return (v, None)

def back_low(kept, grad):
    return (low(grad),)
low.defvjp(low_keep, low_pass)
low_back.defvjp(back_keep, back_low)
norm_eps = 1e-06

def path_head(queries, key_rows, val_rows, mix_rows, beta_logit, kernel, length):
    seq_span = queries.shape[0]
    head_width = queries.shape[1]
    highest = lax.Precision.HIGHEST
    padded = jnp.concatenate([jnp.zeros((KCONV - 1, head_width), queries.dtype), mix_rows], 0)
    convolved = jnp.zeros_like(mix_rows)
    for offset in range(KCONV):
        convolved = convolved + kernel[offset] * padded[KCONV - 1 - offset:KCONV - 1 - offset + seq_span]
    house = convolved * lax.rsqrt(lax.optimization_barrier(jnp.sum(convolved * convolved, -1, keepdims=True)) + 1e-06)
    betas = 2.0 * jax.nn.sigmoid(beta_logit)
    places = jnp.arange(seq_span, dtype=jnp.int32)
    strict = places[:, None] > places[None, :]
    causal = places[:, None] >= places[None, :]
    system = jnp.eye(seq_span, dtype=queries.dtype) + betas[:, None] * jnp.where(strict, jnp.dot(house, house.T, precision=highest), 0.0)
    right_side = betas[:, None] * jnp.where(strict, jnp.dot(house, key_rows.T, precision=highest), 0.0)
    solved = lax.linalg.triangular_solve(system, right_side, left_side=True, lower=True, unit_diagonal=True)
    across = jnp.where(causal, jnp.dot(queries, house.T, precision=highest), 0.0)
    scores = (jnp.dot(queries, key_rows.T, precision=highest) - jnp.dot(across, solved, precision=highest)) * head_width ** (-0.5)
    allowed = causal & (places[None, :] < length)
    scores = jnp.where(allowed, scores, -1e+30)
    top_score = lax.optimization_barrier(jnp.max(scores, -1, keepdims=True))
    weights = jnp.where(allowed, jnp.exp(scores - top_score), 0.0)
    probs = low(weights / lax.optimization_barrier(jnp.sum(weights, -1, keepdims=True)))
    return jnp.dot(probs, val_rows, precision=highest)

def rms_scale(values):
    return lax.rsqrt(lax.optimization_barrier(jnp.mean(values * values, -1, keepdims=True)) + norm_eps)

def reference(inputs, lengths, gain_attn, attn_proj, beta_proj, conv_kernel, out_proj, gain_ffn, gate_proj, up_proj, down_proj, cotangent):
    highest = lax.Precision.HIGHEST

    def forward(inputs_f, gain_one, w_attn, w_beta, kernel, w_out, gain_two, w_gate, w_up, w_down):
        act_one = low(inputs_f * rms_scale(inputs_f) * gain_one)
        proj = low_back(low(jnp.einsum('td,dhe->the', act_one, w_attn, precision=highest)))
        beta_logit = low_back(jnp.dot(act_one, w_beta, precision=highest))
        proj_seq = proj.reshape(SEQS, LEN, HEADS, 4 * HEAD_DIM)
        beta_seq = beta_logit.reshape(SEQS, LEN, HEADS)
        head_map = jax.vmap(path_head, in_axes=(1, 1, 1, 1, 1, 1, None), out_axes=1)

        def one_sequence(items):
            proj_one, beta_one, length = items
            return head_map(proj_one[..., :HEAD_DIM], proj_one[..., HEAD_DIM:2 * HEAD_DIM], proj_one[..., 2 * HEAD_DIM:3 * HEAD_DIM], proj_one[..., 3 * HEAD_DIM:], beta_one, kernel, length)
        attended = lax.map(jax.checkpoint(one_sequence), (proj_seq, beta_seq, lengths))
        attended = low(attended.reshape(TOKENS, HEADS, HEAD_DIM))
        branch = low_back(jnp.einsum('the,hed->td', attended, w_out, precision=highest))
        middle = inputs_f + branch
        act_two = low(middle * rms_scale(middle) * gain_two)
        gate = low_back(jnp.dot(act_two, w_gate, precision=highest))
        up_val = low_back(jnp.dot(act_two, w_up, precision=highest))
        hidden = low(jax.nn.silu(gate) * up_val)
        feed = low_back(jnp.dot(hidden, w_down, precision=highest))
        return middle + feed
    params = (inputs.astype(jnp.float32), gain_attn, attn_proj.astype(jnp.float32), beta_proj.astype(jnp.float32), conv_kernel, out_proj.astype(jnp.float32), gain_ffn, gate_proj.astype(jnp.float32), up_proj.astype(jnp.float32), down_proj.astype(jnp.float32))
    result, pullback = jax.vjp(forward, *params)
    grads = pullback(cotangent.astype(jnp.float32))
    return (result.astype(jnp.bfloat16), grads[0].astype(jnp.bfloat16), grads[1], grads[2], grads[3], grads[4], grads[5], grads[6], grads[7], grads[8], grads[9])
```

```python
import jax
import jax.numpy as jnp
from jax import lax
from jax.experimental import pallas as pl
from jax.experimental.pallas import tpu as pltpu
from jax.sharding import PartitionSpec as P

D = 1536
norm_eps = 1e-06
KCONV = 4
HALF = 256
F32 = jnp.float32
BF16 = jnp.bfloat16
NT = (((1,), (1,)), ((), ()))
NN = (((1,), (0,)), ((), ()))


def dotb(a, b, dims=NN):
    return lax.dot_general(a, b, dims, preferred_element_type=F32)


def split(a):
    hi = a.astype(BF16)
    return hi, (a - hi.astype(F32)).astype(BF16)


def dot3(a, b, dims=NN):
    (ah, al), (bh, bl) = a, b
    return dotb(ah, bh, dims) + (dotb(al, bh, dims) + dotb(ah, bl, dims))


def shift_down(a, m):
    if m == 0:
        return a
    rows = lax.broadcasted_iota(jnp.int32, a.shape, 0)
    return jnp.where(rows >= m, pltpu.roll(a, m, 0), 0.0)


def shift_up(a, m):
    if m == 0:
        return a
    n = a.shape[0]
    rows = lax.broadcasted_iota(jnp.int32, a.shape, 0)
    return jnp.where(rows < n - m, pltpu.roll(a, n - m, 0), 0.0)


def house_of(raws, kern):
    conv = kern[0:1] * raws
    for m in range(1, KCONV):
        conv = conv + kern[m : m + 1] * shift_down(raws, m)
    scale = lax.rsqrt(jnp.sum(conv * conv, -1, keepdims=True) + 1e-06)
    return conv * scale, scale


def forward_body(len_ref, proj_ref, logit_ref, kern_ref, o_ref, x_ref, w_ref, p_ref):
    length = len_ref[0]
    hw = o_ref.shape[-1]
    q = proj_ref[:, 0:hw]
    k = proj_ref[:, hw : 2 * hw]
    v = proj_ref[:, 2 * hw : 3 * hw]
    raws = proj_ref[:, 3 * hw : 4 * hw].astype(F32)
    house, _ = house_of(raws, kern_ref[0])
    beta = 2.0 * jax.nn.sigmoid(logit_ref[0])
    hh, hl = split(house)
    top, low = slice(0, HALF), slice(HALF, 2 * HALF)
    ri = lax.broadcasted_iota(jnp.int32, (HALF, HALF), 0)
    ci = lax.broadcasted_iota(jnp.int32, (HALF, HALF), 1)
    strict = ri > ci
    causal = ri >= ci
    h_left = jnp.concatenate([hh, hl, hh], 1)
    h_right = jnp.concatenate([hh, hh, hl], 1)
    h_two = jnp.concatenate([hh, hl], 1)
    k_two = jnp.concatenate([k, k], 1)
    q_two = jnp.concatenate([q, q], 1)

    def gram(a, b):
        return dotb(h_left[a], h_right[b], NT)

    def keyed(a, b):
        return dotb(h_two[a], k_two[b], NT)

    def asked(a, b):
        return dotb(q_two[a], h_two[b], NT)

    n11 = beta[top] * jnp.where(strict, gram(top, top), 0.0)
    n22 = beta[low] * jnp.where(strict, gram(low, low), 0.0)
    n21 = split(beta[low] * gram(low, top))
    inverses = [n11, n22]
    level = 1
    xor = ri ^ ci
    bits = [split(n11), split(n22)]
    current = None
    while level < HALF:
        mask = (xor >= level) & (xor < 2 * level)
        for d in range(2):
            if level == 1:
                eye = jnp.where(ri == ci, 1.0, 0.0)
                inverses[d] = eye - jnp.where(mask, inverses[d], 0.0)
            else:
                t = split(inverses[d])
                zero = jnp.zeros((), BF16)
                c = tuple(jnp.where(mask, part, zero) for part in bits[d])
                inverses[d] = inverses[d] - dot3(t, split(dot3(c, t)))
        level *= 2
    t1, t2 = split(inverses[0]), split(inverses[1])
    b11 = split(beta[top] * jnp.where(strict, keyed(top, top), 0.0))
    b22 = split(beta[low] * jnp.where(strict, keyed(low, low), 0.0))
    b21f = beta[low] * keyed(low, top)
    b21 = split(b21f)
    m11 = split(jnp.where(causal, asked(top, top), 0.0))
    m22 = split(jnp.where(causal, asked(low, low), 0.0))
    m21 = asked(low, top)
    x11 = split(dot3(t1, b11))
    x22 = split(dot3(t2, b22))
    x21 = split(dot3(t2, split(b21f - dot3(n21, x11))))
    w11 = split(dot3(m11, t1))
    w22 = split(dot3(m22, t2))
    w21 = split(dot3(split(m21 - dot3(w22, n21)), t1))
    scale = hw ** (-0.5)

    def soften(scores, allowed):
        scores = jnp.where(allowed, scores, -1e30)
        weights = jnp.exp(scores - jnp.max(scores, -1, keepdims=True))
        return (weights * (1.0 / jnp.sum(weights, -1, keepdims=True))).astype(BF16)

    s11 = (dotb(q[top], k[top], NT) - dot3(w11, b11)) * scale
    s21 = (dotb(q[low], k[top], NT) - (dot3(w21, b11) + dot3(w22, b21))) * scale
    s22 = (dotb(q[low], k[low], NT) - dot3(w22, b22)) * scale
    p1 = soften(s11, causal & (ci < length))
    p2 = soften(
        jnp.concatenate([s21, s22], 1),
        jnp.concatenate([ci < length, causal & (ci + HALF < length)], 1),
    )
    o_ref[top, :] = dotb(p1, v[top]).astype(o_ref.dtype)
    o_ref[low, :] = dotb(p2, v).astype(o_ref.dtype)
    p_ref[0, 0] = p1
    p_ref[0, 1] = p2[:, :HALF]
    p_ref[0, 2] = p2[:, HALF:]
    for i, (xx, ww) in enumerate(((x11, w11), (x21, w21), (x22, w22))):
        for j in range(2):
            x_ref[0, i, j] = xx[j]
            w_ref[0, i, j] = ww[j].T


def backward_body(proj_ref, logit_ref, kern_ref, g_ref, x_ref, w_ref, p_ref, dproj_ref, dlogit_ref, dkern_ref):
    hw = g_ref.shape[-1]
    q = proj_ref[:, 0:hw]
    k = proj_ref[:, hw : 2 * hw]
    v = proj_ref[:, 2 * hw : 3 * hw]
    raws = proj_ref[:, 3 * hw : 4 * hw].astype(F32)
    kern = kern_ref[0]
    house, rs = house_of(raws, kern)
    beta = 2.0 * jax.nn.sigmoid(logit_ref[0])
    g = g_ref[...]
    hh, hl = split(house)
    top, low = slice(0, HALF), slice(HALF, 2 * HALF)
    ri = lax.broadcasted_iota(jnp.int32, (HALF, HALF), 0)
    ci = lax.broadcasted_iota(jnp.int32, (HALF, HALF), 1)
    strict = ri > ci
    causal = ri >= ci
    scale = hw ** (-0.5)
    p11, p21, p22 = (p_ref[0, i] for i in range(3))
    x11, x21, x22 = ((x_ref[0, i, 0], x_ref[0, i, 1]) for i in range(3))
    w11, w21, w22 = ((w_ref[0, i, 0], w_ref[0, i, 1]) for i in range(3))
    q_t, g_t = q.T, g.T
    ht_h, ht_l = hh.T, hl.T

    def soften_back(probs, dprobs):
        pf = probs.astype(F32)
        mixed = pf * dprobs
        return (mixed - pf * jnp.sum(mixed, -1, keepdims=True)) * scale

    z1 = soften_back(p11, dotb(g[top], v[top], NT))
    z2 = soften_back(jnp.concatenate([p21, p22], 1), dotb(g[low], v, NT))
    z11 = split(z1)
    z21 = split(z2[:, :HALF])
    z22 = split(z2[:, HALF:])
    u11 = jnp.where(causal, dot3(z11, x11, NT), 0.0)
    u21 = dot3(z21, x11, NT)
    u22 = jnp.where(causal, dot3(z21, x21, NT) + dot3(z22, x22, NT), 0.0)
    u11, u21, u22 = split(u11), split(u21), split(u22)
    b11 = jnp.where(strict, dot3(w11, z11) + dot3(w21, z21), 0.0)
    b21 = dot3(w22, z21)
    b22 = jnp.where(strict, dot3(w22, z22), 0.0)
    a11 = jnp.where(strict, dot3(w11, u11) + dot3(w21, u21), 0.0)
    a21 = dot3(w22, u21)
    a22 = jnp.where(strict, dot3(w22, u22), 0.0)
    b11s, b21s, b22s = split(b11), split(b21), split(b22)
    a11s, a21s, a22s = split(a11), split(a21), split(a22)

    def rows(c11, c21, c22, mats):
        (mh, ml) = mats
        first = dotb(c11[0], mh[top]) + dotb(c11[1], mh[top])
        second = dotb(c21[0], mh[top]) + dotb(c21[1], mh[top])
        second = second + dotb(c22[0], mh[low]) + dotb(c22[1], mh[low])
        if ml is not None:
            first = first + dotb(c11[0], ml[top])
            second = second + dotb(c21[0], ml[top]) + dotb(c22[0], ml[low])
        return jnp.concatenate([first, second], 0)

    def cols(c11, c21, c22, mats):
        (mh, ml) = mats
        first = dotb(mh[:, top], c11[0]) + dotb(mh[:, top], c11[1])
        first = first + dotb(mh[:, low], c21[0]) + dotb(mh[:, low], c21[1])
        second = dotb(mh[:, low], c22[0]) + dotb(mh[:, low], c22[1])
        if ml is not None:
            first = first + dotb(ml[:, top], c11[0]) + dotb(ml[:, low], c21[0])
            second = second + dotb(ml[:, low], c22[0])
        return jnp.concatenate([first, second], 1)

    dq = rows(z11, z21, z22, (k, None)) - rows(u11, u21, u22, (hh, hl))
    bk = rows(b11s, b21s, b22s, (k, None))
    nh = rows(a11s, a21s, a22s, (hh, hl))
    mixed = nh - bk
    dbeta = jnp.sum(house * mixed, -1, keepdims=True)
    dlogit_ref[0] = dbeta * beta * (1.0 - 0.5 * beta)
    bb = [split(beta[s] * b) for s, b in ((top, b11), (low, b21), (low, b22))]
    ab = [split(beta[s] * a) for s, a in ((top, a11), (low, a21), (low, a22))]
    dk_t = cols(z11, z21, z22, (q_t, None)) - cols(*bb, (ht_h, ht_l))
    dh_t = cols(*ab, (ht_h, ht_l)) - cols(u11, u21, u22, (q_t, None))
    dv_t = jnp.concatenate(
        [dotb(g_t[:, top], p11) + dotb(g_t[:, low], p21), dotb(g_t[:, low], p22)], 1
    )
    dh = beta * mixed + dh_t.T
    dc = rs * (dh - house * jnp.sum(house * dh, -1, keepdims=True))
    dr = kern[0:1] * dc
    taps = [jnp.sum(dc * raws, 0, keepdims=True)]
    for m in range(1, KCONV):
        up = shift_up(dc, m)
        dr = dr + kern[m : m + 1] * up
        taps.append(jnp.sum(up * raws, 0, keepdims=True))
    dkern_ref[0] = jnp.concatenate(taps, 0)
    dproj_ref[:, 0:hw] = dq.astype(BF16)
    dproj_ref[:, hw : 2 * hw] = dk_t.T.astype(BF16)
    dproj_ref[:, 2 * hw : 3 * hw] = dv_t.T.astype(BF16)
    dproj_ref[:, 3 * hw : 4 * hw] = dr.astype(BF16)


def attend_forward(proj, logit, kern, lengths):
    heads, span = logit.shape[0], logit.shape[1]
    hw = kern.shape[-1]
    head3 = lambda h: (h, 0, 0)
    kept = (heads, 3, 2, HALF, HALF)
    return pl.pallas_call(
        forward_body,
        grid=(heads,),
        in_specs=[
            pl.BlockSpec(memory_space=pltpu.SMEM),
            pl.BlockSpec((span, 4 * hw), lambda h: (0, h)),
            pl.BlockSpec((1, span, 1), head3),
            pl.BlockSpec((1, KCONV, hw), head3),
        ],
        out_specs=[
            pl.BlockSpec((span, hw), lambda h: (0, h)),
            pl.BlockSpec((1,) + kept[1:], lambda h: (h, 0, 0, 0, 0)),
            pl.BlockSpec((1,) + kept[1:], lambda h: (h, 0, 0, 0, 0)),
            pl.BlockSpec((1, 3, HALF, HALF), lambda h: (h, 0, 0, 0)),
        ],
        out_shape=[
            jax.ShapeDtypeStruct((span, heads * hw), BF16),
            jax.ShapeDtypeStruct(kept, BF16),
            jax.ShapeDtypeStruct(kept, BF16),
            jax.ShapeDtypeStruct((heads, 3, HALF, HALF), BF16),
        ],
        compiler_params=pltpu.CompilerParams(vmem_limit_bytes=40 * 2**20),
        cost_estimate=pl.CostEstimate(flops=12_000_000_000, bytes_accessed=8_000_000, transcendentals=0),
        name="attend_forward",
    )(lengths, proj, logit, kern)


def attend_backward(proj, logit, kern, grad, kept_x, kept_w, kept_p):
    heads, span = logit.shape[0], logit.shape[1]
    hw = kern.shape[-1]
    head3 = lambda h: (h, 0, 0)
    kept = kept_x.shape
    return pl.pallas_call(
        backward_body,
        grid=(heads,),
        in_specs=[
            pl.BlockSpec((span, 4 * hw), lambda h: (0, h)),
            pl.BlockSpec((1, span, 1), head3),
            pl.BlockSpec((1, KCONV, hw), head3),
            pl.BlockSpec((span, hw), lambda h: (0, h)),
            pl.BlockSpec((1,) + kept[1:], lambda h: (h, 0, 0, 0, 0)),
            pl.BlockSpec((1,) + kept[1:], lambda h: (h, 0, 0, 0, 0)),
            pl.BlockSpec((1, 3, HALF, HALF), lambda h: (h, 0, 0, 0)),
        ],
        out_specs=[
            pl.BlockSpec((span, 4 * hw), lambda h: (0, h)),
            pl.BlockSpec((1, span, 1), head3),
            pl.BlockSpec((1, KCONV, hw), head3),
        ],
        out_shape=[
            jax.ShapeDtypeStruct((span, heads * 4 * hw), BF16),
            jax.ShapeDtypeStruct((heads, span, 1), F32),
            jax.ShapeDtypeStruct((heads, KCONV, hw), F32),
        ],
        compiler_params=pltpu.CompilerParams(vmem_limit_bytes=40 * 2**20),
        cost_estimate=pl.CostEstimate(flops=12_000_000_000, bytes_accessed=8_000_000, transcendentals=0),
        name="attend_backward",
    )(proj, logit, kern, grad, kept_x, kept_w, kept_p)


def on_device(
    inputs,
    lengths,
    gain_attn,
    attn_proj,
    beta_proj,
    conv_kernel,
    out_proj,
    gain_ffn,
    gate_proj,
    up_proj,
    down_proj,
    cotangent,
):
    tok_rows = inputs.shape[0]
    seq_count = lengths.shape[0]
    seq_span = tok_rows // seq_count
    head_local = conv_kernel.shape[1]
    head_width = conv_kernel.shape[2]

    def row_total(values):
        return lax.psum(values, "wd")

    def width_total(values):
        return lax.psum(values.astype(jnp.bfloat16), "tp").astype(jnp.float32)

    inputs_f = inputs.astype(jnp.float32)
    rinv_one = lax.rsqrt(row_total(jnp.sum(inputs_f * inputs_f, -1)) / D + norm_eps)
    act_one = (inputs_f * rinv_one[:, None] * gain_attn).astype(jnp.bfloat16)
    w_attn, w_beta, w_gate, w_up, w_out, w_down = (
        attn_proj,
        beta_proj,
        gate_proj,
        up_proj,
        out_proj,
        down_proj,
    )
    part_proj = jnp.einsum("td,dhe->the", act_one, attn_proj, preferred_element_type=jnp.float32)
    part_beta = jnp.dot(act_one, beta_proj, preferred_element_type=jnp.float32)
    proj_sum, beta_logit = (
        lax.psum_scatter(part_proj, "wd", scatter_dimension=1, tiled=True),
        lax.psum_scatter(part_beta, "wd", scatter_dimension=1, tiled=True),
    )
    proj_own = proj_sum.astype(jnp.bfloat16).reshape(tok_rows, -1)
    kern_own = jnp.transpose(conv_kernel, (1, 0, 2))
    logit_own = jnp.transpose(beta_logit, (1, 0))[..., None]
    parts = []
    for seq in range(seq_count):
        rows = slice(seq * seq_span, (seq + 1) * seq_span)
        parts.append(
            attend_forward(
                proj_own[rows], logit_own[:, rows], kern_own, lengths[seq : seq + 1]
            )
        )
    heads_own = jnp.concatenate([part[0] for part in parts], 0)
    heads_own = heads_own.reshape(tok_rows, head_local, head_width)
    heads_src = lax.all_gather(heads_own, "wd", axis=1, tiled=True)
    branch_part = jnp.einsum("the,hed->td", heads_src, w_out, preferred_element_type=jnp.float32)
    branch = width_total(branch_part)
    middle = inputs_f + branch
    rinv_two = lax.rsqrt(row_total(jnp.sum(middle * middle, -1)) / D + norm_eps)
    act_two = (middle * rinv_two[:, None] * gain_ffn).astype(jnp.bfloat16)
    gate_part = jnp.dot(act_two, gate_proj, preferred_element_type=jnp.float32)
    up_part = jnp.dot(act_two, up_proj, preferred_element_type=jnp.float32)
    gate_sum, up_sum = (
        lax.psum_scatter(
            gate_part.astype(jnp.bfloat16), "wd", scatter_dimension=1, tiled=True
        ).astype(jnp.float32),
        lax.psum_scatter(
            up_part.astype(jnp.bfloat16), "wd", scatter_dimension=1, tiled=True
        ).astype(jnp.float32),
    )
    hidden_own = (jax.nn.silu(gate_sum) * up_sum).astype(jnp.bfloat16)
    hidden_all = lax.all_gather(hidden_own, "wd", axis=1, tiled=True)
    feed_part = jnp.dot(hidden_all, down_proj, preferred_element_type=jnp.float32)
    feed = width_total(feed_part)
    outputs = (middle + feed).astype(jnp.bfloat16)
    cot_f = cotangent.astype(jnp.float32)
    grad_down = jnp.einsum("tf,td->fd", hidden_all, cotangent, preferred_element_type=jnp.float32)
    hidden_part = jnp.einsum("td,fd->tf", cotangent, down_proj, preferred_element_type=jnp.float32)
    hidden_grad = lax.psum_scatter(
        hidden_part.astype(jnp.bfloat16), "wd", scatter_dimension=1, tiled=True
    ).astype(jnp.float32)
    sigma = jax.nn.sigmoid(gate_sum)
    gate_grad = (hidden_grad * up_sum * sigma * (1.0 + gate_sum * (1.0 - sigma))).astype(
        jnp.bfloat16
    )
    up_grad = (hidden_grad * gate_sum * sigma).astype(jnp.bfloat16)
    gate_all, up_all = (
        lax.all_gather(gate_grad, "wd", axis=1, tiled=True),
        lax.all_gather(up_grad, "wd", axis=1, tiled=True),
    )
    grad_gate = jnp.einsum("td,tf->df", act_two, gate_all, preferred_element_type=jnp.float32)
    grad_up = jnp.einsum("td,tf->df", act_two, up_all, preferred_element_type=jnp.float32)
    two_part = jnp.einsum("tf,df->td", gate_all, w_gate, preferred_element_type=jnp.float32)
    two_part = two_part + jnp.einsum("tf,df->td", up_all, w_up, preferred_element_type=jnp.float32)
    act_two_grad = width_total(two_part)
    grad_gain_two = jnp.sum(act_two_grad * middle * rinv_two[:, None], 0)
    cross_two = row_total(jnp.sum(act_two_grad * gain_ffn * middle, -1))
    cube_two = rinv_two * rinv_two * rinv_two * cross_two / D
    middle_grad = cot_f + act_two_grad * gain_ffn * rinv_two[:, None] - middle * cube_two[:, None]
    branch_grad = middle_grad.astype(jnp.bfloat16)
    grad_out = jnp.einsum("the,td->hed", heads_src, branch_grad, preferred_element_type=jnp.float32)
    heads_part = jnp.einsum("td,hed->the", branch_grad, w_out, preferred_element_type=jnp.float32)
    heads_grad = lax.psum_scatter(
        heads_part.astype(jnp.bfloat16), "wd", scatter_dimension=1, tiled=True
    )
    heads_grad = heads_grad.reshape(tok_rows, -1)
    backs = []
    for seq in range(seq_count):
        rows = slice(seq * seq_span, (seq + 1) * seq_span)
        backs.append(
            attend_backward(
                proj_own[rows], logit_own[:, rows], kern_own, heads_grad[rows], *parts[seq][1:]
            )
        )
    proj_low = jnp.concatenate([back[0] for back in backs], 0)
    proj_low = proj_low.reshape(tok_rows, head_local, 4 * head_width)
    beta_low = jnp.concatenate([back[1] for back in backs], 1)[..., 0].T.astype(jnp.bfloat16)
    grad_kernel = jnp.transpose(sum(back[2] for back in backs), (1, 0, 2))
    proj_all, beta_all = (
        lax.all_gather(proj_low, "wd", axis=1, tiled=True),
        lax.all_gather(beta_low, "wd", axis=1, tiled=True),
    )
    grad_attn = jnp.einsum("td,the->dhe", act_one, proj_all, preferred_element_type=jnp.float32)
    grad_beta = jnp.einsum("td,th->dh", act_one, beta_all, preferred_element_type=jnp.float32)
    one_part = jnp.einsum("the,dhe->td", proj_all, w_attn, preferred_element_type=jnp.float32)
    one_part = one_part + jnp.einsum(
        "th,dh->td", beta_all, w_beta, preferred_element_type=jnp.float32
    )
    act_one_grad = width_total(one_part)
    grad_gain_one = jnp.sum(act_one_grad * inputs_f * rinv_one[:, None], 0)
    cross_one = row_total(jnp.sum(act_one_grad * gain_attn * inputs_f, -1))
    cube_one = rinv_one * rinv_one * rinv_one * cross_one / D
    input_grad = (
        middle_grad + act_one_grad * gain_attn * rinv_one[:, None] - inputs_f * cube_one[:, None]
    )
    summed = (
        lax.psum(grad_gain_one.astype(jnp.bfloat16), "dp").astype(jnp.float32),
        lax.psum(grad_attn.astype(jnp.bfloat16), "dp").astype(jnp.float32),
        lax.psum(grad_beta.astype(jnp.bfloat16), "dp").astype(jnp.float32),
        lax.psum(grad_kernel.astype(jnp.bfloat16), "dp").astype(jnp.float32),
        lax.psum(grad_out.astype(jnp.bfloat16), "dp").astype(jnp.float32),
        lax.psum(grad_gain_two.astype(jnp.bfloat16), "dp").astype(jnp.float32),
        lax.psum(grad_gate.astype(jnp.bfloat16), "dp").astype(jnp.float32),
        lax.psum(grad_up.astype(jnp.bfloat16), "dp").astype(jnp.float32),
        lax.psum(grad_down.astype(jnp.bfloat16), "dp").astype(jnp.float32),
    )
    total_attn, total_beta, total_gate, total_up = (summed[1], summed[2], summed[6], summed[7])
    total_out, total_down = (summed[4], summed[8])
    return (
        outputs,
        input_grad.astype(jnp.bfloat16),
        summed[0],
        total_attn,
        total_beta,
        summed[3],
        total_out,
        summed[5],
        total_gate,
        total_up,
        total_down,
    )


def solution(mesh):
    return jax.shard_map(
        on_device,
        mesh=mesh,
        in_specs=(
            P("dp", "wd"),
            P("dp"),
            P("wd"),
            P("wd", "tp", None),
            P("wd", "tp"),
            P(None, ("tp", "wd"), None),
            P("tp", None, "wd"),
            P("wd"),
            P("wd", "tp"),
            P("wd", "tp"),
            P("tp", "wd"),
            P("dp", "wd"),
        ),
        out_specs=(
            P("dp", "wd"),
            P("dp", "wd"),
            P("wd"),
            P("wd", "tp", None),
            P("wd", "tp"),
            P(None, ("tp", "wd"), None),
            P("tp", None, "wd"),
            P("wd"),
            P("wd", "tp"),
            P("wd", "tp"),
            P("tp", "wd"),
        ),
        check_vma=False,
    )
```

```python
import functools

import jax
import jax.numpy as jnp
from jax import lax
from jax.experimental import pallas as pl
from jax.experimental.pallas import tpu as pltpu
from jax.sharding import PartitionSpec as P

norm_eps = 1e-06
KCONV = 4
HALF = 256
F32 = jnp.float32
BF16 = jnp.bfloat16
NT = (((1,), (1,)), ((), ()))
NN = (((1,), (0,)), ((), ()))


def dotb(a, b, dims=NN):
    return lax.dot_general(a, b, dims, preferred_element_type=F32)


def split(a):
    hi = a.astype(BF16)
    return hi, (a - hi.astype(F32)).astype(BF16)


def dot3(a, b, dims=NN):
    (ah, al), (bh, bl) = a, b
    return dotb(ah, bh, dims) + (dotb(al, bh, dims) + dotb(ah, bl, dims))


def shift_down(a, m):
    if m == 0:
        return a
    rows = lax.broadcasted_iota(jnp.int32, a.shape, 0)
    return jnp.where(rows >= m, pltpu.roll(a, m, 0), 0.0)


def shift_up(a, m):
    if m == 0:
        return a
    n = a.shape[0]
    rows = lax.broadcasted_iota(jnp.int32, a.shape, 0)
    return jnp.where(rows < n - m, pltpu.roll(a, n - m, 0), 0.0)


def house_of(raws, kern):
    conv = kern[0:1] * raws
    for m in range(1, KCONV):
        conv = conv + kern[m : m + 1] * shift_down(raws, m)
    scale = lax.rsqrt(jnp.sum(conv * conv, -1, keepdims=True) + 1e-06)
    return conv * scale, scale


def forward_body(len_ref, proj_ref, logit_ref, kern_ref, o_ref, x_ref, w_ref, p_ref):
    length = len_ref[0]
    hw = o_ref.shape[-1]
    q = proj_ref[:, 0:hw]
    k = proj_ref[:, hw : 2 * hw]
    v = proj_ref[:, 2 * hw : 3 * hw]
    raws = proj_ref[:, 3 * hw : 4 * hw].astype(F32)
    house, _ = house_of(raws, kern_ref[0])
    beta = 2.0 * jax.nn.sigmoid(logit_ref[0])
    hh, hl = split(house)
    top, low = slice(0, HALF), slice(HALF, 2 * HALF)
    ri = lax.broadcasted_iota(jnp.int32, (HALF, HALF), 0)
    ci = lax.broadcasted_iota(jnp.int32, (HALF, HALF), 1)
    strict = ri > ci
    causal = ri >= ci
    h_left = jnp.concatenate([hh, hl, hh], 1)
    h_right = jnp.concatenate([hh, hh, hl], 1)
    h_two = jnp.concatenate([hh, hl], 1)
    k_two = jnp.concatenate([k, k], 1)
    q_two = jnp.concatenate([q, q], 1)

    def gram(a, b):
        return dotb(h_left[a], h_right[b], NT)

    def keyed(a, b):
        return dotb(h_two[a], k_two[b], NT)

    def asked(a, b):
        return dotb(q_two[a], h_two[b], NT)

    n11 = beta[top] * jnp.where(strict, gram(top, top), 0.0)
    n22 = beta[low] * jnp.where(strict, gram(low, low), 0.0)
    n21 = split(beta[low] * gram(low, top))
    inverses = [n11, n22]
    level = 1
    xor = ri ^ ci
    bits = [split(n11), split(n22)]
    current = None
    while level < HALF:
        mask = (xor >= level) & (xor < 2 * level)
        for d in range(2):
            if level == 1:
                eye = jnp.where(ri == ci, 1.0, 0.0)
                inverses[d] = eye - jnp.where(mask, inverses[d], 0.0)
            else:
                t = split(inverses[d])
                zero = jnp.zeros((), BF16)
                c = tuple(jnp.where(mask, part, zero) for part in bits[d])
                inverses[d] = inverses[d] - dot3(t, split(dot3(c, t)))
        level *= 2
    t1, t2 = split(inverses[0]), split(inverses[1])
    b11 = split(beta[top] * jnp.where(strict, keyed(top, top), 0.0))
    b22 = split(beta[low] * jnp.where(strict, keyed(low, low), 0.0))
    b21f = beta[low] * keyed(low, top)
    b21 = split(b21f)
    m11 = split(jnp.where(causal, asked(top, top), 0.0))
    m22 = split(jnp.where(causal, asked(low, low), 0.0))
    m21 = asked(low, top)
    x11 = split(dot3(t1, b11))
    x22 = split(dot3(t2, b22))
    x21 = split(dot3(t2, split(b21f - dot3(n21, x11))))
    w11 = split(dot3(m11, t1))
    w22 = split(dot3(m22, t2))
    w21 = split(dot3(split(m21 - dot3(w22, n21)), t1))
    scale = hw ** (-0.5)

    def soften(scores, allowed):
        scores = jnp.where(allowed, scores, -1e30)
        weights = jnp.exp(scores - jnp.max(scores, -1, keepdims=True))
        return (weights * (1.0 / jnp.sum(weights, -1, keepdims=True))).astype(BF16)

    s11 = (dotb(q[top], k[top], NT) - dot3(w11, b11)) * scale
    s21 = (dotb(q[low], k[top], NT) - (dot3(w21, b11) + dot3(w22, b21))) * scale
    s22 = (dotb(q[low], k[low], NT) - dot3(w22, b22)) * scale
    p1 = soften(s11, causal & (ci < length))
    p2 = soften(
        jnp.concatenate([s21, s22], 1),
        jnp.concatenate([ci < length, causal & (ci + HALF < length)], 1),
    )
    o_ref[top, :] = dotb(p1, v[top]).astype(o_ref.dtype)
    o_ref[low, :] = dotb(p2, v).astype(o_ref.dtype)
    p_ref[0, 0] = p1
    p_ref[0, 1] = p2[:, :HALF]
    p_ref[0, 2] = p2[:, HALF:]
    for i, (xx, ww) in enumerate(((x11, w11), (x21, w21), (x22, w22))):
        for j in range(2):
            x_ref[0, i, j] = xx[j]
            w_ref[0, i, j] = ww[j].T


def backward_body(proj_ref, logit_ref, kern_ref, g_ref, x_ref, w_ref, p_ref, dproj_ref, dlogit_ref, dkern_ref):
    hw = g_ref.shape[-1]
    q = proj_ref[:, 0:hw]
    k = proj_ref[:, hw : 2 * hw]
    v = proj_ref[:, 2 * hw : 3 * hw]
    raws = proj_ref[:, 3 * hw : 4 * hw].astype(F32)
    kern = kern_ref[0]
    house, rs = house_of(raws, kern)
    beta = 2.0 * jax.nn.sigmoid(logit_ref[0])
    g = g_ref[...]
    hh, hl = split(house)
    top, low = slice(0, HALF), slice(HALF, 2 * HALF)
    ri = lax.broadcasted_iota(jnp.int32, (HALF, HALF), 0)
    ci = lax.broadcasted_iota(jnp.int32, (HALF, HALF), 1)
    strict = ri > ci
    causal = ri >= ci
    scale = hw ** (-0.5)
    p11, p21, p22 = (p_ref[0, i] for i in range(3))
    x11, x21, x22 = ((x_ref[0, i, 0], x_ref[0, i, 1]) for i in range(3))
    w11, w21, w22 = ((w_ref[0, i, 0], w_ref[0, i, 1]) for i in range(3))
    q_t, g_t = q.T, g.T
    ht_h, ht_l = hh.T, hl.T

    def soften_back(probs, dprobs):
        pf = probs.astype(F32)
        mixed = pf * dprobs
        return (mixed - pf * jnp.sum(mixed, -1, keepdims=True)) * scale

    z1 = soften_back(p11, dotb(g[top], v[top], NT))
    z2 = soften_back(jnp.concatenate([p21, p22], 1), dotb(g[low], v, NT))
    z11 = split(z1)
    z21 = split(z2[:, :HALF])
    z22 = split(z2[:, HALF:])
    u11 = jnp.where(causal, dot3(z11, x11, NT), 0.0)
    u21 = dot3(z21, x11, NT)
    u22 = jnp.where(causal, dot3(z21, x21, NT) + dot3(z22, x22, NT), 0.0)
    u11, u21, u22 = split(u11), split(u21), split(u22)
    b11 = jnp.where(strict, dot3(w11, z11) + dot3(w21, z21), 0.0)
    b21 = dot3(w22, z21)
    b22 = jnp.where(strict, dot3(w22, z22), 0.0)
    a11 = jnp.where(strict, dot3(w11, u11) + dot3(w21, u21), 0.0)
    a21 = dot3(w22, u21)
    a22 = jnp.where(strict, dot3(w22, u22), 0.0)
    b11s, b21s, b22s = split(b11), split(b21), split(b22)
    a11s, a21s, a22s = split(a11), split(a21), split(a22)

    def rows(c11, c21, c22, mats):
        (mh, ml) = mats
        first = dotb(c11[0], mh[top]) + dotb(c11[1], mh[top])
        second = dotb(c21[0], mh[top]) + dotb(c21[1], mh[top])
        second = second + dotb(c22[0], mh[low]) + dotb(c22[1], mh[low])
        if ml is not None:
            first = first + dotb(c11[0], ml[top])
            second = second + dotb(c21[0], ml[top]) + dotb(c22[0], ml[low])
        return jnp.concatenate([first, second], 0)

    def cols(c11, c21, c22, mats):
        (mh, ml) = mats
        first = dotb(mh[:, top], c11[0]) + dotb(mh[:, top], c11[1])
        first = first + dotb(mh[:, low], c21[0]) + dotb(mh[:, low], c21[1])
        second = dotb(mh[:, low], c22[0]) + dotb(mh[:, low], c22[1])
        if ml is not None:
            first = first + dotb(ml[:, top], c11[0]) + dotb(ml[:, low], c21[0])
            second = second + dotb(ml[:, low], c22[0])
        return jnp.concatenate([first, second], 1)

    dq = rows(z11, z21, z22, (k, None)) - rows(u11, u21, u22, (hh, hl))
    bk = rows(b11s, b21s, b22s, (k, None))
    nh = rows(a11s, a21s, a22s, (hh, hl))
    mixed = nh - bk
    dbeta = jnp.sum(house * mixed, -1, keepdims=True)
    dlogit_ref[0] = dbeta * beta * (1.0 - 0.5 * beta)
    bb = [split(beta[s] * b) for s, b in ((top, b11), (low, b21), (low, b22))]
    ab = [split(beta[s] * a) for s, a in ((top, a11), (low, a21), (low, a22))]
    dk_t = cols(z11, z21, z22, (q_t, None)) - cols(*bb, (ht_h, ht_l))
    dh_t = cols(*ab, (ht_h, ht_l)) - cols(u11, u21, u22, (q_t, None))
    dv_t = jnp.concatenate(
        [dotb(g_t[:, top], p11) + dotb(g_t[:, low], p21), dotb(g_t[:, low], p22)], 1
    )
    dh = beta * mixed + dh_t.T
    dc = rs * (dh - house * jnp.sum(house * dh, -1, keepdims=True))
    dr = kern[0:1] * dc
    taps = [jnp.sum(dc * raws, 0, keepdims=True)]
    for m in range(1, KCONV):
        up = shift_up(dc, m)
        dr = dr + kern[m : m + 1] * up
        taps.append(jnp.sum(up * raws, 0, keepdims=True))
    dkern_ref[0] = jnp.concatenate(taps, 0)
    dproj_ref[:, 0:hw] = dq.astype(BF16)
    dproj_ref[:, hw : 2 * hw] = dk_t.T.astype(BF16)
    dproj_ref[:, 2 * hw : 3 * hw] = dv_t.T.astype(BF16)
    dproj_ref[:, 3 * hw : 4 * hw] = dr.astype(BF16)


def attend_forward(proj, logit, kern, lengths):
    heads, span = logit.shape[0], logit.shape[1]
    hw = kern.shape[-1]
    head3 = lambda h: (h, 0, 0)
    kept = (heads, 3, 2, HALF, HALF)
    return pl.pallas_call(
        forward_body,
        grid=(heads,),
        in_specs=[
            pl.BlockSpec(memory_space=pltpu.SMEM),
            pl.BlockSpec((span, 4 * hw), lambda h: (0, h)),
            pl.BlockSpec((1, span, 1), head3),
            pl.BlockSpec((1, KCONV, hw), head3),
        ],
        out_specs=[
            pl.BlockSpec((span, hw), lambda h: (0, h)),
            pl.BlockSpec((1,) + kept[1:], lambda h: (h, 0, 0, 0, 0)),
            pl.BlockSpec((1,) + kept[1:], lambda h: (h, 0, 0, 0, 0)),
            pl.BlockSpec((1, 3, HALF, HALF), lambda h: (h, 0, 0, 0)),
        ],
        out_shape=[
            jax.ShapeDtypeStruct((span, heads * hw), BF16),
            jax.ShapeDtypeStruct(kept, BF16),
            jax.ShapeDtypeStruct(kept, BF16),
            jax.ShapeDtypeStruct((heads, 3, HALF, HALF), BF16),
        ],
        compiler_params=pltpu.CompilerParams(vmem_limit_bytes=40 * 2**20),
        cost_estimate=pl.CostEstimate(flops=12_000_000_000, bytes_accessed=8_000_000, transcendentals=0),
        name="attend_forward",
    )(lengths, proj, logit, kern)


def attend_backward(proj, logit, kern, grad, kept_x, kept_w, kept_p):
    heads, span = logit.shape[0], logit.shape[1]
    hw = kern.shape[-1]
    head3 = lambda h: (h, 0, 0)
    kept = kept_x.shape
    return pl.pallas_call(
        backward_body,
        grid=(heads,),
        in_specs=[
            pl.BlockSpec((span, 4 * hw), lambda h: (0, h)),
            pl.BlockSpec((1, span, 1), head3),
            pl.BlockSpec((1, KCONV, hw), head3),
            pl.BlockSpec((span, hw), lambda h: (0, h)),
            pl.BlockSpec((1,) + kept[1:], lambda h: (h, 0, 0, 0, 0)),
            pl.BlockSpec((1,) + kept[1:], lambda h: (h, 0, 0, 0, 0)),
            pl.BlockSpec((1, 3, HALF, HALF), lambda h: (h, 0, 0, 0)),
        ],
        out_specs=[
            pl.BlockSpec((span, 4 * hw), lambda h: (0, h)),
            pl.BlockSpec((1, span, 1), head3),
            pl.BlockSpec((1, KCONV, hw), head3),
        ],
        out_shape=[
            jax.ShapeDtypeStruct((span, heads * 4 * hw), BF16),
            jax.ShapeDtypeStruct((heads, span, 1), F32),
            jax.ShapeDtypeStruct((heads, KCONV, hw), F32),
        ],
        compiler_params=pltpu.CompilerParams(vmem_limit_bytes=40 * 2**20),
        cost_estimate=pl.CostEstimate(flops=12_000_000_000, bytes_accessed=8_000_000, transcendentals=0),
        name="attend_backward",
    )(proj, logit, kern, grad, kept_x, kept_w, kept_p)


MESH = pl.DeviceIdType.MESH


def own_bits(bits):
    group = lax.axis_index("dp")
    return group, [lax.rem(lax.div(group, 1 << b), 2) for b in range(bits)]


class Reduce:
    def __init__(self, order, rows, columns, peer):
        self.order, self.rows, self.columns, self.peer = order, rows, columns, peer
        self.bits = len(order)

    def scratch(self):
        block = (self.rows, self.columns)
        shapes = [pltpu.VMEM((2,) * (self.bits - 1 - k) + block, BF16) for k in range(self.bits)]
        shapes += [pltpu.VMEM((2,) * (self.bits - 1 - k) + block, BF16) for k in range(1, self.bits)]
        shapes += [pltpu.VMEM(block, BF16)]
        if self.peer:
            shapes += [pltpu.VMEM(block, BF16)]
        count = 2 * self.bits + 1
        return shapes + [pltpu.SemaphoreType.DMA((count,)), pltpu.SemaphoreType.DMA((count + 1,))]

    def bind(self, group, bit_of, source, out, refs):
        self.group, self.bit_of, self.source, self.out = group, bit_of, source, out
        refs = list(refs)
        self.recv = [refs.pop(0) for _ in range(self.bits)]
        self.send = [None] + [refs.pop(0) for _ in range(1, self.bits)]
        self.shard = refs.pop(0)
        self.from_peer = refs.pop(0) if self.peer else None
        self.send_sem, self.recv_sem = refs
        stages = [functools.partial(self.halve, k) for k in range(self.bits)] + [self.finish]
        if self.peer:
            stages.append(self.take_peer)
        stages += [functools.partial(self.double, k) for k in range(1, self.bits)] + [self.end]
        self.stages = stages
        self.copies = {}
        return self

    def at(self, fixed, gone=()):
        return tuple(
            fixed.get(b, slice(None)) for b in range(self.bits - 1, -1, -1) if b not in gone
        )

    def remote(self, key, slot, source, target, bit=None):
        if bit is None:
            device = {"wd": 1 - lax.axis_index("wd")}
        else:
            step = 1 << bit
            device = {"dp": self.group + step - 2 * step * self.bit_of[bit]}
        copy = pltpu.make_async_remote_copy(
            src_ref=source,
            dst_ref=target,
            send_sem=self.send_sem.at[slot],
            recv_sem=self.recv_sem.at[slot],
            device_id=device,
            device_id_type=MESH,
        )
        copy.start()
        self.copies[key] = copy

    def total(self, step, fixed, target):
        free = [b for b in range(self.bits - 1, -1, -1) if b not in fixed]
        part = 32 if self.rows % 32 == 0 else self.rows
        for combo in range(1 << len(free)):
            place = {b: (combo >> i) & 1 for i, b in enumerate(reversed(free))}
            where = {**fixed, **place}
            head = tuple(place[b] for b in free)

            def body(i, _):
                rows = pl.ds(pl.multiple_of(i * part, part), part)
                value = self.source[self.at(where) + (rows,)].astype(F32)
                for j in range(step):
                    gone = self.order[: j + 1]
                    value = value + self.recv[j][self.at(where, gone) + (rows,)].astype(F32)
                target[head + (rows,)] = value.astype(BF16)
                return 0

            lax.fori_loop(0, self.rows // part, body, 0)

    def halve(self, k):
        bit = self.order[k]
        fixed = {b: self.bit_of[b] for b in self.order[:k]}
        fixed[bit] = 1 - self.bit_of[bit]
        if k == 0:
            source = self.source.at[self.at(fixed)]
        else:
            self.copies["rs", k - 1].wait()
            self.total(k, fixed, self.send[k])
            source = self.send[k]
        self.remote(("rs", k), k, source, self.recv[k], bit)

    def finish(self):
        self.copies["rs", self.bits - 1].wait()
        mine = {b: self.bit_of[b] for b in range(self.bits)}
        self.total(self.bits, mine, self.shard)
        if self.peer:
            self.remote("x", self.bits, self.shard, self.from_peer)
        else:
            self.begin(self.shard)

    def take_peer(self):
        self.copies["x"].wait()
        self.begin(self.from_peer)

    def begin(self, block):
        mine = self.at({b: self.bit_of[b] for b in range(self.bits)})
        local = pltpu.make_async_copy(block, self.out.at[mine], self.recv_sem.at[2 * self.bits + 1])
        local.start()
        self.copies["local"] = local
        self.remote(("ag", 0), self.bits + 1, block, self.out.at[mine], self.order[-1])

    def double(self, k):
        if k == 1:
            self.copies["local"].wait()
        self.copies["ag", k - 1].wait()
        bit = self.order[self.bits - 1 - k]
        fixed = {b: self.bit_of[b] for b in self.order[: self.bits - k]}
        slab = self.out.at[self.at(fixed)]
        self.remote(("ag", k), self.bits + 1 + k, slab, slab, bit)

    def end(self):
        if self.bits == 1:
            self.copies["local"].wait()
        self.copies["ag", self.bits - 1].wait()


def greet(bits, group, bit_of, more=("wd",)):
    barrier = pltpu.get_barrier_semaphore()
    for bit in range(bits):
        step = 1 << bit
        device = {"dp": group + step - 2 * step * bit_of[bit]}
        pl.semaphore_signal(barrier, inc=1, device_id=device, device_id_type=MESH)
    for axis in more:
        device = {axis: 1 - lax.axis_index(axis)}
        pl.semaphore_signal(barrier, inc=1, device_id=device, device_id_type=MESH)
    pl.semaphore_wait(barrier, bits + len(more))


def weave(pieces):
    last = max(i + len(p.stages) for i, p in enumerate(pieces))
    for slot in range(last):
        for i in reversed(range(len(pieces))):
            if 0 <= slot - i < len(pieces[i].stages):
                pieces[i].stages[slot - i]()


def sum_body(bits, plans, *refs):
    group, bit_of = own_bits(bits)
    count = len(plans)
    sources, outs, rest = refs[:count], refs[count : 2 * count], list(refs[2 * count :])
    pieces = []
    for plan, source, out in zip(plans, sources, outs):
        size = len(plan.scratch())
        pieces.append(plan.bind(group, bit_of, source, out, rest[:size]))
        rest = rest[size:]
    greet(bits, group, bit_of)
    weave(pieces)


def sum_groups(bits, arrays, orders, peers):
    split_shapes = [
        (2,) * bits + (a.shape[0] >> bits, a.shape[1]) for a in arrays
    ]
    plans = [
        Reduce(order, shape[-2], shape[-1], peer)
        for order, shape, peer in zip(orders, split_shapes, peers)
    ]
    scratch = [s for plan in plans for s in plan.scratch()]
    outs = pl.pallas_call(
        functools.partial(sum_body, bits, plans),
        in_specs=[pl.BlockSpec(memory_space=pltpu.VMEM)] * len(arrays),
        out_specs=[pl.BlockSpec(memory_space=pl.ANY)] * len(arrays),
        out_shape=[jax.ShapeDtypeStruct(shape, BF16) for shape in split_shapes],
        scratch_shapes=scratch,
        compiler_params=pltpu.CompilerParams(
            collective_id=0, has_side_effects=True, vmem_limit_bytes=58 * 2**20
        ),
        name="sum_groups",
    )(*[a.reshape(shape) for a, shape in zip(arrays, split_shapes)])
    return [o.reshape(a.shape) for o, a in zip(outs, arrays)]


def pick(a, index, axis=0):
    return lax.dynamic_index_in_dim(a, index, axis, keepdims=False)


def after(value, *deps):
    return lax.optimization_barrier((value,) + deps)[0]


def mm(a, b):
    return jnp.dot(a, b, preferred_element_type=F32)


def mm_nt(a, b):
    return lax.dot_general(a, b, NT, preferred_element_type=F32)


def mm_tn(a, b):
    return lax.dot_general(a, b, (((0,), (0,)), ((), ())), preferred_element_type=F32)


def on_device(
    group_count,
    inputs,
    lengths,
    gain_attn,
    attn_proj,
    beta_proj,
    conv_kernel,
    out_proj,
    gain_ffn,
    gate_proj,
    up_proj,
    down_proj,
    cotangent,
):
    span, width = inputs.shape
    heads_all = attn_proj.shape[1]
    heads = conv_kernel.shape[1]
    hw = conv_kernel.shape[2]
    hidden_own = gate_proj.shape[1] // 2
    bits = group_count.bit_length() - 1
    core, side, group = lax.axis_index("tp"), lax.axis_index("wd"), lax.axis_index("dp")
    bit_of = [(group >> b) & 1 for b in range(bits)]

    def xswap(a):
        return lax.ppermute(a, "wd", [(0, 1), (1, 0)])

    def cswap(a):
        return lax.ppermute(a, "tp", [(0, 1), (1, 0)])

    def gswap(a, bit):
        return lax.ppermute(a, "dp", [(i, i ^ (1 << bit)) for i in range(group_count)])

    def ordered(flag, mine, other, axis=0):
        return jnp.where(
            flag == 0,
            jnp.concatenate([mine, other], axis),
            jnp.concatenate([other, mine], axis),
        )

    def halves(a):
        return a.reshape((2, a.shape[0] // 2) + a.shape[1:])

    def fetch(send):
        got = xswap(pick(halves(send), bit_of[0]))
        return ordered(bit_of[0], got, gswap(got, 0)), got

    def fetch_rows(a):
        got = xswap(pick(halves(a), core))
        return ordered(core, got, cswap(got)), got

    w_attn = attn_proj.reshape(width, 2, heads * 4 * hw)
    w_beta = beta_proj.reshape(width, 2, heads)
    w_out = out_proj.reshape(heads_all * hw, width)
    w_gate = gate_proj.reshape(width, 2, hidden_own)
    w_up = up_proj.reshape(width, 2, hidden_own)
    w_down = down_proj.reshape(2, hidden_own, width)
    in_peer, dep = fetch_rows(inputs)
    attn_m = pick(w_attn, side, 1)
    attn_p, dep = fetch(after(pick(w_attn, 1 - side, 1), dep))
    beta_m = pick(w_beta, side, 1)
    beta_p = xswap(pick(w_beta, 1 - side, 1))
    gain_one_p = xswap(gain_attn)
    gain_two_p = xswap(gain_ffn)
    out_m = w_out
    out_p, dep = fetch(after(w_out, dep))
    gate_m = pick(w_gate, side, 1)
    gate_p, dep = fetch(after(pick(w_gate, 1 - side, 1), dep))
    up_m = pick(w_up, side, 1)
    up_p, dep = fetch(after(pick(w_up, 1 - side, 1), dep))
    down_m = pick(w_down, side, 0)
    down_p, dep = fetch(after(pick(w_down, 1 - side, 0), dep))
    cot_peer, dep = fetch_rows(after(cotangent, dep))
    out_m_far, out_p_far = cswap(out_m), cswap(out_p)

    x_m, x_p = inputs.astype(F32), in_peer.astype(F32)
    model = 2 * width
    square = jnp.sum(x_m * x_m, -1, keepdims=True) + jnp.sum(x_p * x_p, -1, keepdims=True)
    rinv_one = lax.rsqrt(square / model + norm_eps)
    act_m = (x_m * rinv_one * gain_attn).astype(BF16)
    act_p = (x_p * rinv_one * gain_one_p).astype(BF16)
    proj = (mm(act_m, attn_m) + mm(act_p, attn_p)).astype(BF16)
    logit = (mm(act_m, beta_m) + mm(act_p, beta_p)).T[..., None]
    kern = jnp.transpose(conv_kernel, (1, 0, 2))
    attended, kept_x, kept_w, kept_p = attend_forward(proj, logit, kern, lengths)
    heads_near = ordered(side, attended, xswap(attended), 1)
    heads_far = cswap(heads_near)
    mid_m = x_m + mm(heads_near, out_m) + mm(heads_far, out_m_far)
    mid_p = x_p + mm(heads_near, out_p) + mm(heads_far, out_p_far)
    square = jnp.sum(mid_m * mid_m, -1, keepdims=True) + jnp.sum(mid_p * mid_p, -1, keepdims=True)
    rinv_two = lax.rsqrt(square / model + norm_eps)
    two_m = (mid_m * rinv_two * gain_ffn).astype(BF16)
    two_p = (mid_p * rinv_two * gain_two_p).astype(BF16)
    gate = mm(two_m, gate_m) + mm(two_p, gate_p)
    up = mm(two_m, up_m) + mm(two_p, up_p)
    hidden_grad = mm_nt(cotangent, down_m) + mm_nt(cot_peer, down_p)
    sigma = jax.nn.sigmoid(gate)
    hidden = (gate * sigma * up).astype(BF16)
    gate_grad = (hidden_grad * up * sigma * (1.0 + gate * (1.0 - sigma))).astype(BF16)
    up_grad = (hidden_grad * gate * sigma).astype(BF16)

    def core_sum(part):
        part = halves(part)
        return pick(part, core).astype(F32) + cswap(pick(part, 1 - core)).astype(F32)

    def full_sum(part_m, part_p):
        mine = core_sum(part_m.astype(BF16)).astype(BF16)
        peer = core_sum(part_p.astype(BF16)).astype(BF16)
        mine_sum = (mine.astype(F32) + xswap(peer).astype(F32)).astype(BF16)
        peer_sum = (peer.astype(F32) + xswap(mine).astype(F32)).astype(BF16)
        return (
            ordered(core, mine_sum, cswap(mine_sum)).astype(F32),
            ordered(core, peer_sum, cswap(peer_sum)).astype(F32),
        )

    two_grad_m, two_grad_p = full_sum(
        mm_nt(gate_grad, gate_m) + mm_nt(up_grad, up_m),
        mm_nt(gate_grad, gate_p) + mm_nt(up_grad, up_p),
    )

    def norm_back(grad_m, grad_p, base_m, base_p, rinv, gain_m, gain_p):
        cross = jnp.sum(grad_m * gain_m * base_m, -1, keepdims=True)
        cross = cross + jnp.sum(grad_p * gain_p * base_p, -1, keepdims=True)
        cube = rinv * rinv * rinv * cross / model
        gain_grad = jnp.sum(grad_m * base_m * rinv, 0)
        back_m = grad_m * gain_m * rinv - base_m * cube
        back_p = grad_p * gain_p * rinv - base_p * cube
        return back_m, back_p, gain_grad

    back_m, back_p, grad_gain_two = norm_back(
        two_grad_m, two_grad_p, mid_m, mid_p, rinv_two, gain_ffn, gain_two_p
    )
    mid_grad_m = cotangent.astype(F32) + back_m
    branch_m = mid_grad_m.astype(BF16)
    branch_p = (cot_peer.astype(F32) + back_p).astype(BF16)
    own_rows = heads * hw
    out_own_m = lax.dynamic_slice_in_dim(out_m, side * own_rows, own_rows, 0)
    out_own_p = lax.dynamic_slice_in_dim(out_p, side * own_rows, own_rows, 0)
    heads_grad = (mm_nt(branch_m, out_own_m) + mm_nt(branch_p, out_own_p)).astype(BF16)

    order_a = list(range(bits))
    order_b = [1, 0] + list(range(2, bits)) if bits > 1 else order_a
    proj_grad, logit_grad, kern_grad = attend_backward(
        proj, logit, kern, heads_grad, kept_x, kept_w, kept_p
    )
    beta_grad = logit_grad[..., 0].T.astype(BF16)
    wide = 4 * hw
    weights = [
        mm_tn(hidden, cotangent),
        mm_tn(hidden, cot_peer),
        mm_tn(two_m, gate_grad),
        mm_tn(two_p, gate_grad),
        mm_tn(two_m, up_grad),
        mm_tn(two_p, up_grad),
        mm_tn(heads_near, branch_m),
    ]
    peers = [False, True] * 3 + [False]
    for h in range(heads):
        own = slice(h * wide, (h + 1) * wide)
        weights += [mm_tn(act_m, proj_grad[:, own]), mm_tn(act_p, proj_grad[:, own])]
        peers += [False, True]
    orders = [order_b if i % 4 == 2 else order_a for i in range(len(weights))]
    sums = sum_groups(bits, [w.astype(BF16) for w in weights], orders, peers)
    down_sum, gate_sum, up_sum, out_sum = sums[0:2], sums[2:4], sums[4:6], sums[6]
    attn_sum = [jnp.concatenate(sums[7::2], 1), jnp.concatenate(sums[8::2], 1)]
    grad_beta_m, grad_beta_p = mm_tn(act_m, beta_grad), mm_tn(act_p, beta_grad)
    one_grad_m, one_grad_p = full_sum(
        mm_nt(proj_grad, attn_m) + mm_nt(beta_grad, beta_m),
        mm_nt(proj_grad, attn_p) + mm_nt(beta_grad, beta_p),
    )
    back_m, _, grad_gain_one = norm_back(
        one_grad_m, one_grad_p, x_m, x_p, rinv_one, gain_attn, gain_one_p
    )
    grad_inputs = (mid_grad_m + back_m).astype(BF16)

    feed_m = core_sum(mm(hidden, down_m).astype(BF16))
    feed_p = core_sum(mm(hidden, down_p).astype(BF16))
    feed = feed_m + xswap(feed_p.astype(BF16)).astype(F32)
    mid_half = pick(halves(mid_m), core)
    out_half = (mid_half + feed).astype(BF16)
    outputs = ordered(core, out_half, cswap(out_half))

    small = [grad_gain_one, grad_gain_two, grad_beta_m, xswap(grad_beta_p), kern_grad]
    flat = jnp.concatenate([s.reshape(-1) for s in small]).reshape(-1, 128)
    for bit in range(bits):
        flat = flat + gswap(flat, bit)
    flat = flat.reshape(-1)
    done, at = [], 0
    for s in small:
        done.append(flat[at : at + s.size].reshape(s.shape))
        at += s.size
    gain_one_sum, gain_two_sum, beta_sum_m, beta_sum_p, kern_sum = done

    def columns(pair):
        return ordered(side, pair[0].astype(F32), pair[1].astype(F32), 1)

    return (
        outputs,
        grad_inputs,
        gain_one_sum,
        columns(attn_sum).reshape(attn_proj.shape),
        ordered(side, beta_sum_m, beta_sum_p, 1),
        jnp.transpose(kern_sum, (1, 0, 2)),
        out_sum.astype(F32).reshape(out_proj.shape),
        gain_two_sum,
        columns(gate_sum),
        columns(up_sum),
        ordered(side, down_sum[0].astype(F32), down_sum[1].astype(F32), 0),
    )


def solution(mesh):
    return jax.shard_map(
        functools.partial(on_device, mesh.shape["dp"]),
        mesh=mesh,
        in_specs=(
            P("dp", "wd"),
            P("dp"),
            P("wd"),
            P("wd", "tp", None),
            P("wd", "tp"),
            P(None, ("tp", "wd"), None),
            P("tp", None, "wd"),
            P("wd"),
            P("wd", "tp"),
            P("wd", "tp"),
            P("tp", "wd"),
            P("dp", "wd"),
        ),
        out_specs=(
            P("dp", "wd"),
            P("dp", "wd"),
            P("wd"),
            P("wd", "tp", None),
            P("wd", "tp"),
            P(None, ("tp", "wd"), None),
            P("tp", None, "wd"),
            P("wd"),
            P("wd", "tp"),
            P("wd", "tp"),
            P("tp", "wd"),
        ),
        check_vma=False,
    )
```

```python
import functools
from typing import Any, NamedTuple

import jax
import jax.numpy as jnp
from jax import lax
from jax.experimental import pallas as pl
from jax.experimental.pallas import tpu as pltpu
from jax.sharding import PartitionSpec as P

norm_eps = 1e-06
KCONV = 4
HALF = 256
F32 = jnp.float32
BF16 = jnp.bfloat16
NT = (((1,), (1,)), ((), ()))
NN = (((1,), (0,)), ((), ()))


def dotb(a, b, dims=NN):
    return lax.dot_general(a, b, dims, preferred_element_type=F32)


def split(a):
    hi = a.astype(BF16)
    return hi, (a - hi.astype(F32)).astype(BF16)


def dot3(a, b, dims=NN):
    (ah, al), (bh, bl) = a, b
    return dotb(ah, bh, dims) + (dotb(al, bh, dims) + dotb(ah, bl, dims))


def shift_down(a, m):
    if m == 0:
        return a
    rows = lax.broadcasted_iota(jnp.int32, a.shape, 0)
    return jnp.where(rows >= m, pltpu.roll(a, m, 0), 0.0)


def shift_up(a, m):
    if m == 0:
        return a
    n = a.shape[0]
    rows = lax.broadcasted_iota(jnp.int32, a.shape, 0)
    return jnp.where(rows < n - m, pltpu.roll(a, n - m, 0), 0.0)


def house_of(raws, kern):
    conv = kern[0:1] * raws
    for m in range(1, KCONV):
        conv = conv + kern[m : m + 1] * shift_down(raws, m)
    scale = lax.rsqrt(jnp.sum(conv * conv, -1, keepdims=True) + 1e-06)
    return conv * scale, scale


def forward_body(len_ref, proj_ref, logit_ref, kern_ref, o_ref, x_ref, w_ref, p_ref):
    length = len_ref[0]
    hw = o_ref.shape[-1]
    q = proj_ref[:, 0:hw]
    k = proj_ref[:, hw : 2 * hw]
    v = proj_ref[:, 2 * hw : 3 * hw]
    raws = proj_ref[:, 3 * hw : 4 * hw].astype(F32)
    house, _ = house_of(raws, kern_ref[0])
    beta = 2.0 * jax.nn.sigmoid(logit_ref[0])
    hh, hl = split(house)
    top, low = slice(0, HALF), slice(HALF, 2 * HALF)
    ri = lax.broadcasted_iota(jnp.int32, (HALF, HALF), 0)
    ci = lax.broadcasted_iota(jnp.int32, (HALF, HALF), 1)
    strict = ri > ci
    causal = ri >= ci
    h_left = jnp.concatenate([hh, hl, hh], 1)
    h_right = jnp.concatenate([hh, hh, hl], 1)
    h_two = jnp.concatenate([hh, hl], 1)
    k_two = jnp.concatenate([k, k], 1)
    q_two = jnp.concatenate([q, q], 1)

    def gram(a, b):
        return dotb(h_left[a], h_right[b], NT)

    def keyed(a, b):
        return dotb(h_two[a], k_two[b], NT)

    def asked(a, b):
        return dotb(q_two[a], h_two[b], NT)

    n11 = beta[top] * jnp.where(strict, gram(top, top), 0.0)
    n22 = beta[low] * jnp.where(strict, gram(low, low), 0.0)
    n21 = split(beta[low] * gram(low, top))
    inverses = [n11, n22]
    level = 1
    xor = ri ^ ci
    bits = [split(n11), split(n22)]
    current = None
    while level < HALF:
        mask = (xor >= level) & (xor < 2 * level)
        for d in range(2):
            if level == 1:
                eye = jnp.where(ri == ci, 1.0, 0.0)
                inverses[d] = eye - jnp.where(mask, inverses[d], 0.0)
            else:
                t = split(inverses[d])
                zero = jnp.zeros((), BF16)
                c = tuple(jnp.where(mask, part, zero) for part in bits[d])
                inverses[d] = inverses[d] - dot3(t, split(dot3(c, t)))
        level *= 2
    t1, t2 = split(inverses[0]), split(inverses[1])
    b11 = split(beta[top] * jnp.where(strict, keyed(top, top), 0.0))
    b22 = split(beta[low] * jnp.where(strict, keyed(low, low), 0.0))
    b21f = beta[low] * keyed(low, top)
    b21 = split(b21f)
    m11 = split(jnp.where(causal, asked(top, top), 0.0))
    m22 = split(jnp.where(causal, asked(low, low), 0.0))
    m21 = asked(low, top)
    x11 = split(dot3(t1, b11))
    x22 = split(dot3(t2, b22))
    x21 = split(dot3(t2, split(b21f - dot3(n21, x11))))
    w11 = split(dot3(m11, t1))
    w22 = split(dot3(m22, t2))
    w21 = split(dot3(split(m21 - dot3(w22, n21)), t1))
    scale = hw ** (-0.5)

    def soften(scores, allowed):
        scores = jnp.where(allowed, scores, -1e30)
        weights = jnp.exp(scores - jnp.max(scores, -1, keepdims=True))
        return (weights * (1.0 / jnp.sum(weights, -1, keepdims=True))).astype(BF16)

    s11 = (dotb(q[top], k[top], NT) - dot3(w11, b11)) * scale
    s21 = (dotb(q[low], k[top], NT) - (dot3(w21, b11) + dot3(w22, b21))) * scale
    s22 = (dotb(q[low], k[low], NT) - dot3(w22, b22)) * scale
    p1 = soften(s11, causal & (ci < length))
    p2 = soften(
        jnp.concatenate([s21, s22], 1),
        jnp.concatenate([ci < length, causal & (ci + HALF < length)], 1),
    )
    o_ref[top, :] = dotb(p1, v[top]).astype(o_ref.dtype)
    o_ref[low, :] = dotb(p2, v).astype(o_ref.dtype)
    p_ref[0, 0] = p1
    p_ref[0, 1] = p2[:, :HALF]
    p_ref[0, 2] = p2[:, HALF:]
    for i, (xx, ww) in enumerate(((x11, w11), (x21, w21), (x22, w22))):
        for j in range(2):
            x_ref[0, i, j] = xx[j]
            w_ref[0, i, j] = ww[j].T


def backward_body(proj_ref, logit_ref, kern_ref, g_ref, x_ref, w_ref, p_ref, dproj_ref, dlogit_ref, dkern_ref):
    hw = g_ref.shape[-1]
    q = proj_ref[:, 0:hw]
    k = proj_ref[:, hw : 2 * hw]
    v = proj_ref[:, 2 * hw : 3 * hw]
    raws = proj_ref[:, 3 * hw : 4 * hw].astype(F32)
    kern = kern_ref[0]
    house, rs = house_of(raws, kern)
    beta = 2.0 * jax.nn.sigmoid(logit_ref[0])
    g = g_ref[...]
    hh, hl = split(house)
    top, low = slice(0, HALF), slice(HALF, 2 * HALF)
    ri = lax.broadcasted_iota(jnp.int32, (HALF, HALF), 0)
    ci = lax.broadcasted_iota(jnp.int32, (HALF, HALF), 1)
    strict = ri > ci
    causal = ri >= ci
    scale = hw ** (-0.5)
    p11, p21, p22 = (p_ref[0, i] for i in range(3))
    x11, x21, x22 = ((x_ref[0, i, 0], x_ref[0, i, 1]) for i in range(3))
    w11, w21, w22 = ((w_ref[0, i, 0], w_ref[0, i, 1]) for i in range(3))
    q_t, g_t = q.T, g.T
    ht_h, ht_l = hh.T, hl.T

    def soften_back(probs, dprobs):
        pf = probs.astype(F32)
        mixed = pf * dprobs
        return (mixed - pf * jnp.sum(mixed, -1, keepdims=True)) * scale

    z1 = soften_back(p11, dotb(g[top], v[top], NT))
    z2 = soften_back(jnp.concatenate([p21, p22], 1), dotb(g[low], v, NT))
    z11 = split(z1)
    z21 = split(z2[:, :HALF])
    z22 = split(z2[:, HALF:])
    u11 = jnp.where(causal, dot3(z11, x11, NT), 0.0)
    u21 = dot3(z21, x11, NT)
    u22 = jnp.where(causal, dot3(z21, x21, NT) + dot3(z22, x22, NT), 0.0)
    u11, u21, u22 = split(u11), split(u21), split(u22)
    b11 = jnp.where(strict, dot3(w11, z11) + dot3(w21, z21), 0.0)
    b21 = dot3(w22, z21)
    b22 = jnp.where(strict, dot3(w22, z22), 0.0)
    a11 = jnp.where(strict, dot3(w11, u11) + dot3(w21, u21), 0.0)
    a21 = dot3(w22, u21)
    a22 = jnp.where(strict, dot3(w22, u22), 0.0)
    b11s, b21s, b22s = split(b11), split(b21), split(b22)
    a11s, a21s, a22s = split(a11), split(a21), split(a22)

    def rows(c11, c21, c22, mats):
        (mh, ml) = mats
        first = dotb(c11[0], mh[top]) + dotb(c11[1], mh[top])
        second = dotb(c21[0], mh[top]) + dotb(c21[1], mh[top])
        second = second + dotb(c22[0], mh[low]) + dotb(c22[1], mh[low])
        if ml is not None:
            first = first + dotb(c11[0], ml[top])
            second = second + dotb(c21[0], ml[top]) + dotb(c22[0], ml[low])
        return jnp.concatenate([first, second], 0)

    def cols(c11, c21, c22, mats):
        (mh, ml) = mats
        first = dotb(mh[:, top], c11[0]) + dotb(mh[:, top], c11[1])
        first = first + dotb(mh[:, low], c21[0]) + dotb(mh[:, low], c21[1])
        second = dotb(mh[:, low], c22[0]) + dotb(mh[:, low], c22[1])
        if ml is not None:
            first = first + dotb(ml[:, top], c11[0]) + dotb(ml[:, low], c21[0])
            second = second + dotb(ml[:, low], c22[0])
        return jnp.concatenate([first, second], 1)

    dq = rows(z11, z21, z22, (k, None)) - rows(u11, u21, u22, (hh, hl))
    bk = rows(b11s, b21s, b22s, (k, None))
    nh = rows(a11s, a21s, a22s, (hh, hl))
    mixed = nh - bk
    dbeta = jnp.sum(house * mixed, -1, keepdims=True)
    dlogit_ref[0] = dbeta * beta * (1.0 - 0.5 * beta)
    bb = [split(beta[s] * b) for s, b in ((top, b11), (low, b21), (low, b22))]
    ab = [split(beta[s] * a) for s, a in ((top, a11), (low, a21), (low, a22))]
    dk_t = cols(z11, z21, z22, (q_t, None)) - cols(*bb, (ht_h, ht_l))
    dh_t = cols(*ab, (ht_h, ht_l)) - cols(u11, u21, u22, (q_t, None))
    dv_t = jnp.concatenate(
        [dotb(g_t[:, top], p11) + dotb(g_t[:, low], p21), dotb(g_t[:, low], p22)], 1
    )
    dh = beta * mixed + dh_t.T
    dc = rs * (dh - house * jnp.sum(house * dh, -1, keepdims=True))
    dr = kern[0:1] * dc
    taps = [jnp.sum(dc * raws, 0, keepdims=True)]
    for m in range(1, KCONV):
        up = shift_up(dc, m)
        dr = dr + kern[m : m + 1] * up
        taps.append(jnp.sum(up * raws, 0, keepdims=True))
    dkern_ref[0] = jnp.concatenate(taps, 0)
    dproj_ref[:, 0:hw] = dq.astype(BF16)
    dproj_ref[:, hw : 2 * hw] = dk_t.T.astype(BF16)
    dproj_ref[:, 2 * hw : 3 * hw] = dv_t.T.astype(BF16)
    dproj_ref[:, 3 * hw : 4 * hw] = dr.astype(BF16)


MESH = pl.DeviceIdType.MESH
TN = (((0,), (0,)), ((), ()))


def own_bits(bits):
    group = lax.axis_index("dp")
    return group, [lax.rem(lax.div(group, 1 << b), 2) for b in range(bits)]


class Reduce:
    def __init__(self, order, rows, columns, peer):
        self.order, self.rows, self.columns, self.peer = order, rows, columns, peer
        self.bits = len(order)

    def dims(self, taken):
        return (2,) * (self.bits - taken) + (self.rows, self.columns)

    def scratch(self):
        shapes = [pltpu.VMEM(self.dims(1), BF16)]
        shapes += [pltpu.VMEM(self.dims(1 + k), BF16) for k in range(self.bits)]
        shapes += [pltpu.VMEM(self.dims(self.bits), BF16)]
        if self.peer:
            shapes += [pltpu.VMEM(self.dims(self.bits), BF16)]
        count = 2 * self.bits + 1
        return shapes + [pltpu.SemaphoreType.DMA((count,)), pltpu.SemaphoreType.DMA((count + 1,))]

    def bind(self, group, bit_of, compute, out, refs, send):
        self.group, self.bit_of, self.compute, self.out = group, bit_of, compute, out
        refs = list(refs)
        self.kept = refs.pop(0)
        self.recv = [refs.pop(0) for _ in range(self.bits)]
        self.shard = refs.pop(0)
        self.from_peer = refs.pop(0) if self.peer else None
        self.send_sem, self.recv_sem = refs
        self.send = send
        stages = [functools.partial(self.halve, k) for k in range(self.bits)] + [self.finish]
        if self.peer:
            stages.append(self.take_peer)
        stages += [functools.partial(self.double, k) for k in range(1, self.bits)] + [self.end]
        self.stages = stages
        self.copies = {}
        return self

    def at(self, fixed, gone=()):
        return tuple(
            fixed.get(b, slice(None)) for b in range(self.bits - 1, -1, -1) if b not in gone
        )

    def remote(self, slot, source, target, bit=None):
        if bit is None:
            device = {"wd": 1 - lax.axis_index("wd")}
        else:
            step = 1 << bit
            device = {"dp": self.group + step - 2 * step * self.bit_of[bit]}
        copy = pltpu.make_async_remote_copy(
            src_ref=source,
            dst_ref=target,
            send_sem=self.send_sem.at[slot],
            recv_sem=self.recv_sem.at[slot],
            device_id=device,
            device_id_type=MESH,
        )
        copy.start()
        self.copies[slot] = copy

    def total(self, step, fixed, target):
        free = [b for b in range(self.bits - 1, -1, -1) if b not in fixed]
        part = 32 if self.rows % 32 == 0 else self.rows
        for combo in range(1 << len(free)):
            place = {b: (combo >> i) & 1 for i, b in enumerate(reversed(free))}
            where = {**fixed, **place}
            head = tuple(place[b] for b in free)

            def body(i, _):
                rows = pl.ds(pl.multiple_of(i * part, part), part)
                value = self.kept[self.at(where, self.order[:1]) + (rows,)].astype(F32)
                for j in range(step):
                    gone = self.order[: j + 1]
                    value = value + self.recv[j][self.at(where, gone) + (rows,)].astype(F32)
                target[head + (rows,)] = value.astype(BF16)
                return 0

            lax.fori_loop(0, self.rows // part, body, 0)

    def halve(self, k):
        bit = self.order[k]
        if k == 0:
            self.compute(self, {bit: 1 - self.bit_of[bit]}, self.send[0])
        else:
            self.copies[k - 1].wait()
            fixed = {b: self.bit_of[b] for b in self.order[:k]}
            fixed[bit] = 1 - self.bit_of[bit]
            self.total(k, fixed, self.send[k])
        self.remote(k, self.send[k], self.recv[k], bit)
        if k == 0:
            self.compute(self, {bit: self.bit_of[bit]}, self.kept)

    def finish(self):
        self.copies[self.bits - 1].wait()
        mine = {b: self.bit_of[b] for b in range(self.bits)}
        self.total(self.bits, mine, self.shard)
        if self.peer:
            self.remote(self.bits, self.shard, self.from_peer)
        else:
            self.begin(self.shard)

    def take_peer(self):
        self.copies[self.bits].wait()
        self.begin(self.from_peer)

    def begin(self, block):
        mine = self.at({b: self.bit_of[b] for b in range(self.bits)})
        local = pltpu.make_async_copy(block, self.out(mine), self.recv_sem.at[2 * self.bits + 1])
        local.start()
        self.copies[-1] = local
        self.remote(self.bits + 1, block, self.out(mine), self.order[-1])

    def double(self, k):
        if k == 1:
            self.copies[-1].wait()
        self.copies[self.bits + k].wait()
        bit = self.order[self.bits - 1 - k]
        fixed = {b: self.bit_of[b] for b in self.order[: self.bits - k]}
        slab = self.out(self.at(fixed))
        self.remote(self.bits + 1 + k, slab, slab, bit)

    def end(self):
        if self.bits == 1:
            self.copies[-1].wait()
        self.copies[2 * self.bits].wait()


def turned(source, target, bits):
    columns, tokens = source.shape[1], source.shape[0]
    rows = columns >> bits
    if rows % 16 == 0:
        target[...] = source[...].T.reshape(target.shape)
    else:
        value = source[...].astype(F32).T
        for i in range(1 << bits):
            place = tuple((i >> b) & 1 for b in range(bits - 1, -1, -1))
            target[place] = value[i * rows : (i + 1) * rows].astype(BF16)


def gradient(left, right):
    def compute(piece, fixed, target):
        where = piece.at(fixed)
        rows, columns = piece.rows, piece.columns
        values = right()
        if rows % 16 == 0:
            part = left[where]
            part = part.reshape(-1, part.shape[-1])
            target[...] = dotb(part, values).astype(BF16).reshape(target.shape)
        else:
            free = [b for b in range(piece.bits - 1, -1, -1) if b not in fixed]
            for combo in range(1 << len(free)):
                place = {b: (combo >> i) & 1 for i, b in enumerate(reversed(free))}
                head = tuple(place[b] for b in free)
                part = left[piece.at({**fixed, **place})]
                target[head] = dotb(part, values).astype(BF16)

    return compute


LAG = 2
DEEP = 3
SMALL = 64


class Given(NamedTuple):
    part: Any
    feed: Any
    cot: Any
    hidden: Any
    gate_grad: Any
    up_grad: Any
    two: Any
    mid: Any
    rinv_one: Any
    rinv_two: Any
    gain_one: Any
    gain_two: Any
    near: Any
    out: Any
    proj: Any
    logit: Any
    kern: Any
    kept: Any
    act: Any
    x: Any
    attn_all: Any
    attn_peer: Any
    beta: Any


class Spots(NamedTuple):
    cot: Any
    hidden: Any
    gate_grad: Any
    up_grad: Any
    two: Any
    near: Any
    out_own: Any
    proj: Any
    core_in: Any
    core_own: Any
    sum: Any
    side_in: Any
    mid: Any
    mid_grad: Any
    branch: Any
    heads_grad: Any
    feed_out: Any
    feed_in: Any
    aw: Any
    dproj: Any
    logit: Any
    dlogit: Any
    dkern: Any
    kept: Any
    left_hidden: Any
    left: Any
    small: Any
    small_in: Any
    beta_out: Any
    beta_in: Any
    local_sem: Any
    send_sem: Any
    recv_sem: Any


class Loads:
    def __init__(self, sems):
        self.sems, self.used = sems, 0

    def start(self, source, target):
        copy = pltpu.make_async_copy(source, target, self.sems.at[self.used])
        self.used += 1
        copy.start()
        return [copy]


class Links:
    def __init__(self, send_sems, recv_sems):
        self.send_sems, self.recv_sems, self.used = send_sems, recv_sems, 0

    def start(self, device, source, target):
        copy = pltpu.make_async_remote_copy(
            src_ref=source,
            dst_ref=target,
            send_sem=self.send_sems.at[self.used],
            recv_sem=self.recv_sems.at[self.used],
            device_id=device,
            device_id_type=MESH,
        )
        self.used += 1
        copy.start()
        return copy


def settle(copies):
    for copy in copies:
        copy.wait()
    copies.clear()


def flipped(axis):
    return {axis: 1 - lax.axis_index(axis)}


def group_peer(group, bit_of, bit):
    step = 1 << bit
    return {"dp": group + step - 2 * step * bit_of[bit]}


def back_body(bits, plans, r, outs, out_ref, gin_ref, small_ref, v, rest):
    group, bit_of = own_bits(bits)
    count = len(plans)
    core, side = lax.axis_index("tp"), lax.axis_index("wd")
    span, width = r.cot[0].shape
    half = span // 2
    wide = v.aw.shape[-1]
    hw = wide // 4
    heads = r.kern.shape[0]
    model = 2 * width
    hidden_own = r.hidden.shape[1]
    mine = pl.ds(pl.multiple_of(core * half, half), half)
    far = pl.ds(pl.multiple_of((1 - core) * half, half), half)
    loads = Loads(v.local_sem)
    links = Links(v.send_sem, v.recv_sem)
    x_peer, c_peer = flipped("wd"), flipped("tp")

    barrier = pltpu.get_barrier_semaphore()
    for device in [group_peer(group, bit_of, b) for b in range(bits)] + [x_peer, c_peer]:
        pl.semaphore_signal(barrier, inc=1, device_id=device, device_id_type=MESH)
    pl.semaphore_wait(barrier, bits + 2)

    first = [links.start(c_peer, r.part[i].at[far], v.core_in.at[i]) for i in range(2)]
    got_hidden = loads.start(r.hidden, v.hidden)
    got_cot = [loads.start(r.cot[i], v.cot[i]) for i in range(2)]
    got_part = [loads.start(r.part[i].at[mine], v.core_own.at[i])[0] for i in range(2)]
    got_ffn = [loads.start(r.two[i], v.two[i])[0] for i in range(2)]
    got_ffn += loads.start(r.gate_grad, v.gate_grad)
    got_ffn += loads.start(r.up_grad, v.up_grad)
    got_mid = [loads.start(r.mid[i].at[mine], v.mid.at[i])[0] for i in range(2)]
    own_rows = pl.ds(pl.multiple_of(side * heads * hw, heads * hw), heads * hw)
    got_out = [loads.start(r.out[i].at[own_rows], v.out_own.at[i])[0] for i in range(2)]
    got_near = loads.start(r.near, v.near)
    got_proj = loads.start(r.proj, v.proj)

    def load_kept(h):
        copies = [loads.start(a.at[pl.ds(h, 1)], b)[0] for a, b in zip(r.kept, v.kept)]
        return copies + loads.start(r.logit.at[pl.ds(h, 1)], v.logit)

    got_kept = load_kept(0)

    pieces = []
    shared = {}
    cut_width, cut_hidden = width // 2, hidden_own // 2

    def piece(left, right, view):
        plan = plans[len(pieces)]
        size = len(plan.scratch())
        own = [rest.pop(0) for _ in range(size)]
        pieces.append(plan.bind(group, bit_of, gradient(left, right), view, own, None))

    def columns(out, start, size):
        cols = pl.ds(pl.multiple_of(start, 128), size)
        return lambda where: out.at[where + (slice(None), cols)]

    def owner(j):
        return side if j == 0 else 1 - side

    for j in range(2):
        for i in range(2):
            cut = slice(i * cut_width, (i + 1) * cut_width)
            piece(
                v.left_hidden,
                lambda j=j, cut=cut: v.cot[j][:, cut],
                lambda where, j=j, cut=cut: outs[0].at[(owner(j),) + where + (slice(None), cut)],
            )
    for n, values in ((1, v.gate_grad), (2, v.up_grad)):
        for j in range(2):
            for i in range(2):
                cut = slice(i * cut_hidden, (i + 1) * cut_hidden)
                piece(
                    v.left.at[j],
                    lambda values=values, cut=cut: values[:, cut],
                    columns(outs[n], owner(j) * hidden_own + i * cut_hidden, cut_hidden),
                )
    for i in range(2):
        cut = slice(i * cut_width, (i + 1) * cut_width)
        piece(
            v.left.at[0],
            lambda cut=cut: v.branch[0, :, cut],
            lambda where, cut=cut: outs[3].at[where + (slice(None), cut)],
        )
    for h in range(heads):
        for j in range(2):
            piece(
                v.left.at[j],
                lambda h=h: v.dproj[h],
                lambda where, h=h, j=j: outs[4].at[(owner(j) * heads + h,) + where],
            )
    for i, plan in enumerate(plans):
        key = (plan.rows, plan.columns)
        place = shared.setdefault(key, [])
        at = sum((p.rows, p.columns) == key for p in plans[:i])
        if at < DEEP:
            place.append([rest.pop(0) for _ in range(bits)])
        pieces[i].send = place[at % DEEP]

    position = [0]

    def pump(until):
        last = max(i + LAG * len(p.stages) for i, p in enumerate(pieces))
        for slot in range(position[0], min(until, last)):
            for i in reversed(range(count)):
                step, off = divmod(slot - i, LAG)
                if off == 0 and 0 <= step < len(pieces[i].stages):
                    pieces[i].stages[step]()
        position[0] = max(position[0], until)

    settle(got_hidden)
    turned(v.hidden, v.left_hidden, bits)
    settle(got_cot[0])
    pump(2)
    settle(got_part)
    settle(first)
    for i in range(2):
        v.sum[i] = (v.core_own[i].astype(F32) + v.core_in[i].astype(F32)).astype(BF16)
    first = [links.start(x_peer, v.sum.at[i], v.side_in.at[1 - i]) for i in range(2)]
    settle(got_cot[1])
    settle(got_ffn)
    for i in range(2):
        turned(v.two[i], v.left.at[i], bits)
    pump(4)
    settle(first)
    settle(got_mid)

    def norm_back(base_of, rinv, gains):
        grads = [v.sum[i].astype(F32) + v.side_in[i].astype(F32) for i in range(2)]
        cross = sum(
            jnp.sum(grads[i] * gains[i] * base_of(i), -1, keepdims=True) for i in range(2)
        )
        cube = rinv * rinv * rinv * cross / model
        backs = [grads[i] * gains[i] * rinv - base_of(i) * cube for i in range(2)]
        return backs, jnp.sum(grads[0] * base_of(0) * rinv, 0, keepdims=True)

    gains = [g[...] for g in r.gain_two]
    backs, gain_two = norm_back(lambda i: v.mid[i], r.rinv_two[mine, :], gains)
    for i in range(2):
        value = v.cot[i][mine, :].astype(F32) + backs[i]
        if i == 0:
            v.mid_grad[...] = value
        v.branch[i, mine, :] = value.astype(BF16)
    first = [links.start(c_peer, v.branch.at[i, mine], v.branch.at[i, mine]) for i in range(2)]
    pump(5)
    settle(first)
    settle(got_out)
    grad = dotb(v.branch[0], v.out_own[0], NT) + dotb(v.branch[1], v.out_own[1], NT)
    for h in range(heads):
        v.heads_grad[h] = grad[:, h * hw : (h + 1) * hw].astype(BF16)
    first = [links.start(c_peer, r.feed[i].at[far], v.core_in.at[i]) for i in range(2)]
    got_part = [loads.start(r.feed[i].at[mine], v.core_own.at[i])[0] for i in range(2)]
    pump(6)
    settle(first)
    settle(got_part)
    feed = [v.core_own[i].astype(F32) + v.core_in[i].astype(F32) for i in range(2)]
    v.feed_out[...] = feed[1].astype(BF16)
    v.mid[0] = v.mid[0] + feed[0]
    first = [links.start(x_peer, v.feed_out, v.feed_in)]
    settle(got_proj)
    lanes = lax.broadcasted_iota(jnp.int32, (span, 128), 1)
    grad_beta = jnp.zeros((span, 128), F32)
    got_x = []

    def give_outputs():
        settle(first)
        v.feed_out[...] = (v.mid[0] + v.feed_in[...].astype(F32)).astype(BF16)
        first.append(links.start(c_peer, v.feed_out, out_ref.at[mine]))
        first.extend(loads.start(v.feed_out, out_ref.at[mine]))

    def take_inputs():
        settle(first)
        got_x.extend(loads.start(r.x[i].at[mine], v.core_own.at[i])[0] for i in range(2))

    for h in range(heads):
        settle(got_kept)
        got_aw = loads.start(r.attn_all.at[side * heads + h], v.aw.at[0])
        got_aw += loads.start(r.attn_peer.at[h], v.aw.at[1])
        backward_body(
            v.proj.at[h],
            v.logit,
            r.kern.at[pl.ds(h, 1)],
            v.heads_grad.at[h],
            v.kept[0],
            v.kept[1],
            v.kept[2],
            v.dproj.at[h],
            v.dlogit,
            v.dkern.at[pl.ds(h, 1)],
        )
        grad_beta = grad_beta + jnp.where(lanes == side * heads + h, v.dlogit[0], 0.0)
        if h + 1 < heads:
            got_kept = load_kept(h + 1)
        settle(got_aw)
        for i in range(2):
            value = dotb(v.dproj[h], v.aw[i], NT)
            if h > 0:
                value = value + v.cot[i][...].astype(F32)
            if h == heads - 1:
                low = grad_beta.astype(BF16)
                value = value + dotb(low[:, : 2 * heads], r.beta[i][...], NT)
            v.cot[i][...] = value.astype(BF16)
        pump(7 + h)
        if h == 0:
            give_outputs()
        if h == min(1, heads - 1):
            take_inputs()
    beta_low = grad_beta.astype(BF16)
    first = [links.start(c_peer, v.cot[i].at[far], v.core_in.at[i]) for i in range(2)]
    pump(12)
    settle(got_near)
    turned(v.near, v.left.at[0], bits)
    settle(first)
    for i in range(2):
        total = v.cot[i][mine, :].astype(F32) + v.core_in[i].astype(F32)
        v.sum[i] = total.astype(BF16)
    first = [links.start(x_peer, v.sum.at[i], v.side_in.at[1 - i]) for i in range(2)]
    pump(14)
    got_act = [loads.start(r.act[i], v.two[i])[0] for i in range(2)]
    settle(got_act)
    for i in range(2):
        turned(v.two[i], v.left.at[i], bits)
    pump(15)
    settle(first)
    settle(got_x)
    gains = [g[...] for g in r.gain_one]
    backs, gain_one = norm_back(lambda i: v.core_own[i].astype(F32), r.rinv_one[mine, :], gains)
    v.feed_out[...] = (v.mid_grad[...] + backs[0]).astype(BF16)
    first = [links.start(c_peer, v.feed_out, gin_ref.at[mine])]
    first += loads.start(v.feed_out, gin_ref.at[mine])
    rows = width // 128
    small = v.small
    for i in range(rows):
        cut = slice(i * 128, (i + 1) * 128)
        small[0, i : i + 1, :] = gain_one[:, cut]
        small[0, 8 + i : 9 + i, :] = gain_two[:, cut]
    small[0, rows:8, :] = jnp.zeros((8 - rows, 128), F32)
    small[0, 8 + rows : 16, :] = jnp.zeros((8 - rows, 128), F32)
    gain_rows = pl.ds(0, 16)
    first.append(links.start(c_peer, small.at[0, gain_rows], v.small_in.at[bits, gain_rows]))
    for i in range(2):
        value = lax.dot_general(beta_low, v.two[i][...], TN, preferred_element_type=F32)
        v.beta_out[i] = jnp.where(side == 0, value[0:8], value[heads : heads + 8])
    first.append(links.start(x_peer, v.beta_out.at[1], v.beta_in))
    pump(16)
    settle(first)
    small[0, 0:16, :] = small[0, 0:16, :] + v.small_in[bits, 0:16, :]
    for h in range(heads):
        for i in range(rows):
            cut = slice(i * 128, (i + 1) * 128)
            at = 16 + h * rows + i
            small[0, at : at + 1, :] = v.beta_out[0, h : h + 1, cut]
            at = at + heads * rows
            small[0, at : at + 1, :] = v.beta_in[h : h + 1, cut]
    at = 16 + 2 * heads * rows
    taps = KCONV * heads
    small[0, at : at + taps, :] = v.dkern[...].reshape(taps, hw)
    if at + taps < small.shape[1]:
        small[0, at + taps :, :] = jnp.zeros((small.shape[1] - at - taps, 128), F32)
    for bit in range(bits):
        copy = links.start(group_peer(group, bit_of, bit), small.at[bit], v.small_in.at[bit])
        pump(17 + bit)
        copy.wait()
        small[bit + 1] = small[bit] + v.small_in[bit]
    small_ref[...] = small[bits]
    pump(1000)


def backward_all(bits, given):
    span, width = given.cot[0].shape
    hidden_own = given.hidden.shape[1]
    heads, hw = given.kern.shape[0], given.kern.shape[-1]
    wide = 4 * hw
    half = span // 2
    order_a = list(range(bits))
    order_b = [1, 0] + list(range(2, bits)) if bits > 1 else order_a
    shapes = [(hidden_own, width // 2)] * 4
    shapes += [(width, hidden_own // 2)] * 8
    shapes += [(width, width // 2)] * 2
    shapes += [(width, wide)] * (2 * heads)
    peers = [False, False, True, True] * 3 + [False, False] + [False, True] * heads
    plans = [
        Reduce(order_b if i % 4 == 2 else order_a, rows >> bits, columns, peer)
        for i, ((rows, columns), peer) in enumerate(zip(shapes, peers))
    ]
    rows = (span, width)
    part = (2, half, width)
    lefts = (2,) * bits

    def like(a):
        return pltpu.VMEM(a.shape, a.dtype)

    spots = Spots(
        cot=[like(a) for a in given.cot],
        hidden=like(given.hidden),
        gate_grad=like(given.gate_grad),
        up_grad=like(given.up_grad),
        two=[like(a) for a in given.two],
        near=like(given.near),
        out_own=pltpu.VMEM((2, heads * hw, width), BF16),
        proj=like(given.proj),
        core_in=pltpu.VMEM(part, BF16),
        core_own=pltpu.VMEM(part, BF16),
        sum=pltpu.VMEM(part, BF16),
        side_in=pltpu.VMEM(part, BF16),
        mid=pltpu.VMEM(part, F32),
        mid_grad=pltpu.VMEM(part[1:], F32),
        branch=pltpu.VMEM((2,) + rows, BF16),
        heads_grad=pltpu.VMEM((heads, span, hw), BF16),
        feed_out=pltpu.VMEM(part[1:], BF16),
        feed_in=pltpu.VMEM(part[1:], BF16),
        aw=pltpu.VMEM((2, width, wide), BF16),
        dproj=pltpu.VMEM((heads, span, wide), BF16),
        logit=pltpu.VMEM((1, span, 1), F32),
        dlogit=pltpu.VMEM((1, span, 1), F32),
        dkern=pltpu.VMEM((heads, KCONV, hw), F32),
        kept=[pltpu.VMEM((1,) + a.shape[1:], a.dtype) for a in given.kept],
        left_hidden=pltpu.VMEM(lefts + (hidden_own >> bits, span), BF16),
        left=pltpu.VMEM((2,) + lefts + (width >> bits, span), BF16),
        small=pltpu.VMEM((bits + 1, SMALL, 128), F32),
        small_in=pltpu.VMEM((bits + 1, SMALL, 128), F32),
        beta_out=pltpu.VMEM((2, 8, width), F32),
        beta_in=pltpu.VMEM((8, width), F32),
        local_sem=pltpu.SemaphoreType.DMA((64,)),
        send_sem=pltpu.SemaphoreType.DMA((64,)),
        recv_sem=pltpu.SemaphoreType.DMA((64,)),
    )
    more = [s for plan in plans for s in plan.scratch()]
    seen = {}
    for plan in plans:
        key = (plan.rows, plan.columns)
        seen[key] = seen.get(key, 0) + 1
        if seen[key] <= DEEP:
            more += [pltpu.VMEM(plan.dims(1 + k), BF16) for k in range(bits)]
    out_shapes = [
        (2,) + lefts + (hidden_own >> bits, width),
        lefts + (width >> bits, 2 * hidden_own),
        lefts + (width >> bits, 2 * hidden_own),
        lefts + (width >> bits, width),
        (2 * heads,) + lefts + (width >> bits, wide),
    ]
    any_spec = pl.BlockSpec(memory_space=pl.ANY)
    vmem_spec = pl.BlockSpec(memory_space=pltpu.VMEM)
    specs = jax.tree.map(lambda _: any_spec, given)
    specs = specs._replace(
        rinv_one=vmem_spec,
        rinv_two=vmem_spec,
        gain_one=[vmem_spec] * 2,
        gain_two=[vmem_spec] * 2,
        kern=vmem_spec,
        beta=[vmem_spec] * 2,
    )
    return pl.pallas_call(
        functools.partial(back_body, bits, plans),
        in_specs=[specs],
        out_specs=[[any_spec] * 5, any_spec, any_spec, vmem_spec],
        out_shape=[
            [jax.ShapeDtypeStruct(shape, BF16) for shape in out_shapes],
            jax.ShapeDtypeStruct(rows, BF16),
            jax.ShapeDtypeStruct(rows, BF16),
            jax.ShapeDtypeStruct((SMALL, 128), F32),
        ],
        scratch_shapes=[spots, more],
        compiler_params=pltpu.CompilerParams(
            collective_id=0, has_side_effects=True, vmem_limit_bytes=62 * 2**20
        ),
        name="backward_all",
    )(given)


class Front(NamedTuple):
    inputs: Any
    cot: Any
    attn_all: Any
    out: Any
    gate: Any
    up: Any
    down: Any
    beta: Any
    gain_one: Any
    gain_two: Any
    kern: Any
    lengths: Any


class Made(NamedTuple):
    part: Any
    feed: Any
    cot: Any
    hidden: Any
    gate_grad: Any
    up_grad: Any
    two: Any
    mid: Any
    rinv_one: Any
    rinv_two: Any
    gain_one: Any
    gain_two: Any
    near: Any
    proj: Any
    logit: Any
    kept: Any
    act: Any
    x: Any
    out: Any
    attn: Any
    beta: Any


class Rooms(NamedTuple):
    x: Any
    cot: Any
    attn: Any
    out: Any
    out_far: Any
    gate: Any
    up: Any
    down: Any
    act: Any
    two: Any
    mid: Any
    proj: Any
    logit: Any
    attended: Any
    near: Any
    far: Any
    hidden: Any
    gate_grad: Any
    up_grad: Any
    part: Any
    feed: Any
    kept: Any
    local_sem: Any
    send_sem: Any
    recv_sem: Any


class Fetch:
    def __init__(self, links, group, bit_of, source, target, rows):
        self.links, self.source, self.target = links, source, target
        self.eighth = rows // 8
        self.bit_of = bit_of
        self.first, self.second = (group_peer(group, bit_of, b) for b in range(2))

    def chunk(self, one, two, which, count=1):
        start = ((one * 2 + two) * 2 + which) * self.eighth
        return pl.ds(pl.multiple_of(start, self.eighth), count * self.eighth)

    def start(self):
        rows = self.chunk(self.bit_of[0], self.bit_of[1], 0, 2)
        self.straight = self.links.start(flipped("wd"), self.source(rows), self.target(rows))
        return self

    def pass_on(self):
        self.straight.wait()
        self.sent = []
        for which in range(2):
            ref = self.target(self.chunk(self.bit_of[0], self.bit_of[1], which))
            for device in (self.first, self.second):
                self.sent.append(self.links.start(device, ref, ref))
        return self

    def pass_far(self):
        self.sent[0].wait()
        ref = self.target(self.chunk(1 - self.bit_of[0], self.bit_of[1], 0))
        self.sent.append(self.links.start(self.second, ref, ref))
        self.sent[3].wait()
        ref = self.target(self.chunk(self.bit_of[0], 1 - self.bit_of[1], 1))
        self.sent.append(self.links.start(self.first, ref, ref))
        return self

    def end(self):
        for i in (1, 2, 4, 5):
            self.sent[i].wait()


def front_body(bits, r, out, v):
    group, bit_of = own_bits(bits)
    core, side = lax.axis_index("tp"), lax.axis_index("wd")
    span, width = r.inputs.shape
    half = span // 2
    heads, hw = r.kern.shape[0], r.kern.shape[-1]
    own_width = heads * hw
    hidden_own = v.hidden.shape[1]
    model = 2 * width
    mine = pl.ds(pl.multiple_of(core * half, half), half)
    loads = Loads(v.local_sem)
    links = Links(v.send_sem, v.recv_sem)
    x_peer, c_peer = flipped("wd"), flipped("tp")
    own_cols = pl.ds(pl.multiple_of(side * hidden_own, hidden_own), hidden_own)
    other_cols = pl.ds(pl.multiple_of((1 - side) * hidden_own, hidden_own), hidden_own)

    barrier = pltpu.get_barrier_semaphore()
    for device in [group_peer(group, bit_of, b) for b in range(2)] + [x_peer, c_peer]:
        pl.semaphore_signal(barrier, inc=1, device_id=device, device_id_type=MESH)
    pl.semaphore_wait(barrier, 4)

    def fetch(source, target, rows):
        return Fetch(links, group, bit_of, source, target, rows)

    def down_rows(rows):
        start = (1 - side) * hidden_own + rows.start
        return r.down.at[pl.ds(pl.multiple_of(start, rows.size), rows.size)]

    attn = [
        fetch(
            lambda rows, h=h: r.attn_all.at[(1 - side) * heads + h, rows],
            lambda rows, h=h: v.attn[1].at[h, rows],
            width,
        )
        for h in range(heads)
    ]
    out_w = fetch(lambda rows: r.out.at[rows], lambda rows: v.out[1].at[rows], width)
    gate_w = fetch(lambda rows: r.gate.at[rows, other_cols], lambda rows: v.gate[1].at[rows], width)
    up_w = fetch(lambda rows: r.up.at[rows, other_cols], lambda rows: v.up[1].at[rows], width)
    down_w = fetch(down_rows, lambda rows: v.down[1].at[rows], hidden_own)

    x_half = links.start(x_peer, r.inputs.at[mine], v.x[1].at[mine])
    tiny = [
        links.start(x_peer, r.beta, out.beta),
        links.start(x_peer, r.gain_one, out.gain_one),
        links.start(x_peer, r.gain_two, out.gain_two),
    ]
    attn[0].start()
    got_x = loads.start(r.inputs, v.x[0])
    got_attn = [loads.start(r.attn_all.at[side * heads + h], v.attn[0].at[h]) for h in range(heads)]
    got_rest = loads.start(r.out, v.out[0])
    got_rest += loads.start(r.gate.at[:, own_cols], v.gate[0])
    got_rest += loads.start(r.up.at[:, own_cols], v.up[0])
    got_rest += loads.start(r.down.at[own_cols], v.down[0])
    got_rest += loads.start(r.cot, v.cot[0])
    out_far = [links.start(c_peer, r.out, v.out_far[0])]
    given = []

    x_half.wait()
    x_rest = links.start(c_peer, v.x[1].at[mine], v.x[1].at[mine])
    attn[1].start()
    settle(tiny)
    settle(got_x)
    x_rest.wait()
    given += loads.start(v.x[1], out.x)
    attn[0].pass_on()
    attn[2].start()
    xs = [v.x[i][...].astype(F32) for i in range(2)]
    square = sum(jnp.sum(x * x, -1, keepdims=True) for x in xs)
    rinv = lax.rsqrt(square / model + norm_eps)
    out.rinv_one[...] = rinv
    for i, gain in enumerate((r.gain_one, out.gain_one)):
        v.act[i][...] = (xs[i] * rinv * gain[...]).astype(BF16)
        given += loads.start(v.act[i], out.act[i])
    logits = dotb(v.act[0][...], r.beta[...]) + dotb(v.act[1][...], out.beta[...])
    for h in range(heads):
        v.logit[h] = jnp.where(side == 0, logits[:, h : h + 1], logits[:, heads + h : heads + h + 1])
    given += loads.start(v.logit, out.logit)
    attn[0].pass_far()
    attn[1].pass_on()
    out_w.start()
    cot_half = None
    near_in, far_in = [], []
    saved = [[], []]
    for h in range(heads):
        attn[h].end()
        given += loads.start(v.attn[1].at[h], out.attn.at[h])
        settle(got_attn[h])
        value = dotb(v.act[0][...], v.attn[0][h]) + dotb(v.act[1][...], v.attn[1][h])
        v.proj[h] = value.astype(BF16)
        if h == 0:
            attn[1].pass_far()
            attn[2].pass_on()
            gate_w.start()
        elif h == 1:
            out_w.pass_far()
            gate_w.pass_on()
            down_w.start()
        else:
            gate_w.pass_far()
            up_w.pass_on()
            cot_half = links.start(x_peer, r.cot.at[mine], v.cot[1].at[mine])
        kept = v.kept[h % 2]
        settle(saved[h % 2])
        forward_body(
            r.lengths,
            v.proj.at[h],
            v.logit.at[pl.ds(h, 1)],
            r.kern.at[pl.ds(h, 1)],
            v.attended.at[h],
            kept[0],
            kept[1],
            kept[2],
        )
        saved[h % 2] += [
            loads.start(a, b.at[pl.ds(h, 1)])[0] for a, b in zip(kept, out.kept)
        ]
        place = pl.ds(pl.multiple_of((side * heads + h) * hw, hw), hw)
        v.near[:, place] = v.attended[h]
        near_in.append(links.start(x_peer, v.near.at[:, place], v.near.at[:, place]))
        far_in.append(links.start(c_peer, v.near.at[:, place], v.far.at[:, place]))
        if h == 0:
            attn[2].pass_far()
            out_w.pass_on()
            up_w.start()
    given += loads.start(v.proj, out.proj)
    out_w.end()
    out_far.append(links.start(c_peer, v.out[1], v.out_far[1]))
    given += loads.start(v.out[1], out.out)
    for h in range(heads):
        near_in[h].wait()
        place = pl.ds(pl.multiple_of(((1 - side) * heads + h) * hw, hw), hw)
        far_in.append(links.start(c_peer, v.near.at[:, place], v.far.at[:, place]))
    given += loads.start(v.near, out.near)
    down_w.pass_on()
    up_w.pass_far()
    cot_half.wait()
    cot_rest = links.start(c_peer, v.cot[1].at[mine], v.cot[1].at[mine])
    settle(far_in)
    settle(out_far)
    settle(got_rest)

    def branch_rows(j, _):
        rows = pl.ds(pl.multiple_of(j * 256, 256), 256)
        near, far = v.near[rows, :], v.far[rows, :]
        mids = [
            v.x[i][rows, :].astype(F32) + dotb(near, v.out[i][...]) + dotb(far, v.out_far[i][...])
            for i in range(2)
        ]
        square = sum(jnp.sum(m * m, -1, keepdims=True) for m in mids)
        rinv = lax.rsqrt(square / model + norm_eps)
        out.rinv_two[rows, :] = rinv
        for i, gain in enumerate((r.gain_two, out.gain_two)):
            v.mid[i][rows, :] = mids[i]
            v.two[i][rows, :] = (mids[i] * rinv * gain[...]).astype(BF16)
        return 0

    lax.fori_loop(0, span // 256, branch_rows, 0)
    for i in range(2):
        given += loads.start(v.mid[i], out.mid[i])
        given += loads.start(v.two[i], out.two[i])
    down_w.pass_far()
    gate_w.end()
    up_w.end()
    cot_rest.wait()
    given += loads.start(v.cot[1], out.cot)
    down_w.end()

    def hidden_columns(j, _):
        cols = pl.ds(pl.multiple_of(j * 256, 256), 256)
        two = [t[...] for t in v.two]
        gate = dotb(two[0], v.gate[0][:, cols]) + dotb(two[1], v.gate[1][:, cols])
        up = dotb(two[0], v.up[0][:, cols]) + dotb(two[1], v.up[1][:, cols])
        grad = dotb(v.cot[0][...], v.down[0][cols, :], NT)
        grad = grad + dotb(v.cot[1][...], v.down[1][cols, :], NT)
        sigma = jax.nn.sigmoid(gate)
        silu = gate * sigma
        v.hidden[:, cols] = (silu * up).astype(BF16)
        v.gate_grad[:, cols] = (grad * up * sigma * (1.0 + gate * (1.0 - sigma))).astype(BF16)
        v.up_grad[:, cols] = (grad * silu).astype(BF16)
        return 0

    lax.fori_loop(0, hidden_own // 256, hidden_columns, 0)
    given += loads.start(v.hidden, out.hidden)
    given += loads.start(v.gate_grad, out.gate_grad)
    given += loads.start(v.up_grad, out.up_grad)
    for i in range(2):

        def model_columns(j, _, i=i):
            cols = pl.ds(pl.multiple_of(j * 256, 256), 256)
            value = dotb(v.gate_grad[...], v.gate[i][cols, :], NT)
            value = value + dotb(v.up_grad[...], v.up[i][cols, :], NT)
            v.part[i][:, cols] = value.astype(BF16)
            v.feed[i][:, cols] = dotb(v.hidden[...], v.down[i][:, cols]).astype(BF16)
            return 0

        lax.fori_loop(0, width // 256, model_columns, 0)
        given += loads.start(v.part[i], out.part[i])
        given += loads.start(v.feed[i], out.feed[i])
    settle(saved[0])
    settle(saved[1])
    settle(given)


def forward_all(bits, front):
    span, width = front.inputs.shape
    heads, hw = front.kern.shape[0], front.kern.shape[-1]
    wide = 4 * hw
    hidden_own = front.gate.shape[1] // 2
    rows = (span, width)
    kept = [(3, 2, HALF, HALF), (3, 2, HALF, HALF), (3, HALF, HALF)]

    def room(shape, dtype=BF16):
        return pltpu.VMEM(shape, dtype)

    def twice(shape, dtype=BF16):
        return [room(shape, dtype) for _ in range(2)]

    rooms = Rooms(
        x=twice(rows),
        cot=twice(rows),
        attn=twice((heads, width, wide)),
        out=twice((2 * heads * hw, width)),
        out_far=twice((2 * heads * hw, width)),
        gate=twice((width, hidden_own)),
        up=twice((width, hidden_own)),
        down=twice((hidden_own, width)),
        act=twice(rows),
        two=twice(rows),
        mid=twice(rows, F32),
        proj=room((heads, span, wide)),
        logit=room((heads, span, 1), F32),
        attended=room((heads, span, hw)),
        near=room((span, 2 * heads * hw)),
        far=room((span, 2 * heads * hw)),
        hidden=room((span, hidden_own)),
        gate_grad=room((span, hidden_own)),
        up_grad=room((span, hidden_own)),
        part=twice(rows),
        feed=twice(rows),
        kept=[[room((1,) + shape) for shape in kept] for _ in range(2)],
        local_sem=pltpu.SemaphoreType.DMA((64,)),
        send_sem=pltpu.SemaphoreType.DMA((96,)),
        recv_sem=pltpu.SemaphoreType.DMA((96,)),
    )

    def give(shape, dtype=BF16):
        return jax.ShapeDtypeStruct(shape, dtype)

    made = Made(
        part=[give(rows)] * 2,
        feed=[give(rows)] * 2,
        cot=give(rows),
        hidden=give((span, hidden_own)),
        gate_grad=give((span, hidden_own)),
        up_grad=give((span, hidden_own)),
        two=[give(rows)] * 2,
        mid=[give(rows, F32)] * 2,
        rinv_one=give((span, 1), F32),
        rinv_two=give((span, 1), F32),
        gain_one=give((1, width), F32),
        gain_two=give((1, width), F32),
        near=give((span, 2 * heads * hw)),
        proj=give((heads, span, wide)),
        logit=give((heads, span, 1), F32),
        kept=[give((heads,) + shape) for shape in kept],
        act=[give(rows)] * 2,
        x=give(rows),
        out=give((2 * heads * hw, width)),
        attn=give((heads, width, wide)),
        beta=give(front.beta.shape),
    )
    any_spec = pl.BlockSpec(memory_space=pl.ANY)
    vmem_spec = pl.BlockSpec(memory_space=pltpu.VMEM)
    specs = jax.tree.map(lambda _: any_spec, front)
    specs = specs._replace(
        beta=vmem_spec,
        gain_one=vmem_spec,
        gain_two=vmem_spec,
        kern=vmem_spec,
        lengths=pl.BlockSpec(memory_space=pltpu.SMEM),
    )
    out_specs = jax.tree.map(lambda _: any_spec, made)
    out_specs = out_specs._replace(
        rinv_one=vmem_spec, rinv_two=vmem_spec, gain_one=vmem_spec, gain_two=vmem_spec, beta=vmem_spec
    )
    return pl.pallas_call(
        functools.partial(front_body, bits),
        in_specs=[specs],
        out_specs=[out_specs],
        out_shape=[made],
        scratch_shapes=[rooms],
        compiler_params=pltpu.CompilerParams(
            collective_id=1, has_side_effects=True, vmem_limit_bytes=62 * 2**20
        ),
        name="forward_all",
    )(front)[0]


def on_device(
    group_count,
    inputs,
    lengths,
    gain_attn,
    attn_proj,
    beta_proj,
    conv_kernel,
    out_proj,
    gain_ffn,
    gate_proj,
    up_proj,
    down_proj,
    cotangent,
):
    width = inputs.shape[1]
    heads, hw = conv_kernel.shape[1], conv_kernel.shape[2]
    bits = group_count.bit_length() - 1
    attn_all = jnp.transpose(attn_proj, (1, 0, 2))
    out_rows = out_proj.reshape(-1, width)
    kern = jnp.transpose(conv_kernel, (1, 0, 2))
    made = forward_all(
        bits,
        Front(
            inputs=inputs,
            cot=cotangent,
            attn_all=attn_all,
            out=out_rows,
            gate=gate_proj,
            up=up_proj,
            down=down_proj,
            beta=beta_proj,
            gain_one=gain_attn[None],
            gain_two=gain_ffn[None],
            kern=kern,
            lengths=lengths,
        ),
    )
    given = Given(
        part=made.part,
        feed=made.feed,
        cot=[cotangent, made.cot],
        hidden=made.hidden,
        gate_grad=made.gate_grad,
        up_grad=made.up_grad,
        two=made.two,
        mid=made.mid,
        rinv_one=made.rinv_one,
        rinv_two=made.rinv_two,
        gain_one=[gain_attn[None], made.gain_one],
        gain_two=[gain_ffn[None], made.gain_two],
        near=made.near,
        out=[out_rows, made.out],
        proj=made.proj,
        logit=made.logit,
        kern=kern,
        kept=made.kept,
        act=made.act,
        x=[inputs, made.x],
        attn_all=attn_all,
        attn_peer=made.attn,
        beta=[beta_proj, made.beta],
    )
    (down_sum, gate_sum, up_sum, out_sum, attn_sum), outputs, grad_inputs, small = backward_all(
        bits, given
    )
    rows = width // 128
    gain_one_sum = small[0:rows].reshape(-1)
    gain_two_sum = small[8 : 8 + rows].reshape(-1)
    at = 16 + 2 * heads * rows
    beta_sum = small[16:at].reshape(2, heads, width)
    beta_sum = jnp.where(lax.axis_index("wd") == 0, beta_sum, beta_sum[::-1])
    beta_sum = beta_sum.reshape(2 * heads, width).T
    kern_sum = small[at : at + KCONV * heads].reshape(heads, KCONV, hw)
    attn_sum = attn_sum.reshape(2 * heads, width, -1)
    return (
        outputs,
        grad_inputs,
        gain_one_sum,
        jnp.transpose(attn_sum, (1, 0, 2)).astype(F32),
        beta_sum,
        jnp.transpose(kern_sum, (1, 0, 2)),
        out_sum.astype(F32).reshape(out_proj.shape),
        gain_two_sum,
        gate_sum.astype(F32).reshape(gate_proj.shape),
        up_sum.astype(F32).reshape(up_proj.shape),
        down_sum.astype(F32).reshape(down_proj.shape),
    )


def solution(mesh):
    return jax.shard_map(
        functools.partial(on_device, mesh.shape["dp"]),
        mesh=mesh,
        in_specs=(
            P("dp", "wd"),
            P("dp"),
            P("wd"),
            P("wd", "tp", None),
            P("wd", "tp"),
            P(None, ("tp", "wd"), None),
            P("tp", None, "wd"),
            P("wd"),
            P("wd", "tp"),
            P("wd", "tp"),
            P("tp", "wd"),
            P("dp", "wd"),
        ),
        out_specs=(
            P("dp", "wd"),
            P("dp", "wd"),
            P("wd"),
            P("wd", "tp", None),
            P("wd", "tp"),
            P(None, ("tp", "wd"), None),
            P("tp", None, "wd"),
            P("wd"),
            P("wd", "tp"),
            P("wd", "tp"),
            P("tp", "wd"),
        ),
        check_vma=False,
    )
```

```python
import functools
from typing import Any, NamedTuple

import jax
import jax.numpy as jnp
import numpy as np
from jax import lax
from jax.experimental import pallas as pl
from jax.experimental.pallas import tpu as pltpu
from jax.sharding import PartitionSpec as P

norm_eps = 1e-06
KCONV = 4
HALF = 256
F32 = jnp.float32
BF16 = jnp.bfloat16
NT = (((1,), (1,)), ((), ()))
NN = (((1,), (0,)), ((), ()))


def dotb(a, b, dims=NN):
    return lax.dot_general(a, b, dims, preferred_element_type=F32)


def split(a):
    hi = a.astype(BF16)
    return hi, (a - hi.astype(F32)).astype(BF16)


def dot3(a, b, dims=NN):
    (ah, al), (bh, bl) = a, b
    return dotb(ah, bh, dims) + (dotb(al, bh, dims) + dotb(ah, bl, dims))


def shift_down(a, m):
    if m == 0:
        return a
    rows = lax.broadcasted_iota(jnp.int32, a.shape, 0)
    return jnp.where(rows >= m, pltpu.roll(a, m, 0), 0.0)


def shift_up(a, m):
    if m == 0:
        return a
    n = a.shape[0]
    rows = lax.broadcasted_iota(jnp.int32, a.shape, 0)
    return jnp.where(rows < n - m, pltpu.roll(a, n - m, 0), 0.0)


def house_of(raws, kern):
    conv = kern[0:1] * raws
    for m in range(1, KCONV):
        conv = conv + kern[m : m + 1] * shift_down(raws, m)
    scale = lax.rsqrt(jnp.sum(conv * conv, -1, keepdims=True) + 1e-06)
    return conv * scale, scale


def forward_body(len_ref, proj_ref, logit_ref, kern_ref, o_ref, x_ref, w_ref, p_ref):
    length = len_ref[0]
    hw = o_ref.shape[-1]
    q = proj_ref[:, 0:hw]
    k = proj_ref[:, hw : 2 * hw]
    v = proj_ref[:, 2 * hw : 3 * hw]
    raws = proj_ref[:, 3 * hw : 4 * hw].astype(F32)
    house, _ = house_of(raws, kern_ref[0])
    beta = 2.0 * jax.nn.sigmoid(logit_ref[0])
    hh, hl = split(house)
    top, low = slice(0, HALF), slice(HALF, 2 * HALF)
    ri = lax.broadcasted_iota(jnp.int32, (HALF, HALF), 0)
    ci = lax.broadcasted_iota(jnp.int32, (HALF, HALF), 1)
    strict = ri > ci
    causal = ri >= ci
    h_left = jnp.concatenate([hh, hl, hh], 1)
    h_right = jnp.concatenate([hh, hh, hl], 1)
    h_two = jnp.concatenate([hh, hl], 1)
    k_two = jnp.concatenate([k, k], 1)
    q_two = jnp.concatenate([q, q], 1)

    def gram(a, b):
        return dotb(h_left[a], h_right[b], NT)

    def keyed(a, b):
        return dotb(h_two[a], k_two[b], NT)

    def asked(a, b):
        return dotb(q_two[a], h_two[b], NT)

    n11 = beta[top] * jnp.where(strict, gram(top, top), 0.0)
    n22 = beta[low] * jnp.where(strict, gram(low, low), 0.0)
    n21 = split(beta[low] * gram(low, top))
    inverses = [n11, n22]
    level = 1
    xor = ri ^ ci
    bits = [split(n11), split(n22)]
    current = None
    while level < HALF:
        mask = (xor >= level) & (xor < 2 * level)
        for d in range(2):
            if level == 1:
                eye = jnp.where(ri == ci, 1.0, 0.0)
                inverses[d] = eye - jnp.where(mask, inverses[d], 0.0)
            else:
                t = split(inverses[d])
                zero = jnp.zeros((), BF16)
                c = tuple(jnp.where(mask, part, zero) for part in bits[d])
                inverses[d] = inverses[d] - dot3(t, split(dot3(c, t)))
        level *= 2
    t1, t2 = split(inverses[0]), split(inverses[1])
    b11 = split(beta[top] * jnp.where(strict, keyed(top, top), 0.0))
    b22 = split(beta[low] * jnp.where(strict, keyed(low, low), 0.0))
    b21f = beta[low] * keyed(low, top)
    b21 = split(b21f)
    m11 = split(jnp.where(causal, asked(top, top), 0.0))
    m22 = split(jnp.where(causal, asked(low, low), 0.0))
    m21 = asked(low, top)
    x11 = split(dot3(t1, b11))
    x22 = split(dot3(t2, b22))
    x21 = split(dot3(t2, split(b21f - dot3(n21, x11))))
    w11 = split(dot3(m11, t1))
    w22 = split(dot3(m22, t2))
    w21 = split(dot3(split(m21 - dot3(w22, n21)), t1))
    scale = hw ** (-0.5)

    def soften(scores, allowed):
        scores = jnp.where(allowed, scores, -1e30)
        weights = jnp.exp(scores - jnp.max(scores, -1, keepdims=True))
        return (weights * (1.0 / jnp.sum(weights, -1, keepdims=True))).astype(BF16)

    s11 = (dotb(q[top], k[top], NT) - dot3(w11, b11)) * scale
    s21 = (dotb(q[low], k[top], NT) - (dot3(w21, b11) + dot3(w22, b21))) * scale
    s22 = (dotb(q[low], k[low], NT) - dot3(w22, b22)) * scale
    p1 = soften(s11, causal & (ci < length))
    p2 = soften(
        jnp.concatenate([s21, s22], 1),
        jnp.concatenate([ci < length, causal & (ci + HALF < length)], 1),
    )
    o_ref[top, :] = dotb(p1, v[top]).astype(o_ref.dtype)
    o_ref[low, :] = dotb(p2, v).astype(o_ref.dtype)
    p_ref[0, 0] = p1
    p_ref[0, 1] = p2[:, :HALF]
    p_ref[0, 2] = p2[:, HALF:]
    for i, (xx, ww) in enumerate(((x11, w11), (x21, w21), (x22, w22))):
        for j in range(2):
            x_ref[0, i, j] = xx[j]
            w_ref[0, i, j] = ww[j].T


def backward_body(proj_ref, logit_ref, kern_ref, g_ref, x_ref, w_ref, p_ref, dproj_ref, dlogit_ref, dkern_ref):
    hw = g_ref.shape[-1]
    q = proj_ref[:, 0:hw]
    k = proj_ref[:, hw : 2 * hw]
    v = proj_ref[:, 2 * hw : 3 * hw]
    raws = proj_ref[:, 3 * hw : 4 * hw].astype(F32)
    kern = kern_ref[0]
    house, rs = house_of(raws, kern)
    beta = 2.0 * jax.nn.sigmoid(logit_ref[0])
    g = g_ref[...]
    hh, hl = split(house)
    top, low = slice(0, HALF), slice(HALF, 2 * HALF)
    ri = lax.broadcasted_iota(jnp.int32, (HALF, HALF), 0)
    ci = lax.broadcasted_iota(jnp.int32, (HALF, HALF), 1)
    strict = ri > ci
    causal = ri >= ci
    scale = hw ** (-0.5)
    p11, p21, p22 = (p_ref[0, i] for i in range(3))
    x11, x21, x22 = ((x_ref[0, i, 0], x_ref[0, i, 1]) for i in range(3))
    w11, w21, w22 = ((w_ref[0, i, 0], w_ref[0, i, 1]) for i in range(3))
    q_t, g_t = q.T, g.T
    ht_h, ht_l = hh.T, hl.T

    def soften_back(probs, dprobs):
        pf = probs.astype(F32)
        mixed = pf * dprobs
        return (mixed - pf * jnp.sum(mixed, -1, keepdims=True)) * scale

    z1 = soften_back(p11, dotb(g[top], v[top], NT))
    z2 = soften_back(jnp.concatenate([p21, p22], 1), dotb(g[low], v, NT))
    z11 = split(z1)
    z21 = split(z2[:, :HALF])
    z22 = split(z2[:, HALF:])
    u11 = jnp.where(causal, dot3(z11, x11, NT), 0.0)
    u21 = dot3(z21, x11, NT)
    u22 = jnp.where(causal, dot3(z21, x21, NT) + dot3(z22, x22, NT), 0.0)
    u11, u21, u22 = split(u11), split(u21), split(u22)
    b11 = jnp.where(strict, dot3(w11, z11) + dot3(w21, z21), 0.0)
    b21 = dot3(w22, z21)
    b22 = jnp.where(strict, dot3(w22, z22), 0.0)
    a11 = jnp.where(strict, dot3(w11, u11) + dot3(w21, u21), 0.0)
    a21 = dot3(w22, u21)
    a22 = jnp.where(strict, dot3(w22, u22), 0.0)
    b11s, b21s, b22s = split(b11), split(b21), split(b22)
    a11s, a21s, a22s = split(a11), split(a21), split(a22)

    def rows(c11, c21, c22, mats):
        (mh, ml) = mats
        first = dotb(c11[0], mh[top]) + dotb(c11[1], mh[top])
        second = dotb(c21[0], mh[top]) + dotb(c21[1], mh[top])
        second = second + dotb(c22[0], mh[low]) + dotb(c22[1], mh[low])
        if ml is not None:
            first = first + dotb(c11[0], ml[top])
            second = second + dotb(c21[0], ml[top]) + dotb(c22[0], ml[low])
        return jnp.concatenate([first, second], 0)

    def cols(c11, c21, c22, mats):
        (mh, ml) = mats
        first = dotb(mh[:, top], c11[0]) + dotb(mh[:, top], c11[1])
        first = first + dotb(mh[:, low], c21[0]) + dotb(mh[:, low], c21[1])
        second = dotb(mh[:, low], c22[0]) + dotb(mh[:, low], c22[1])
        if ml is not None:
            first = first + dotb(ml[:, top], c11[0]) + dotb(ml[:, low], c21[0])
            second = second + dotb(ml[:, low], c22[0])
        return jnp.concatenate([first, second], 1)

    dq = rows(z11, z21, z22, (k, None)) - rows(u11, u21, u22, (hh, hl))
    bk = rows(b11s, b21s, b22s, (k, None))
    nh = rows(a11s, a21s, a22s, (hh, hl))
    mixed = nh - bk
    dbeta = jnp.sum(house * mixed, -1, keepdims=True)
    dlogit_ref[0] = dbeta * beta * (1.0 - 0.5 * beta)
    bb = [split(beta[s] * b) for s, b in ((top, b11), (low, b21), (low, b22))]
    ab = [split(beta[s] * a) for s, a in ((top, a11), (low, a21), (low, a22))]
    dk_t = cols(z11, z21, z22, (q_t, None)) - cols(*bb, (ht_h, ht_l))
    dh_t = cols(*ab, (ht_h, ht_l)) - cols(u11, u21, u22, (q_t, None))
    dv_t = jnp.concatenate(
        [dotb(g_t[:, top], p11) + dotb(g_t[:, low], p21), dotb(g_t[:, low], p22)], 1
    )
    dh = beta * mixed + dh_t.T
    dc = rs * (dh - house * jnp.sum(house * dh, -1, keepdims=True))
    dr = kern[0:1] * dc
    taps = [jnp.sum(dc * raws, 0, keepdims=True)]
    for m in range(1, KCONV):
        up = shift_up(dc, m)
        dr = dr + kern[m : m + 1] * up
        taps.append(jnp.sum(up * raws, 0, keepdims=True))
    dkern_ref[0] = jnp.concatenate(taps, 0)
    dproj_ref[:, 0:hw] = dq.astype(BF16)
    dproj_ref[:, hw : 2 * hw] = dk_t.T.astype(BF16)
    dproj_ref[:, 2 * hw : 3 * hw] = dv_t.T.astype(BF16)
    dproj_ref[:, 3 * hw : 4 * hw] = dr.astype(BF16)


MESH = pl.DeviceIdType.MESH
TN = (((0,), (0,)), ((), ()))


def own_bits(bits):
    group = lax.axis_index("dp")
    return group, [lax.rem(lax.div(group, 1 << b), 2) for b in range(bits)]


class Reduce:
    def __init__(self, order, rows, columns, peer):
        self.order, self.rows, self.columns, self.peer = order, rows, columns, peer
        self.bits = len(order)

    def dims(self, taken):
        return (2,) * (self.bits - taken) + (self.rows, self.columns)

    def scratch(self):
        shapes = [pltpu.VMEM(self.dims(1), BF16)]
        shapes += [pltpu.VMEM(self.dims(1 + k), BF16) for k in range(self.bits)]
        shapes += [pltpu.VMEM(self.dims(self.bits), BF16)]
        if self.peer:
            shapes += [pltpu.VMEM(self.dims(self.bits), BF16)]
        count = 2 * self.bits + 1
        return shapes + [pltpu.SemaphoreType.DMA((count,)), pltpu.SemaphoreType.DMA((count + 1,))]

    def rotating(self):
        return [pltpu.VMEM(self.dims(1 + k), BF16) for k in range(self.bits)]

    def bind(self, group, bit_of, compute, out, refs):
        self.group, self.bit_of, self.compute, self.out = group, bit_of, compute, out
        refs = list(refs)
        self.kept = refs.pop(0)
        self.recv = [refs.pop(0) for _ in range(self.bits)]
        self.shard = refs.pop(0)
        self.from_peer = refs.pop(0) if self.peer else None
        self.send_sem, self.recv_sem = refs
        stages = [functools.partial(self.halve, k) for k in range(self.bits)] + [self.finish]
        if self.peer:
            stages.append(self.take_peer)
        stages += [functools.partial(self.double, k) for k in range(1, self.bits)] + [self.end]
        self.stages = stages
        self.copies = {}
        return self

    def at(self, fixed, gone=()):
        return tuple(
            fixed.get(b, slice(None)) for b in range(self.bits - 1, -1, -1) if b not in gone
        )

    def remote(self, slot, source, target, bit=None):
        if bit is None:
            device = {"wd": 1 - lax.axis_index("wd")}
        else:
            step = 1 << bit
            device = {"dp": self.group + step - 2 * step * self.bit_of[bit]}
        copy = pltpu.make_async_remote_copy(
            src_ref=source,
            dst_ref=target,
            send_sem=self.send_sem.at[slot],
            recv_sem=self.recv_sem.at[slot],
            device_id=device,
            device_id_type=MESH,
        )
        copy.start()
        self.copies[slot] = copy

    def total(self, step, fixed, target):
        free = [b for b in range(self.bits - 1, -1, -1) if b not in fixed]
        part = 32 if self.rows % 32 == 0 else self.rows
        for combo in range(1 << len(free)):
            place = {b: (combo >> i) & 1 for i, b in enumerate(reversed(free))}
            where = {**fixed, **place}
            head = tuple(place[b] for b in free)

            def body(i, _):
                rows = pl.ds(pl.multiple_of(i * part, part), part)
                value = self.kept[self.at(where, self.order[:1]) + (rows,)].astype(F32)
                for j in range(step):
                    gone = self.order[: j + 1]
                    value = value + self.recv[j][self.at(where, gone) + (rows,)].astype(F32)
                target[head + (rows,)] = value.astype(BF16)
                return 0

            lax.fori_loop(0, self.rows // part, body, 0)

    def halve(self, k):
        bit = self.order[k]
        if k == 0:
            self.compute(self, self.at({bit: 1 - self.bit_of[bit]}), self.send[0])
        else:
            self.copies[k - 1].wait()
            fixed = {b: self.bit_of[b] for b in self.order[:k]}
            fixed[bit] = 1 - self.bit_of[bit]
            self.total(k, fixed, self.send[k])
        self.remote(k, self.send[k], self.recv[k], bit)
        if k == 0:
            self.compute(self, self.at({bit: self.bit_of[bit]}), self.kept)

    def finish(self):
        self.copies[self.bits - 1].wait()
        mine = {b: self.bit_of[b] for b in range(self.bits)}
        self.total(self.bits, mine, self.shard)
        if self.peer:
            self.remote(self.bits, self.shard, self.from_peer)
        else:
            self.begin(self.shard)

    def take_peer(self):
        self.copies[self.bits].wait()
        self.begin(self.from_peer)

    def begin(self, block):
        mine = self.at({b: self.bit_of[b] for b in range(self.bits)})
        local = pltpu.make_async_copy(block, self.out(mine), self.recv_sem.at[2 * self.bits + 1])
        local.start()
        self.copies[-1] = local
        self.remote(self.bits + 1, block, self.out(mine), self.order[-1])

    def double(self, k):
        if k == 1:
            self.copies[-1].wait()
        self.copies[self.bits + k].wait()
        bit = self.order[self.bits - 1 - k]
        fixed = {b: self.bit_of[b] for b in self.order[: self.bits - k]}
        slab = self.out(self.at(fixed))
        self.remote(self.bits + 1 + k, slab, slab, bit)

    def end(self):
        if self.bits == 1:
            self.copies[-1].wait()
        self.copies[2 * self.bits].wait()


def turned(source, target):
    rows, lead = target.shape[-2], target.shape[:-2]
    if rows % 16 == 0:
        target[...] = source[...].T.reshape(target.shape)
    else:
        value = source[...].astype(F32).T
        for i, place in enumerate(np.ndindex(*lead)):
            target[place] = value[i * rows : (i + 1) * rows].astype(BF16)


def gradient(left, right):
    def compute(piece, where, target):
        values = right()
        if piece.rows % 16 == 0:
            part = left[where]
            part = part.reshape(-1, part.shape[-1])
            target[...] = dotb(part, values).astype(BF16).reshape(target.shape)
        else:
            for place in np.ndindex(*target.shape[:-2]):
                free = iter(place)
                index = tuple(next(free) if isinstance(w, slice) else w for w in where)
                target[place] = dotb(left[index + tuple(free)], values).astype(BF16)

    return compute


class Chain:
    bits = 3
    last_z = 3

    def __init__(self, rows, columns, peer, split_first):
        self.rows, self.columns, self.peer, self.split_first = rows, columns, peer, split_first

    def scratch(self):
        block = (self.rows, self.columns)
        if self.split_first:
            shapes = [pltpu.VMEM((2,) + block, BF16)] * 2 + [pltpu.VMEM(block, BF16)] * 2
        else:
            shapes = [pltpu.VMEM((2, 2) + block, BF16)] + [pltpu.VMEM((2,) + block, BF16)] * 2
        return shapes + [pltpu.SemaphoreType.DMA((8,)), pltpu.SemaphoreType.DMA((9,))]

    def rotating(self):
        return [pltpu.VMEM((2, self.rows, self.columns), BF16)] if self.split_first else []

    def bind(self, group, bit_of, compute, out, refs):
        self.compute, self.out = compute, out
        self.group, self.y, self.z = group, bit_of[0], lax.div(group, 2)
        refs = list(refs)
        self.kept = refs.pop(0)
        if self.split_first:
            self.halved = refs.pop(0)
        self.come = refs[:2]
        self.send_sem, self.recv_sem = refs[2:]
        ends = [self.finish] + ([self.take_peer] if self.peer else [])
        if self.split_first:
            self.stages = [self.first_split, self.climb_first]
            self.stages += [self.climb_second, self.climb_third] + ends
            self.stages += [functools.partial(self.fall, k) for k in range(3)] + [self.end]
        else:
            self.stages = [self.first_whole, self.climb_second, self.climb_third, self.halve_end]
            self.stages += ends + [self.fall_start]
            self.stages += [functools.partial(self.fall, k) for k in range(3)] + [self.end]
        return self

    def hop(self, slot, source, target, step=None, axis=None):
        if axis is not None:
            device = {axis: 1 - lax.axis_index(axis)}
        elif step is None:
            device = {"dp": self.group + 1 - 2 * self.y}
        else:
            device = {"dp": self.group + 2 * step}
        return pltpu.make_async_remote_copy(
            src_ref=source,
            dst_ref=target,
            send_sem=self.send_sem.at[slot],
            recv_sem=self.recv_sem.at[slot],
            device_id=device,
            device_id_type=MESH,
        )

    def climb(self, part):
        return self.hop(part, self.kept.at[part], self.come[part], 1 if part else -1)

    def part_of_out(self, part):
        if self.split_first:
            return self.out((self.y, part))
        return self.out((part, slice(None)))

    def descend(self, part):
        ref = self.part_of_out(part)
        return self.hop(2 + part, ref, ref, -1 if part else 1)

    def across(self, part):
        ref = self.out((self.y, part)) if self.split_first else self.out((part, self.y))
        return self.hop(4 + part, ref, ref)

    def swap(self, part):
        spare = self.come[1 - part] if self.split_first else self.come[1 - part].at[1]
        block = self.kept.at[part] if self.split_first else self.kept.at[part, self.y]
        return self.hop(6, block, spare, axis="wd")

    def end_swap(self, part):
        block = self.kept.at[part, 1 - self.y]
        return self.hop(7, block, self.come[1 - part].at[0])

    def add(self, target, *others):
        part = 32 if self.rows % 32 == 0 else self.rows

        def body(i, _):
            rows = pl.ds(pl.multiple_of(i * part, part), part)
            value = target[rows].astype(F32)
            for other in others:
                value = value + other[rows].astype(F32)
            target[rows] = value.astype(BF16)
            return 0

        lax.fori_loop(0, self.rows // part, body, 0)

    def gather(self, part, first):
        if self.split_first:
            others = [self.halved.at[part]] + ([] if first else [self.come[part]])
            self.add(self.kept.at[part], *others)
        elif not first:
            for y in range(2):
                self.add(self.kept.at[part, y], self.come[part].at[y])

    def at_level(self, level, action):
        pl.when(self.z == level)(lambda: action(1))
        pl.when(self.z == self.last_z - level)(lambda: action(0))

    def first_split(self):
        self.compute(self, (1 - self.y,), self.send[0])
        self.hop(7, self.send[0], self.halved).start()
        self.compute(self, (self.y,), self.kept)

    def climb_first(self):
        self.hop(7, self.send[0], self.halved).wait()

        def action(part):
            self.gather(part, True)
            self.climb(part).start()

        self.at_level(0, action)

    def first_whole(self):
        self.compute(self, (), self.kept)
        self.at_level(0, lambda part: self.climb(part).start())

    def onwards(self, level):
        def action(part):
            self.climb(part).wait_recv()
            self.gather(part, False)
            self.climb(part).start()

        self.at_level(level, action)

    def climb_second(self):
        self.onwards(1)

    def climb_third(self):
        self.onwards(2)

    def halve_end(self):
        def action(part):
            self.climb(part).wait_recv()
            self.add(self.kept.at[part, 1 - self.y], self.come[part].at[1 - self.y])
            self.end_swap(part).start()

        self.at_level(3, action)

    def finish(self):
        def action(part):
            if self.split_first:
                self.climb(part).wait_recv()
                self.gather(part, False)
            else:
                self.end_swap(part).wait()
                self.add(
                    self.kept.at[part, self.y],
                    self.come[part].at[self.y],
                    self.come[1 - part].at[0],
                )
            if self.peer:
                self.swap(part).start()
            else:
                self.begin(part, False)

        self.at_level(3, action)

    def take_peer(self):
        def action(part):
            self.swap(part).wait()
            self.begin(part, True)

        self.at_level(3, action)

    def local(self, part, taken):
        if self.split_first:
            block = self.come[1 - part] if taken else self.kept.at[part]
            ref = self.out((self.y, part))
        else:
            block = self.come[1 - part].at[1] if taken else self.kept.at[part, self.y]
            ref = self.out((part, self.y))
        return block, ref, pltpu.make_async_copy(block, ref, self.recv_sem.at[8])

    def begin(self, part, taken):
        block, ref, copy = self.local(part, taken)
        copy.start()
        self.hop(4 + part, block, ref).start()
        if self.split_first:
            self.hop(2 + part, block, ref, -1 if part else 1).start()

    def fall_start(self):
        def action(part):
            self.local(part, self.peer)[2].wait()
            self.across(part).wait()
            self.descend(part).start()

        self.at_level(3, action)

    def fall(self, k):
        def action(part):
            self.descend(part).wait_recv()
            if k < 2:
                self.descend(part).start()
            if self.split_first:
                self.across(part).start()

        self.at_level(2 - k, action)

    def end(self):
        def sent(part):
            self.climb(part).wait_send()

        def fallen(part):
            self.descend(part).wait_send()

        def here(part):
            self.local(part, self.peer)[2].wait()

        for level in range(3):
            self.at_level(level, sent)
        for level in range(1, 4):
            self.at_level(level, fallen)
        if self.split_first:
            self.at_level(3, here)
            for part in range(2):
                self.across(part).wait()


LAG = 2
DEEP = 3
SMALL = 64
WHOLE_FIRST = (1, 3, 5, 7, 9, 11, 13, 15)


def chained(bits):
    return bits == 3


class Given(NamedTuple):
    part: Any
    feed: Any
    cot: Any
    hidden: Any
    gate_grad: Any
    up_grad: Any
    two: Any
    mid: Any
    rinv_one: Any
    rinv_two: Any
    gains: Any
    near: Any
    out: Any
    proj: Any
    logit: Any
    kern: Any
    kept: Any
    act: Any
    x: Any
    attn_all: Any
    attn_peer: Any
    beta: Any


class Spots(NamedTuple):
    cot: Any
    hidden: Any
    gate_grad: Any
    up_grad: Any
    two: Any
    near: Any
    out_own: Any
    proj: Any
    core_in: Any
    core_own: Any
    sum: Any
    side_in: Any
    mid: Any
    mid_grad: Any
    branch: Any
    heads_grad: Any
    feed_out: Any
    feed_in: Any
    aw: Any
    dproj: Any
    logit: Any
    dlogit: Any
    dkern: Any
    kept: Any
    left_hidden: Any
    left: Any
    small: Any
    small_in: Any
    beta_out: Any
    beta_in: Any
    local_sem: Any
    send_sem: Any
    recv_sem: Any


class Loads:
    def __init__(self, sems):
        self.sems, self.used = sems, 0

    def start(self, source, target):
        copy = pltpu.make_async_copy(source, target, self.sems.at[self.used])
        self.used += 1
        copy.start()
        return [copy]


class Links:
    def __init__(self, send_sems, recv_sems):
        self.send_sems, self.recv_sems, self.used = send_sems, recv_sems, 0

    def start(self, device, source, target):
        copy = pltpu.make_async_remote_copy(
            src_ref=source,
            dst_ref=target,
            send_sem=self.send_sems.at[self.used],
            recv_sem=self.recv_sems.at[self.used],
            device_id=device,
            device_id_type=MESH,
        )
        self.used += 1
        copy.start()
        return copy


def settle(copies):
    for copy in copies:
        copy.wait()
    copies.clear()


def flipped(axis):
    return {axis: 1 - lax.axis_index(axis)}


def group_peer(group, bit_of, bit):
    step = 1 << bit
    return {"dp": group + step - 2 * step * bit_of[bit]}


def back_body(bits, plans, r, outs, out_ref, gin_ref, small_ref, v, rest):
    group, bit_of = own_bits(bits)
    count = len(plans)
    core, side = lax.axis_index("tp"), lax.axis_index("wd")
    span, width = r.cot[0].shape
    half = span // 2
    wide = v.aw.shape[-1]
    hw = wide // 4
    heads = r.kern.shape[0]
    model = 2 * width
    hidden_own = r.hidden.shape[1]
    mine = pl.ds(pl.multiple_of(core * half, half), half)
    far = pl.ds(pl.multiple_of((1 - core) * half, half), half)
    loads = Loads(v.local_sem)
    links = Links(v.send_sem, v.recv_sem)
    x_peer, c_peer = flipped("wd"), flipped("tp")

    barrier = pltpu.get_barrier_semaphore()
    for device in [group_peer(group, bit_of, b) for b in range(bits)] + [x_peer, c_peer]:
        pl.semaphore_signal(barrier, inc=1, device_id=device, device_id_type=MESH)
    if chained(bits):
        z = lax.div(group, 2)

        def greet_middle(step):
            device = {"dp": group + step}
            pl.semaphore_signal(barrier, inc=1, device_id=device, device_id_type=MESH)

        pl.when(z == 1)(lambda: greet_middle(2))
        pl.when(z == 2)(lambda: greet_middle(-2))
        inside = (z == 1) | (z == 2)
        pl.when(inside)(lambda: pl.semaphore_wait(barrier, bits + 3))
        pl.when(jnp.logical_not(inside))(lambda: pl.semaphore_wait(barrier, bits + 2))
    else:
        pl.semaphore_wait(barrier, bits + 2)

    first = [links.start(c_peer, r.part[i].at[far], v.core_in.at[i]) for i in range(2)]
    got_hidden = loads.start(r.hidden, v.hidden)
    got_cot = [loads.start(r.cot[i], v.cot[i]) for i in range(2)]
    got_part = [loads.start(r.part[i].at[mine], v.core_own.at[i])[0] for i in range(2)]
    got_ffn = [loads.start(r.two[i], v.two[i])[0] for i in range(2)]
    got_ffn += loads.start(r.gate_grad, v.gate_grad)
    got_ffn += loads.start(r.up_grad, v.up_grad)
    got_mid = [loads.start(r.mid[i].at[mine], v.mid.at[i])[0] for i in range(2)]
    own_rows = pl.ds(pl.multiple_of(side * heads * hw, heads * hw), heads * hw)
    got_out = [loads.start(r.out[i].at[own_rows], v.out_own.at[i])[0] for i in range(2)]
    got_near = loads.start(r.near, v.near)
    got_proj = loads.start(r.proj, v.proj)

    def load_kept(h):
        copies = [loads.start(a.at[pl.ds(h, 1)], b)[0] for a, b in zip(r.kept, v.kept)]
        return copies + loads.start(r.logit.at[pl.ds(h, 1)], v.logit)

    got_kept = load_kept(0)

    pieces = []
    shared, used = {}, {}
    cut_width, cut_hidden = width // 2, hidden_own // 2

    def piece(left, right, view):
        plan = plans[len(pieces)]
        size = len(plan.scratch())
        own = [rest.pop(0) for _ in range(size)]
        pieces.append(plan.bind(group, bit_of, gradient(left, right), view, own))

    def columns(out, start, size):
        cols = pl.ds(pl.multiple_of(start, 128), size)
        return lambda where: out.at[where + (slice(None), cols)]

    def owner(j):
        return side if j == 0 else 1 - side

    for j in range(2):
        for i in range(2):
            cut = slice(i * cut_width, (i + 1) * cut_width)
            piece(
                v.left_hidden,
                lambda j=j, cut=cut: v.cot[j][:, cut],
                lambda where, j=j, cut=cut: outs[0].at[(owner(j),) + where + (slice(None), cut)],
            )
    for n, values in ((1, v.gate_grad), (2, v.up_grad)):
        for j in range(2):
            for i in range(2):
                cut = slice(i * cut_hidden, (i + 1) * cut_hidden)
                piece(
                    v.left.at[j],
                    lambda values=values, cut=cut: values[:, cut],
                    columns(outs[n], owner(j) * hidden_own + i * cut_hidden, cut_hidden),
                )
    for i in range(2):
        cut = slice(i * cut_width, (i + 1) * cut_width)
        piece(
            v.left.at[0],
            lambda cut=cut: v.branch[0, :, cut],
            lambda where, cut=cut: outs[3].at[where + (slice(None), cut)],
        )
    for h in range(heads):
        for j in range(2):
            piece(
                v.left.at[j],
                lambda h=h: v.dproj[h],
                lambda where, h=h, j=j: outs[4].at[(owner(j) * heads + h,) + where],
            )
    for i, plan in enumerate(plans):
        shapes = plan.rotating()
        if shapes:
            key = (plan.rows, plan.columns)
            place = shared.setdefault(key, [])
            at = used.get(key, 0)
            used[key] = at + 1
            if at < DEEP:
                place.append([rest.pop(0) for _ in shapes])
            pieces[i].send = place[at % DEEP]

    position = [0]

    def pump(until):
        last = max(i + LAG * len(p.stages) for i, p in enumerate(pieces))
        for slot in range(position[0], min(until, last)):
            for i in reversed(range(count)):
                step, off = divmod(slot - i, LAG)
                if off == 0 and 0 <= step < len(pieces[i].stages):
                    pieces[i].stages[step]()
        position[0] = max(position[0], until)

    settle(got_hidden)
    turned(v.hidden, v.left_hidden)
    settle(got_cot[0])
    pump(2)
    settle(got_part)
    settle(first)
    for i in range(2):
        v.sum[i] = (v.core_own[i].astype(F32) + v.core_in[i].astype(F32)).astype(BF16)
    first = [links.start(x_peer, v.sum.at[i], v.side_in.at[1 - i]) for i in range(2)]
    settle(got_cot[1])
    settle(got_ffn)
    for i in range(2):
        turned(v.two[i], v.left.at[i])
    pump(4)
    settle(first)
    settle(got_mid)

    def norm_back(base_of, rinv, gains):
        grads = [v.sum[i].astype(F32) + v.side_in[i].astype(F32) for i in range(2)]
        cross = sum(
            jnp.sum(grads[i] * gains[i] * base_of(i), -1, keepdims=True) for i in range(2)
        )
        cube = rinv * rinv * rinv * cross / model
        backs = [grads[i] * gains[i] * rinv - base_of(i) * cube for i in range(2)]
        return backs, jnp.sum(grads[0] * base_of(0) * rinv, 0, keepdims=True)

    gains = [g[1:2, :] for g in r.gains]
    backs, gain_two = norm_back(lambda i: v.mid[i], r.rinv_two[mine, :], gains)
    for i in range(2):
        value = v.cot[i][mine, :].astype(F32) + backs[i]
        if i == 0:
            v.mid_grad[...] = value
        v.branch[i, mine, :] = value.astype(BF16)
    first = [links.start(c_peer, v.branch.at[i, mine], v.branch.at[i, mine]) for i in range(2)]
    pump(5)
    settle(first)
    settle(got_out)
    grad = dotb(v.branch[0], v.out_own[0], NT) + dotb(v.branch[1], v.out_own[1], NT)
    for h in range(heads):
        v.heads_grad[h] = grad[:, h * hw : (h + 1) * hw].astype(BF16)
    first = [links.start(c_peer, r.feed[i].at[far], v.core_in.at[i]) for i in range(2)]
    got_part = [loads.start(r.feed[i].at[mine], v.core_own.at[i])[0] for i in range(2)]
    pump(6)
    settle(first)
    settle(got_part)
    feed = [v.core_own[i].astype(F32) + v.core_in[i].astype(F32) for i in range(2)]
    v.feed_out[...] = feed[1].astype(BF16)
    v.mid[0] = v.mid[0] + feed[0]
    first = [links.start(x_peer, v.feed_out, v.feed_in)]
    settle(got_proj)
    lanes = lax.broadcasted_iota(jnp.int32, (span, 128), 1)
    grad_beta = jnp.zeros((span, 128), F32)
    got_x = []

    def give_outputs():
        settle(first)
        v.feed_out[...] = (v.mid[0] + v.feed_in[...].astype(F32)).astype(BF16)
        first.append(links.start(c_peer, v.feed_out, out_ref.at[mine]))
        first.extend(loads.start(v.feed_out, out_ref.at[mine]))

    def take_inputs():
        settle(first)
        got_x.extend(loads.start(r.x[i].at[mine], v.core_own.at[i])[0] for i in range(2))

    for h in range(heads):
        settle(got_kept)
        got_aw = loads.start(r.attn_all.at[side * heads + h], v.aw.at[0])
        got_aw += loads.start(r.attn_peer.at[h], v.aw.at[1])
        backward_body(
            v.proj.at[h],
            v.logit,
            r.kern.at[pl.ds(h, 1)],
            v.heads_grad.at[h],
            v.kept[0],
            v.kept[1],
            v.kept[2],
            v.dproj.at[h],
            v.dlogit,
            v.dkern.at[pl.ds(h, 1)],
        )
        grad_beta = grad_beta + jnp.where(lanes == side * heads + h, v.dlogit[0], 0.0)
        if h + 1 < heads:
            got_kept = load_kept(h + 1)
        settle(got_aw)
        for i in range(2):
            value = dotb(v.dproj[h], v.aw[i], NT)
            if h > 0:
                value = value + v.cot[i][...].astype(F32)
            if h == heads - 1:
                low = grad_beta.astype(BF16)
                value = value + dotb(low[:, : 2 * heads], r.beta[i][...])
            v.cot[i][...] = value.astype(BF16)
        pump(7 + h)
        if h == 0:
            give_outputs()
        if h == min(1, heads - 1):
            take_inputs()
    beta_low = grad_beta.astype(BF16)
    first = [links.start(c_peer, v.cot[i].at[far], v.core_in.at[i]) for i in range(2)]
    pump(12)
    settle(got_near)
    turned(v.near, v.left.at[0])
    settle(first)
    for i in range(2):
        total = v.cot[i][mine, :].astype(F32) + v.core_in[i].astype(F32)
        v.sum[i] = total.astype(BF16)
    first = [links.start(x_peer, v.sum.at[i], v.side_in.at[1 - i]) for i in range(2)]
    pump(14)
    got_act = [loads.start(r.act[i], v.two[i])[0] for i in range(2)]
    settle(got_act)
    for i in range(2):
        turned(v.two[i], v.left.at[i])
    pump(15)
    settle(first)
    settle(got_x)
    gains = [g[0:1, :] for g in r.gains]
    backs, gain_one = norm_back(lambda i: v.core_own[i].astype(F32), r.rinv_one[mine, :], gains)
    v.feed_out[...] = (v.mid_grad[...] + backs[0]).astype(BF16)
    first = [links.start(c_peer, v.feed_out, gin_ref.at[mine])]
    first += loads.start(v.feed_out, gin_ref.at[mine])
    rows = width // 128
    small = v.small
    for i in range(rows):
        cut = slice(i * 128, (i + 1) * 128)
        small[0, i : i + 1, :] = gain_one[:, cut]
        small[0, 8 + i : 9 + i, :] = gain_two[:, cut]
    small[0, rows:8, :] = jnp.zeros((8 - rows, 128), F32)
    small[0, 8 + rows : 16, :] = jnp.zeros((8 - rows, 128), F32)
    gain_rows = pl.ds(0, 16)
    first.append(links.start(c_peer, small.at[0, gain_rows], v.small_in.at[bits, gain_rows]))
    for i in range(2):
        value = lax.dot_general(beta_low, v.two[i][...], TN, preferred_element_type=F32)
        v.beta_out[i] = jnp.where(side == 0, value[0:8], value[heads : heads + 8])
    first.append(links.start(x_peer, v.beta_out.at[1], v.beta_in))
    pump(16)
    settle(first)
    small[0, 0:16, :] = small[0, 0:16, :] + v.small_in[bits, 0:16, :]
    for h in range(heads):
        for i in range(rows):
            cut = slice(i * 128, (i + 1) * 128)
            at = 16 + h * rows + i
            small[0, at : at + 1, :] = v.beta_out[0, h : h + 1, cut]
            at = at + heads * rows
            small[0, at : at + 1, :] = v.beta_in[h : h + 1, cut]
    at = 16 + 2 * heads * rows
    taps = KCONV * heads
    small[0, at : at + taps, :] = v.dkern[...].reshape(taps, hw)
    if at + taps < small.shape[1]:
        small[0, at + taps :, :] = jnp.zeros((small.shape[1] - at - taps, 128), F32)
    for bit in range(bits):
        copy = links.start(group_peer(group, bit_of, bit), small.at[bit], v.small_in.at[bit])
        pump(17 + bit)
        copy.wait()
        small[bit + 1] = small[bit] + v.small_in[bit]
    small_ref[...] = small[bits]
    pump(1000)


def backward_all(bits, given):
    span, width = given.cot[0].shape
    hidden_own = given.hidden.shape[1]
    heads, hw = given.kern.shape[0], given.kern.shape[-1]
    wide = 4 * hw
    half = span // 2
    order_a = list(range(bits))
    order_b = [1, 0] + list(range(2, bits)) if bits > 1 else order_a
    shapes = [(hidden_own, width // 2)] * 4
    shapes += [(width, hidden_own // 2)] * 8
    shapes += [(width, width // 2)] * 2
    shapes += [(width, wide)] * (2 * heads)
    peers = [False, False, True, True] * 3 + [False, False] + [False, True] * heads
    plans = []
    for i, ((rows, columns), peer) in enumerate(zip(shapes, peers)):
        if chained(bits):
            plans.append(Chain(rows // 4, columns, peer, i not in WHOLE_FIRST))
        else:
            order = order_b if i % 4 == 2 else order_a
            plans.append(Reduce(order, rows >> bits, columns, peer))
    rows = (span, width)
    part = (2, half, width)
    lefts = (2, 2) if chained(bits) else (2,) * bits
    cuts = 2 ** len(lefts)

    def like(a):
        return pltpu.VMEM(a.shape, a.dtype)

    spots = Spots(
        cot=[like(a) for a in given.cot],
        hidden=like(given.hidden),
        gate_grad=like(given.gate_grad),
        up_grad=like(given.up_grad),
        two=[like(a) for a in given.two],
        near=like(given.near),
        out_own=pltpu.VMEM((2, heads * hw, width), BF16),
        proj=like(given.proj),
        core_in=pltpu.VMEM(part, BF16),
        core_own=pltpu.VMEM(part, BF16),
        sum=pltpu.VMEM(part, BF16),
        side_in=pltpu.VMEM(part, BF16),
        mid=pltpu.VMEM(part, F32),
        mid_grad=pltpu.VMEM(part[1:], F32),
        branch=pltpu.VMEM((2,) + rows, BF16),
        heads_grad=pltpu.VMEM((heads, span, hw), BF16),
        feed_out=pltpu.VMEM(part[1:], BF16),
        feed_in=pltpu.VMEM(part[1:], BF16),
        aw=pltpu.VMEM((2, width, wide), BF16),
        dproj=pltpu.VMEM((heads, span, wide), BF16),
        logit=pltpu.VMEM((1, span, 1), F32),
        dlogit=pltpu.VMEM((1, span, 1), F32),
        dkern=pltpu.VMEM((heads, KCONV, hw), F32),
        kept=[pltpu.VMEM((1,) + a.shape[1:], a.dtype) for a in given.kept],
        left_hidden=pltpu.VMEM(lefts + (hidden_own // cuts, span), BF16),
        left=pltpu.VMEM((2,) + lefts + (width // cuts, span), BF16),
        small=pltpu.VMEM((bits + 1, SMALL, 128), F32),
        small_in=pltpu.VMEM((bits + 1, SMALL, 128), F32),
        beta_out=pltpu.VMEM((2, 8, width), F32),
        beta_in=pltpu.VMEM((8, width), F32),
        local_sem=pltpu.SemaphoreType.DMA((64,)),
        send_sem=pltpu.SemaphoreType.DMA((64,)),
        recv_sem=pltpu.SemaphoreType.DMA((64,)),
    )
    more = [s for plan in plans for s in plan.scratch()]
    seen = {}
    for plan in plans:
        key = (plan.rows, plan.columns)
        if plan.rotating():
            seen[key] = seen.get(key, 0) + 1
            if seen[key] <= DEEP:
                more += plan.rotating()
    out_shapes = [
        (2,) + lefts + (hidden_own // cuts, width),
        lefts + (width // cuts, 2 * hidden_own),
        lefts + (width // cuts, 2 * hidden_own),
        lefts + (width // cuts, width),
        (2 * heads,) + lefts + (width // cuts, wide),
    ]
    any_spec = pl.BlockSpec(memory_space=pl.ANY)
    vmem_spec = pl.BlockSpec(memory_space=pltpu.VMEM)
    specs = jax.tree.map(lambda _: any_spec, given)
    specs = specs._replace(
        rinv_one=vmem_spec,
        rinv_two=vmem_spec,
        gains=[vmem_spec] * 2,
        kern=vmem_spec,
        beta=[vmem_spec] * 2,
    )
    return pl.pallas_call(
        functools.partial(back_body, bits, plans),
        in_specs=[specs],
        out_specs=[[any_spec] * 5, any_spec, any_spec, vmem_spec],
        out_shape=[
            [jax.ShapeDtypeStruct(shape, BF16) for shape in out_shapes],
            jax.ShapeDtypeStruct(rows, BF16),
            jax.ShapeDtypeStruct(rows, BF16),
            jax.ShapeDtypeStruct((SMALL, 128), F32),
        ],
        scratch_shapes=[spots, more],
        compiler_params=pltpu.CompilerParams(
            collective_id=0, has_side_effects=True, vmem_limit_bytes=62 * 2**20
        ),
        name="backward_all",
    )(given)


class Front(NamedTuple):
    inputs: Any
    cot: Any
    attn_all: Any
    out: Any
    gate: Any
    up: Any
    down: Any
    beta: Any
    gains: Any
    kern: Any
    lengths: Any


class Made(NamedTuple):
    part: Any
    feed: Any
    cot: Any
    hidden: Any
    gate_grad: Any
    up_grad: Any
    two: Any
    mid: Any
    rinv_one: Any
    rinv_two: Any
    gains: Any
    near: Any
    proj: Any
    logit: Any
    kept: Any
    act: Any
    x: Any
    out: Any
    attn: Any
    beta: Any


class Rooms(NamedTuple):
    x: Any
    cot: Any
    attn: Any
    out: Any
    out_far: Any
    gate: Any
    up: Any
    down: Any
    act: Any
    two: Any
    mid: Any
    proj: Any
    logit: Any
    attended: Any
    near: Any
    far: Any
    hidden: Any
    gate_grad: Any
    up_grad: Any
    slope: Any
    silu: Any
    part: Any
    feed: Any
    kept: Any
    local_sem: Any
    send_sem: Any
    recv_sem: Any


class Fetch:
    def __init__(self, links, group, bit_of, source, target, rows):
        self.links, self.source, self.target = links, source, target
        self.eighth = rows // 8
        self.bit_of = bit_of
        self.first, self.second = (group_peer(group, bit_of, b) for b in range(2))

    def chunk(self, one, two, which, count=1):
        start = ((one * 2 + two) * 2 + which) * self.eighth
        return pl.ds(pl.multiple_of(start, self.eighth), count * self.eighth)

    def start(self):
        rows = self.chunk(self.bit_of[0], self.bit_of[1], 0, 2)
        self.straight = self.links.start(flipped("wd"), self.source(rows), self.target(rows))
        return self

    def pass_on(self):
        self.straight.wait()
        self.sent = []
        for which in range(2):
            ref = self.target(self.chunk(self.bit_of[0], self.bit_of[1], which))
            for device in (self.first, self.second):
                self.sent.append(self.links.start(device, ref, ref))
        return self

    def pass_far(self):
        self.sent[0].wait()
        ref = self.target(self.chunk(1 - self.bit_of[0], self.bit_of[1], 0))
        self.sent.append(self.links.start(self.second, ref, ref))
        self.sent[3].wait()
        ref = self.target(self.chunk(self.bit_of[0], 1 - self.bit_of[1], 1))
        self.sent.append(self.links.start(self.first, ref, ref))
        return self

    def end(self):
        for i in (1, 2, 4, 5):
            self.sent[i].wait()


def front_body(bits, r, out, v):
    group, bit_of = own_bits(bits)
    core, side = lax.axis_index("tp"), lax.axis_index("wd")
    span, width = r.inputs.shape
    half = span // 2
    heads, hw = r.kern.shape[0], r.kern.shape[-1]
    own_width = heads * hw
    hidden_own = v.hidden.shape[1]
    model = 2 * width
    mine = pl.ds(pl.multiple_of(core * half, half), half)
    loads = Loads(v.local_sem)
    links = Links(v.send_sem, v.recv_sem)
    x_peer, c_peer = flipped("wd"), flipped("tp")
    own_cols = pl.ds(pl.multiple_of(side * hidden_own, hidden_own), hidden_own)
    other_cols = pl.ds(pl.multiple_of((1 - side) * hidden_own, hidden_own), hidden_own)

    barrier = pltpu.get_barrier_semaphore()
    for device in [group_peer(group, bit_of, b) for b in range(2)] + [x_peer, c_peer]:
        pl.semaphore_signal(barrier, inc=1, device_id=device, device_id_type=MESH)
    pl.semaphore_wait(barrier, 4)

    def fetch(source, target, rows):
        return Fetch(links, group, bit_of, source, target, rows)

    def down_rows(rows):
        start = (1 - side) * hidden_own + rows.start
        return r.down.at[pl.ds(pl.multiple_of(start, rows.size), rows.size)]

    attn = [
        fetch(
            lambda rows, h=h: r.attn_all.at[(1 - side) * heads + h, rows],
            lambda rows, h=h: v.attn[1].at[h, rows],
            width,
        )
        for h in range(heads)
    ]
    out_w = fetch(lambda rows: r.out.at[rows], lambda rows: v.out[1].at[rows], width)
    gate_w = fetch(lambda rows: r.gate.at[rows, other_cols], lambda rows: v.gate[1].at[rows], width)
    up_w = fetch(lambda rows: r.up.at[rows, other_cols], lambda rows: v.up[1].at[rows], width)
    down_w = fetch(down_rows, lambda rows: v.down[1].at[rows], hidden_own)

    attn[0].start()
    x_half = links.start(x_peer, r.inputs.at[mine], v.x[1].at[mine])
    tiny = [links.start(x_peer, r.beta, out.beta), links.start(x_peer, r.gains, out.gains)]
    attn[1].start()
    got_x = loads.start(r.inputs, v.x[0])
    got_attn = [loads.start(r.attn_all.at[side * heads + h], v.attn[0].at[h]) for h in range(heads)]
    got_rest = loads.start(r.out, v.out[0])
    got_rest += loads.start(r.gate.at[:, own_cols], v.gate[0])
    got_rest += loads.start(r.up.at[:, own_cols], v.up[0])
    got_rest += loads.start(r.down.at[own_cols], v.down[0])
    got_rest += loads.start(r.cot, v.cot[0])
    out_far = [links.start(c_peer, r.out, v.out_far[0])]
    given = []

    attn[0].pass_on()
    attn[2].start()
    x_half.wait()
    x_rest = links.start(c_peer, v.x[1].at[mine], v.x[1].at[mine])
    settle(tiny)
    settle(got_x)
    x_rest.wait()
    out_w.start()
    attn[0].pass_far()
    given += loads.start(v.x[1], out.x)
    xs = [v.x[i][...].astype(F32) for i in range(2)]
    square = sum(jnp.sum(x * x, -1, keepdims=True) for x in xs)
    rinv = lax.rsqrt(square / model + norm_eps)
    out.rinv_one[...] = rinv
    for i, gains in enumerate((r.gains, out.gains)):
        v.act[i][...] = (xs[i] * rinv * gains[0:1, :]).astype(BF16)
        given += loads.start(v.act[i], out.act[i])
    logits = dotb(v.act[0][...], r.beta[...], NT) + dotb(v.act[1][...], out.beta[...], NT)
    for h in range(heads):
        v.logit[h] = jnp.where(side == 0, logits[:, h : h + 1], logits[:, heads + h : heads + h + 1])
    given += loads.start(v.logit, out.logit)
    attn[1].pass_on()
    gate_w.start()
    cot_half = []
    near_in, far_in = [], []
    saved = [[], []]
    before = [
        [attn[1].pass_far, attn[2].pass_on, up_w.start],
        [out_w.pass_far, gate_w.pass_on, down_w.start],
        [gate_w.pass_far, up_w.pass_on],
    ]
    afterwards = [
        [attn[2].pass_far, out_w.pass_on],
        [lambda: cot_half.append(links.start(x_peer, r.cot.at[mine], v.cot[1].at[mine]))],
        [up_w.pass_far, down_w.pass_on],
    ]
    for h in range(heads):
        attn[h].end()
        given += loads.start(v.attn[1].at[h], out.attn.at[h])
        settle(got_attn[h])
        value = dotb(v.act[0][...], v.attn[0][h]) + dotb(v.act[1][...], v.attn[1][h])
        v.proj[h] = value.astype(BF16)
        for step in before[h]:
            step()
        kept = v.kept[h % 2]
        settle(saved[h % 2])
        forward_body(
            r.lengths,
            v.proj.at[h],
            v.logit.at[pl.ds(h, 1)],
            r.kern.at[pl.ds(h, 1)],
            v.attended.at[h],
            kept[0],
            kept[1],
            kept[2],
        )
        saved[h % 2] += [
            loads.start(a, b.at[pl.ds(h, 1)])[0] for a, b in zip(kept, out.kept)
        ]
        place = pl.ds(pl.multiple_of((side * heads + h) * hw, hw), hw)
        v.near[:, place] = v.attended[h]
        near_in.append(links.start(x_peer, v.near.at[:, place], v.near.at[:, place]))
        far_in.append(links.start(c_peer, v.near.at[:, place], v.far.at[:, place]))
        for step in afterwards[h]:
            step()
    given += loads.start(v.proj, out.proj)
    out_w.end()
    out_far.append(links.start(c_peer, v.out[1], v.out_far[1]))
    given += loads.start(v.out[1], out.out)
    for h in range(heads):
        near_in[h].wait()
        place = pl.ds(pl.multiple_of(((1 - side) * heads + h) * hw, hw), hw)
        far_in.append(links.start(c_peer, v.near.at[:, place], v.far.at[:, place]))
    given += loads.start(v.near, out.near)
    cot_half[0].wait()
    cot_rest = links.start(c_peer, v.cot[1].at[mine], v.cot[1].at[mine])
    settle(far_in)
    settle(out_far)
    settle(got_rest)

    def branch_rows(j, _):
        rows = pl.ds(pl.multiple_of(j * 256, 256), 256)
        near, far = v.near[rows, :], v.far[rows, :]
        mids = [
            v.x[i][rows, :].astype(F32) + dotb(near, v.out[i][...]) + dotb(far, v.out_far[i][...])
            for i in range(2)
        ]
        square = sum(jnp.sum(m * m, -1, keepdims=True) for m in mids)
        rinv = lax.rsqrt(square / model + norm_eps)
        out.rinv_two[rows, :] = rinv
        for i, gains in enumerate((r.gains, out.gains)):
            v.mid[i][rows, :] = mids[i]
            v.two[i][rows, :] = (mids[i] * rinv * gains[1:2, :]).astype(BF16)
        return 0

    lax.fori_loop(0, span // 256, branch_rows, 0)
    for i in range(2):
        given += loads.start(v.mid[i], out.mid[i])
        given += loads.start(v.two[i], out.two[i])
    down_w.pass_far()
    gate_w.end()
    up_w.end()

    def hidden_columns(j, _):
        cols = pl.ds(pl.multiple_of(j * 256, 256), 256)
        two = [t[...] for t in v.two]
        gate = dotb(two[0], v.gate[0][:, cols]) + dotb(two[1], v.gate[1][:, cols])
        up = dotb(two[0], v.up[0][:, cols]) + dotb(two[1], v.up[1][:, cols])
        sigma = jax.nn.sigmoid(gate)
        silu = gate * sigma
        v.hidden[:, cols] = (silu * up).astype(BF16)
        v.slope[:, cols] = up * sigma * (1.0 + gate * (1.0 - sigma))
        v.silu[:, cols] = silu
        return 0

    lax.fori_loop(0, hidden_own // 256, hidden_columns, 0)
    cot_rest.wait()
    given += loads.start(v.cot[1], out.cot)
    down_w.end()

    def grad_columns(j, _):
        cols = pl.ds(pl.multiple_of(j * 256, 256), 256)
        grad = dotb(v.cot[0][...], v.down[0][cols, :], NT)
        grad = grad + dotb(v.cot[1][...], v.down[1][cols, :], NT)
        v.gate_grad[:, cols] = (grad * v.slope[:, cols]).astype(BF16)
        v.up_grad[:, cols] = (grad * v.silu[:, cols]).astype(BF16)
        return 0

    lax.fori_loop(0, hidden_own // 256, grad_columns, 0)
    given += loads.start(v.hidden, out.hidden)
    given += loads.start(v.gate_grad, out.gate_grad)
    given += loads.start(v.up_grad, out.up_grad)
    for i in range(2):

        def model_columns(j, _, i=i):
            cols = pl.ds(pl.multiple_of(j * 256, 256), 256)
            value = dotb(v.gate_grad[...], v.gate[i][cols, :], NT)
            value = value + dotb(v.up_grad[...], v.up[i][cols, :], NT)
            v.part[i][:, cols] = value.astype(BF16)
            v.feed[i][:, cols] = dotb(v.hidden[...], v.down[i][:, cols]).astype(BF16)
            return 0

        lax.fori_loop(0, width // 256, model_columns, 0)
        given += loads.start(v.part[i], out.part[i])
        given += loads.start(v.feed[i], out.feed[i])
    settle(saved[0])
    settle(saved[1])
    settle(given)


def forward_all(bits, front):
    span, width = front.inputs.shape
    heads, hw = front.kern.shape[0], front.kern.shape[-1]
    wide = 4 * hw
    hidden_own = front.gate.shape[1] // 2
    rows = (span, width)
    kept = [(3, 2, HALF, HALF), (3, 2, HALF, HALF), (3, HALF, HALF)]

    def room(shape, dtype=BF16):
        return pltpu.VMEM(shape, dtype)

    def twice(shape, dtype=BF16):
        return [room(shape, dtype) for _ in range(2)]

    rooms = Rooms(
        x=twice(rows),
        cot=twice(rows),
        attn=twice((heads, width, wide)),
        out=twice((2 * heads * hw, width)),
        out_far=twice((2 * heads * hw, width)),
        gate=twice((width, hidden_own)),
        up=twice((width, hidden_own)),
        down=twice((hidden_own, width)),
        act=twice(rows),
        two=twice(rows),
        mid=twice(rows, F32),
        proj=room((heads, span, wide)),
        logit=room((heads, span, 1), F32),
        attended=room((heads, span, hw)),
        near=room((span, 2 * heads * hw)),
        far=room((span, 2 * heads * hw)),
        hidden=room((span, hidden_own)),
        gate_grad=room((span, hidden_own)),
        up_grad=room((span, hidden_own)),
        slope=room((span, hidden_own), F32),
        silu=room((span, hidden_own), F32),
        part=twice(rows),
        feed=twice(rows),
        kept=[[room((1,) + shape) for shape in kept] for _ in range(2)],
        local_sem=pltpu.SemaphoreType.DMA((64,)),
        send_sem=pltpu.SemaphoreType.DMA((96,)),
        recv_sem=pltpu.SemaphoreType.DMA((96,)),
    )

    def give(shape, dtype=BF16):
        return jax.ShapeDtypeStruct(shape, dtype)

    made = Made(
        part=[give(rows)] * 2,
        feed=[give(rows)] * 2,
        cot=give(rows),
        hidden=give((span, hidden_own)),
        gate_grad=give((span, hidden_own)),
        up_grad=give((span, hidden_own)),
        two=[give(rows)] * 2,
        mid=[give(rows, F32)] * 2,
        rinv_one=give((span, 1), F32),
        rinv_two=give((span, 1), F32),
        gains=give((2, width), F32),
        near=give((span, 2 * heads * hw)),
        proj=give((heads, span, wide)),
        logit=give((heads, span, 1), F32),
        kept=[give((heads,) + shape) for shape in kept],
        act=[give(rows)] * 2,
        x=give(rows),
        out=give((2 * heads * hw, width)),
        attn=give((heads, width, wide)),
        beta=give(front.beta.shape),
    )
    any_spec = pl.BlockSpec(memory_space=pl.ANY)
    vmem_spec = pl.BlockSpec(memory_space=pltpu.VMEM)
    specs = jax.tree.map(lambda _: any_spec, front)
    specs = specs._replace(
        beta=vmem_spec,
        gains=vmem_spec,
        kern=vmem_spec,
        lengths=pl.BlockSpec(memory_space=pltpu.SMEM),
    )
    out_specs = jax.tree.map(lambda _: any_spec, made)
    out_specs = out_specs._replace(
        rinv_one=vmem_spec, rinv_two=vmem_spec, gains=vmem_spec, beta=vmem_spec
    )
    return pl.pallas_call(
        functools.partial(front_body, bits),
        in_specs=[specs],
        out_specs=[out_specs],
        out_shape=[made],
        scratch_shapes=[rooms],
        compiler_params=pltpu.CompilerParams(
            collective_id=1, has_side_effects=True, vmem_limit_bytes=62 * 2**20
        ),
        name="forward_all",
    )(front)[0]


def on_device(
    group_count,
    inputs,
    lengths,
    gain_attn,
    attn_proj,
    beta_proj,
    conv_kernel,
    out_proj,
    gain_ffn,
    gate_proj,
    up_proj,
    down_proj,
    cotangent,
):
    width = inputs.shape[1]
    heads, hw = conv_kernel.shape[1], conv_kernel.shape[2]
    bits = group_count.bit_length() - 1
    attn_all = jnp.transpose(attn_proj, (1, 0, 2))
    out_rows = out_proj.reshape(-1, width)
    kern = jnp.transpose(conv_kernel, (1, 0, 2))
    beta_rows = beta_proj.T
    gains = jnp.stack([gain_attn, gain_ffn])
    made = forward_all(
        bits,
        Front(
            inputs=inputs,
            cot=cotangent,
            attn_all=attn_all,
            out=out_rows,
            gate=gate_proj,
            up=up_proj,
            down=down_proj,
            beta=beta_rows,
            gains=gains,
            kern=kern,
            lengths=lengths,
        ),
    )
    given = Given(
        part=made.part,
        feed=made.feed,
        cot=[cotangent, made.cot],
        hidden=made.hidden,
        gate_grad=made.gate_grad,
        up_grad=made.up_grad,
        two=made.two,
        mid=made.mid,
        rinv_one=made.rinv_one,
        rinv_two=made.rinv_two,
        gains=[gains, made.gains],
        near=made.near,
        out=[out_rows, made.out],
        proj=made.proj,
        logit=made.logit,
        kern=kern,
        kept=made.kept,
        act=made.act,
        x=[inputs, made.x],
        attn_all=attn_all,
        attn_peer=made.attn,
        beta=[beta_rows, made.beta],
    )
    (down_sum, gate_sum, up_sum, out_sum, attn_sum), outputs, grad_inputs, small = backward_all(
        bits, given
    )
    rows = width // 128
    gain_one_sum = small[0:rows].reshape(-1)
    gain_two_sum = small[8 : 8 + rows].reshape(-1)
    at = 16 + 2 * heads * rows
    beta_sum = small[16:at].reshape(2, heads, width)
    beta_sum = jnp.where(lax.axis_index("wd") == 0, beta_sum, beta_sum[::-1])
    beta_sum = beta_sum.reshape(2 * heads, width).T
    kern_sum = small[at : at + KCONV * heads].reshape(heads, KCONV, hw)
    attn_sum = attn_sum.reshape(2 * heads, width, -1)
    return (
        outputs,
        grad_inputs,
        gain_one_sum,
        jnp.transpose(attn_sum, (1, 0, 2)).astype(F32),
        beta_sum,
        jnp.transpose(kern_sum, (1, 0, 2)),
        out_sum.astype(F32).reshape(out_proj.shape),
        gain_two_sum,
        gate_sum.astype(F32).reshape(gate_proj.shape),
        up_sum.astype(F32).reshape(up_proj.shape),
        down_sum.astype(F32).reshape(down_proj.shape),
    )


def solution(mesh):
    return jax.shard_map(
        functools.partial(on_device, mesh.shape["dp"]),
        mesh=mesh,
        in_specs=(
            P("dp", "wd"),
            P("dp"),
            P("wd"),
            P("wd", "tp", None),
            P("wd", "tp"),
            P(None, ("tp", "wd"), None),
            P("tp", None, "wd"),
            P("wd"),
            P("wd", "tp"),
            P("wd", "tp"),
            P("tp", "wd"),
            P("dp", "wd"),
        ),
        out_specs=(
            P("dp", "wd"),
            P("dp", "wd"),
            P("wd"),
            P("wd", "tp", None),
            P("wd", "tp"),
            P(None, ("tp", "wd"), None),
            P("tp", None, "wd"),
            P("wd"),
            P("wd", "tp"),
            P("wd", "tp"),
            P("tp", "wd"),
        ),
        check_vma=False,
    )
```

```python
import functools
from typing import Any, NamedTuple

import jax
import jax.numpy as jnp
import numpy as np
from jax import lax
from jax.experimental import pallas as pl
from jax.experimental.pallas import tpu as pltpu
from jax.sharding import PartitionSpec as P

norm_eps = 1e-06
KCONV = 4
HALF = 256
F32 = jnp.float32
BF16 = jnp.bfloat16
NT = (((1,), (1,)), ((), ()))
NN = (((1,), (0,)), ((), ()))


def dotb(a, b, dims=NN):
    return lax.dot_general(a, b, dims, preferred_element_type=F32)


def split(a):
    hi = a.astype(BF16)
    return hi, (a - hi.astype(F32)).astype(BF16)


def dot3(a, b, dims=NN):
    (ah, al), (bh, bl) = a, b
    return dotb(ah, bh, dims) + (dotb(al, bh, dims) + dotb(ah, bl, dims))


def shift_down(a, m):
    if m == 0:
        return a
    rows = lax.broadcasted_iota(jnp.int32, a.shape, 0)
    return jnp.where(rows >= m, pltpu.roll(a, m, 0), 0.0)


def shift_up(a, m):
    if m == 0:
        return a
    n = a.shape[0]
    rows = lax.broadcasted_iota(jnp.int32, a.shape, 0)
    return jnp.where(rows < n - m, pltpu.roll(a, n - m, 0), 0.0)


def house_of(raws, kern):
    conv = kern[0:1] * raws
    for m in range(1, KCONV):
        conv = conv + kern[m : m + 1] * shift_down(raws, m)
    scale = lax.rsqrt(jnp.sum(conv * conv, -1, keepdims=True) + 1e-06)
    return conv * scale, scale


def forward_body(len_ref, proj_ref, logit_ref, kern_ref, o_ref, x_ref, w_ref, p_ref):
    length = len_ref[0]
    hw = o_ref.shape[-1]
    q = proj_ref[:, 0:hw]
    k = proj_ref[:, hw : 2 * hw]
    v = proj_ref[:, 2 * hw : 3 * hw]
    raws = proj_ref[:, 3 * hw : 4 * hw].astype(F32)
    house, _ = house_of(raws, kern_ref[0])
    beta = 2.0 * jax.nn.sigmoid(logit_ref[0])
    hh, hl = split(house)
    top, low = slice(0, HALF), slice(HALF, 2 * HALF)
    ri = lax.broadcasted_iota(jnp.int32, (HALF, HALF), 0)
    ci = lax.broadcasted_iota(jnp.int32, (HALF, HALF), 1)
    strict = ri > ci
    causal = ri >= ci
    h_left = jnp.concatenate([hh, hl, hh], 1)
    h_right = jnp.concatenate([hh, hh, hl], 1)
    h_two = jnp.concatenate([hh, hl], 1)
    k_two = jnp.concatenate([k, k], 1)
    q_two = jnp.concatenate([q, q], 1)

    def gram(a, b):
        return dotb(h_left[a], h_right[b], NT)

    def keyed(a, b):
        return dotb(h_two[a], k_two[b], NT)

    def asked(a, b):
        return dotb(q_two[a], h_two[b], NT)

    n11 = beta[top] * jnp.where(strict, gram(top, top), 0.0)
    n22 = beta[low] * jnp.where(strict, gram(low, low), 0.0)
    n21 = split(beta[low] * gram(low, top))
    inverses = [n11, n22]
    level = 1
    xor = ri ^ ci
    bits = [split(n11), split(n22)]
    current = None
    while level < HALF:
        mask = (xor >= level) & (xor < 2 * level)
        for d in range(2):
            if level == 1:
                eye = jnp.where(ri == ci, 1.0, 0.0)
                inverses[d] = eye - jnp.where(mask, inverses[d], 0.0)
            else:
                t = split(inverses[d])
                zero = jnp.zeros((), BF16)
                c = tuple(jnp.where(mask, part, zero) for part in bits[d])
                inverses[d] = inverses[d] - dot3(t, split(dot3(c, t)))
        level *= 2
    t1, t2 = split(inverses[0]), split(inverses[1])
    b11 = split(beta[top] * jnp.where(strict, keyed(top, top), 0.0))
    b22 = split(beta[low] * jnp.where(strict, keyed(low, low), 0.0))
    b21f = beta[low] * keyed(low, top)
    b21 = split(b21f)
    m11 = split(jnp.where(causal, asked(top, top), 0.0))
    m22 = split(jnp.where(causal, asked(low, low), 0.0))
    m21 = asked(low, top)
    x11 = split(dot3(t1, b11))
    x22 = split(dot3(t2, b22))
    x21 = split(dot3(t2, split(b21f - dot3(n21, x11))))
    w11 = split(dot3(m11, t1))
    w22 = split(dot3(m22, t2))
    w21 = split(dot3(split(m21 - dot3(w22, n21)), t1))
    scale = hw ** (-0.5)

    def soften(scores, allowed):
        scores = jnp.where(allowed, scores, -1e30)
        weights = jnp.exp(scores - jnp.max(scores, -1, keepdims=True))
        return (weights * (1.0 / jnp.sum(weights, -1, keepdims=True))).astype(BF16)

    s11 = (dotb(q[top], k[top], NT) - dot3(w11, b11)) * scale
    s21 = (dotb(q[low], k[top], NT) - (dot3(w21, b11) + dot3(w22, b21))) * scale
    s22 = (dotb(q[low], k[low], NT) - dot3(w22, b22)) * scale
    p1 = soften(s11, causal & (ci < length))
    p2 = soften(
        jnp.concatenate([s21, s22], 1),
        jnp.concatenate([ci < length, causal & (ci + HALF < length)], 1),
    )
    o_ref[top, :] = dotb(p1, v[top]).astype(o_ref.dtype)
    o_ref[low, :] = dotb(p2, v).astype(o_ref.dtype)
    p_ref[0, 0] = p1
    p_ref[0, 1] = p2[:, :HALF]
    p_ref[0, 2] = p2[:, HALF:]
    for i, (xx, ww) in enumerate(((x11, w11), (x21, w21), (x22, w22))):
        for j in range(2):
            x_ref[0, i, j] = xx[j]
            w_ref[0, i, j] = ww[j].T


def backward_body(proj_ref, logit_ref, kern_ref, g_ref, x_ref, w_ref, p_ref, dproj_ref, dlogit_ref, dkern_ref):
    hw = g_ref.shape[-1]
    q = proj_ref[:, 0:hw]
    k = proj_ref[:, hw : 2 * hw]
    v = proj_ref[:, 2 * hw : 3 * hw]
    raws = proj_ref[:, 3 * hw : 4 * hw].astype(F32)
    kern = kern_ref[0]
    house, rs = house_of(raws, kern)
    beta = 2.0 * jax.nn.sigmoid(logit_ref[0])
    g = g_ref[...]
    hh, hl = split(house)
    top, low = slice(0, HALF), slice(HALF, 2 * HALF)
    ri = lax.broadcasted_iota(jnp.int32, (HALF, HALF), 0)
    ci = lax.broadcasted_iota(jnp.int32, (HALF, HALF), 1)
    strict = ri > ci
    causal = ri >= ci
    scale = hw ** (-0.5)
    p11, p21, p22 = (p_ref[0, i] for i in range(3))
    x11, x21, x22 = ((x_ref[0, i, 0], x_ref[0, i, 1]) for i in range(3))
    w11, w21, w22 = ((w_ref[0, i, 0], w_ref[0, i, 1]) for i in range(3))
    q_t, g_t = q.T, g.T
    ht_h, ht_l = hh.T, hl.T

    def soften_back(probs, dprobs):
        pf = probs.astype(F32)
        mixed = pf * dprobs
        return (mixed - pf * jnp.sum(mixed, -1, keepdims=True)) * scale

    z1 = soften_back(p11, dotb(g[top], v[top], NT))
    z2 = soften_back(jnp.concatenate([p21, p22], 1), dotb(g[low], v, NT))
    z11 = split(z1)
    z21 = split(z2[:, :HALF])
    z22 = split(z2[:, HALF:])
    u11 = jnp.where(causal, dot3(z11, x11, NT), 0.0)
    u21 = dot3(z21, x11, NT)
    u22 = jnp.where(causal, dot3(z21, x21, NT) + dot3(z22, x22, NT), 0.0)
    u11, u21, u22 = split(u11), split(u21), split(u22)
    b11 = jnp.where(strict, dot3(w11, z11) + dot3(w21, z21), 0.0)
    b21 = dot3(w22, z21)
    b22 = jnp.where(strict, dot3(w22, z22), 0.0)
    a11 = jnp.where(strict, dot3(w11, u11) + dot3(w21, u21), 0.0)
    a21 = dot3(w22, u21)
    a22 = jnp.where(strict, dot3(w22, u22), 0.0)
    b11s, b21s, b22s = split(b11), split(b21), split(b22)
    a11s, a21s, a22s = split(a11), split(a21), split(a22)

    def rows(c11, c21, c22, mats):
        (mh, ml) = mats
        first = dotb(c11[0], mh[top]) + dotb(c11[1], mh[top])
        second = dotb(c21[0], mh[top]) + dotb(c21[1], mh[top])
        second = second + dotb(c22[0], mh[low]) + dotb(c22[1], mh[low])
        if ml is not None:
            first = first + dotb(c11[0], ml[top])
            second = second + dotb(c21[0], ml[top]) + dotb(c22[0], ml[low])
        return jnp.concatenate([first, second], 0)

    def cols(c11, c21, c22, mats):
        (mh, ml) = mats
        first = dotb(mh[:, top], c11[0]) + dotb(mh[:, top], c11[1])
        first = first + dotb(mh[:, low], c21[0]) + dotb(mh[:, low], c21[1])
        second = dotb(mh[:, low], c22[0]) + dotb(mh[:, low], c22[1])
        if ml is not None:
            first = first + dotb(ml[:, top], c11[0]) + dotb(ml[:, low], c21[0])
            second = second + dotb(ml[:, low], c22[0])
        return jnp.concatenate([first, second], 1)

    dq = rows(z11, z21, z22, (k, None)) - rows(u11, u21, u22, (hh, hl))
    bk = rows(b11s, b21s, b22s, (k, None))
    nh = rows(a11s, a21s, a22s, (hh, hl))
    mixed = nh - bk
    dbeta = jnp.sum(house * mixed, -1, keepdims=True)
    dlogit_ref[0] = dbeta * beta * (1.0 - 0.5 * beta)
    bb = [split(beta[s] * b) for s, b in ((top, b11), (low, b21), (low, b22))]
    ab = [split(beta[s] * a) for s, a in ((top, a11), (low, a21), (low, a22))]
    dk_t = cols(z11, z21, z22, (q_t, None)) - cols(*bb, (ht_h, ht_l))
    dh_t = cols(*ab, (ht_h, ht_l)) - cols(u11, u21, u22, (q_t, None))
    dv_t = jnp.concatenate(
        [dotb(g_t[:, top], p11) + dotb(g_t[:, low], p21), dotb(g_t[:, low], p22)], 1
    )
    dh = beta * mixed + dh_t.T
    dc = rs * (dh - house * jnp.sum(house * dh, -1, keepdims=True))
    dr = kern[0:1] * dc
    taps = [jnp.sum(dc * raws, 0, keepdims=True)]
    for m in range(1, KCONV):
        up = shift_up(dc, m)
        dr = dr + kern[m : m + 1] * up
        taps.append(jnp.sum(up * raws, 0, keepdims=True))
    dkern_ref[0] = jnp.concatenate(taps, 0)
    dproj_ref[:, 0:hw] = dq.astype(BF16)
    dproj_ref[:, hw : 2 * hw] = dk_t.T.astype(BF16)
    dproj_ref[:, 2 * hw : 3 * hw] = dv_t.T.astype(BF16)
    dproj_ref[:, 3 * hw : 4 * hw] = dr.astype(BF16)


MESH = pl.DeviceIdType.MESH
TN = (((0,), (0,)), ((), ()))


def own_bits(bits):
    group = lax.axis_index("dp")
    return group, [lax.rem(lax.div(group, 1 << b), 2) for b in range(bits)]


class Reduce:
    def __init__(self, order, rows, columns, peer):
        self.order, self.rows, self.columns, self.peer = order, rows, columns, peer
        self.bits = len(order)

    def dims(self, taken):
        return (2,) * (self.bits - taken) + (self.rows, self.columns)

    def scratch(self):
        shapes = [pltpu.VMEM(self.dims(1), BF16)]
        shapes += [pltpu.VMEM(self.dims(1 + k), BF16) for k in range(self.bits)]
        shapes += [pltpu.VMEM(self.dims(self.bits), BF16)]
        if self.peer:
            shapes += [pltpu.VMEM(self.dims(self.bits), BF16)]
        count = 2 * self.bits + 1
        return shapes + [pltpu.SemaphoreType.DMA((count,)), pltpu.SemaphoreType.DMA((count + 1,))]

    def rotating(self):
        return [pltpu.VMEM(self.dims(1 + k), BF16) for k in range(self.bits)]

    def bind(self, group, bit_of, compute, out, refs):
        self.group, self.bit_of, self.compute, self.out = group, bit_of, compute, out
        refs = list(refs)
        self.kept = refs.pop(0)
        self.recv = [refs.pop(0) for _ in range(self.bits)]
        self.shard = refs.pop(0)
        self.from_peer = refs.pop(0) if self.peer else None
        self.send_sem, self.recv_sem = refs
        stages = [functools.partial(self.halve, k) for k in range(self.bits)] + [self.finish]
        if self.peer:
            stages.append(self.take_peer)
        stages += [functools.partial(self.double, k) for k in range(1, self.bits)] + [self.end]
        self.stages = stages
        self.copies = {}
        return self

    def at(self, fixed, gone=()):
        return tuple(
            fixed.get(b, slice(None)) for b in range(self.bits - 1, -1, -1) if b not in gone
        )

    def remote(self, slot, source, target, bit=None):
        if bit is None:
            device = {"wd": 1 - lax.axis_index("wd")}
        else:
            step = 1 << bit
            device = {"dp": self.group + step - 2 * step * self.bit_of[bit]}
        copy = pltpu.make_async_remote_copy(
            src_ref=source,
            dst_ref=target,
            send_sem=self.send_sem.at[slot],
            recv_sem=self.recv_sem.at[slot],
            device_id=device,
            device_id_type=MESH,
        )
        copy.start()
        self.copies[slot] = copy

    def total(self, step, fixed, target):
        free = [b for b in range(self.bits - 1, -1, -1) if b not in fixed]
        part = 32 if self.rows % 32 == 0 else self.rows
        for combo in range(1 << len(free)):
            place = {b: (combo >> i) & 1 for i, b in enumerate(reversed(free))}
            where = {**fixed, **place}
            head = tuple(place[b] for b in free)

            def body(i, _):
                rows = pl.ds(pl.multiple_of(i * part, part), part)
                value = self.kept[self.at(where, self.order[:1]) + (rows,)].astype(F32)
                for j in range(step):
                    gone = self.order[: j + 1]
                    value = value + self.recv[j][self.at(where, gone) + (rows,)].astype(F32)
                target[head + (rows,)] = value.astype(BF16)
                return 0

            lax.fori_loop(0, self.rows // part, body, 0)

    def halve(self, k):
        bit = self.order[k]
        if k == 0:
            self.compute(self, self.at({bit: 1 - self.bit_of[bit]}), self.send[0])
        else:
            self.copies[k - 1].wait()
            fixed = {b: self.bit_of[b] for b in self.order[:k]}
            fixed[bit] = 1 - self.bit_of[bit]
            self.total(k, fixed, self.send[k])
        self.remote(k, self.send[k], self.recv[k], bit)
        if k == 0:
            self.compute(self, self.at({bit: self.bit_of[bit]}), self.kept)

    def finish(self):
        self.copies[self.bits - 1].wait()
        mine = {b: self.bit_of[b] for b in range(self.bits)}
        self.total(self.bits, mine, self.shard)
        if self.peer:
            self.remote(self.bits, self.shard, self.from_peer)
        else:
            self.begin(self.shard)

    def take_peer(self):
        self.copies[self.bits].wait()
        self.begin(self.from_peer)

    def begin(self, block):
        mine = self.at({b: self.bit_of[b] for b in range(self.bits)})
        local = pltpu.make_async_copy(block, self.out(mine), self.recv_sem.at[2 * self.bits + 1])
        local.start()
        self.copies[-1] = local
        self.remote(self.bits + 1, block, self.out(mine), self.order[-1])

    def double(self, k):
        if k == 1:
            self.copies[-1].wait()
        self.copies[self.bits + k].wait()
        bit = self.order[self.bits - 1 - k]
        fixed = {b: self.bit_of[b] for b in self.order[: self.bits - k]}
        slab = self.out(self.at(fixed))
        self.remote(self.bits + 1 + k, slab, slab, bit)

    def end(self):
        if self.bits == 1:
            self.copies[-1].wait()
        self.copies[2 * self.bits].wait()


def turned(source, target):
    rows, lead = target.shape[-2], target.shape[:-2]
    if rows % 16 == 0:
        target[...] = source[...].T.reshape(target.shape)
    else:
        value = source[...].astype(F32).T
        for i, place in enumerate(np.ndindex(*lead)):
            target[place] = value[i * rows : (i + 1) * rows].astype(BF16)


def gradient(left, right):
    def compute(piece, where, target):
        values = right()
        if piece.rows % 16 == 0:
            part = left[where]
            part = part.reshape(-1, part.shape[-1])
            target[...] = dotb(part, values).astype(BF16).reshape(target.shape)
        else:
            for place in np.ndindex(*target.shape[:-2]):
                free = iter(place)
                index = tuple(next(free) if isinstance(w, slice) else w for w in where)
                target[place] = dotb(left[index + tuple(free)], values).astype(BF16)

    return compute


class Chain:
    bits = 3
    last_z = 3

    def __init__(self, rows, columns, peer, split_first):
        self.rows, self.columns, self.peer, self.split_first = rows, columns, peer, split_first

    def scratch(self):
        block = (self.rows, self.columns)
        if self.split_first:
            shapes = [pltpu.VMEM((2,) + block, BF16)] * 2 + [pltpu.VMEM(block, BF16)] * 2
        else:
            shapes = [pltpu.VMEM((2, 2) + block, BF16)] + [pltpu.VMEM((2,) + block, BF16)] * 2
        return shapes + [pltpu.SemaphoreType.DMA((8,)), pltpu.SemaphoreType.DMA((9,))]

    def rotating(self):
        return [pltpu.VMEM((2, self.rows, self.columns), BF16)] if self.split_first else []

    def bind(self, group, bit_of, compute, out, refs):
        self.compute, self.out = compute, out
        self.group, self.y, self.z = group, bit_of[0], lax.div(group, 2)
        refs = list(refs)
        self.kept = refs.pop(0)
        if self.split_first:
            self.halved = refs.pop(0)
        self.come = refs[:2]
        self.send_sem, self.recv_sem = refs[2:]
        ends = [self.finish] + ([self.take_peer] if self.peer else [])
        if self.split_first:
            self.stages = [self.first_split, self.climb_first]
            self.stages += [self.climb_second, self.climb_third] + ends
            self.stages += [functools.partial(self.fall, k) for k in range(3)] + [self.end]
        else:
            self.stages = [self.first_whole, self.climb_second, self.climb_third, self.halve_end]
            self.stages += ends + [self.fall_start]
            self.stages += [functools.partial(self.fall, k) for k in range(3)] + [self.end]
        return self

    def hop(self, slot, source, target, step=None, axis=None):
        if axis is not None:
            device = {axis: 1 - lax.axis_index(axis)}
        elif step is None:
            device = {"dp": self.group + 1 - 2 * self.y}
        else:
            device = {"dp": self.group + 2 * step}
        return pltpu.make_async_remote_copy(
            src_ref=source,
            dst_ref=target,
            send_sem=self.send_sem.at[slot],
            recv_sem=self.recv_sem.at[slot],
            device_id=device,
            device_id_type=MESH,
        )

    def climb(self, part):
        return self.hop(part, self.kept.at[part], self.come[part], 1 if part else -1)

    def part_of_out(self, part):
        if self.split_first:
            return self.out((self.y, part))
        return self.out((part, slice(None)))

    def descend(self, part):
        ref = self.part_of_out(part)
        return self.hop(2 + part, ref, ref, -1 if part else 1)

    def across(self, part):
        ref = self.out((self.y, part)) if self.split_first else self.out((part, self.y))
        return self.hop(4 + part, ref, ref)

    def swap(self, part):
        spare = self.come[1 - part] if self.split_first else self.come[1 - part].at[1]
        block = self.kept.at[part] if self.split_first else self.kept.at[part, self.y]
        return self.hop(6, block, spare, axis="wd")

    def end_swap(self, part):
        block = self.kept.at[part, 1 - self.y]
        return self.hop(7, block, self.come[1 - part].at[0])

    def add(self, target, *others):
        part = 32 if self.rows % 32 == 0 else self.rows

        def body(i, _):
            rows = pl.ds(pl.multiple_of(i * part, part), part)
            value = target[rows].astype(F32)
            for other in others:
                value = value + other[rows].astype(F32)
            target[rows] = value.astype(BF16)
            return 0

        lax.fori_loop(0, self.rows // part, body, 0)

    def gather(self, part, first):
        if self.split_first:
            others = [self.halved.at[part]] + ([] if first else [self.come[part]])
            self.add(self.kept.at[part], *others)
        elif not first:
            for y in range(2):
                self.add(self.kept.at[part, y], self.come[part].at[y])

    def at_level(self, level, action):
        pl.when(self.z == level)(lambda: action(1))
        pl.when(self.z == self.last_z - level)(lambda: action(0))

    def first_split(self):
        self.compute(self, (1 - self.y,), self.send[0])
        self.hop(7, self.send[0], self.halved).start()
        self.compute(self, (self.y,), self.kept)

    def climb_first(self):
        self.hop(7, self.send[0], self.halved).wait()

        def action(part):
            self.gather(part, True)
            self.climb(part).start()

        self.at_level(0, action)

    def first_whole(self):
        self.compute(self, (), self.kept)
        self.at_level(0, lambda part: self.climb(part).start())

    def onwards(self, level):
        def action(part):
            self.climb(part).wait_recv()
            self.gather(part, False)
            self.climb(part).start()

        self.at_level(level, action)

    def climb_second(self):
        self.onwards(1)

    def climb_third(self):
        self.onwards(2)

    def halve_end(self):
        def action(part):
            self.climb(part).wait_recv()
            self.add(self.kept.at[part, 1 - self.y], self.come[part].at[1 - self.y])
            self.end_swap(part).start()

        self.at_level(3, action)

    def finish(self):
        def action(part):
            if self.split_first:
                self.climb(part).wait_recv()
                self.gather(part, False)
            else:
                self.end_swap(part).wait()
                self.add(
                    self.kept.at[part, self.y],
                    self.come[part].at[self.y],
                    self.come[1 - part].at[0],
                )
            if self.peer:
                self.swap(part).start()
            else:
                self.begin(part, False)

        self.at_level(3, action)

    def take_peer(self):
        def action(part):
            self.swap(part).wait()
            self.begin(part, True)

        self.at_level(3, action)

    def local(self, part, taken):
        if self.split_first:
            block = self.come[1 - part] if taken else self.kept.at[part]
            ref = self.out((self.y, part))
        else:
            block = self.come[1 - part].at[1] if taken else self.kept.at[part, self.y]
            ref = self.out((part, self.y))
        return block, ref, pltpu.make_async_copy(block, ref, self.recv_sem.at[8])

    def begin(self, part, taken):
        block, ref, copy = self.local(part, taken)
        copy.start()
        self.hop(4 + part, block, ref).start()
        if self.split_first:
            self.hop(2 + part, block, ref, -1 if part else 1).start()

    def fall_start(self):
        def action(part):
            self.local(part, self.peer)[2].wait()
            self.across(part).wait()
            self.descend(part).start()

        self.at_level(3, action)

    def fall(self, k):
        def action(part):
            self.descend(part).wait_recv()
            if k < 2:
                self.descend(part).start()
            if self.split_first:
                self.across(part).start()

        self.at_level(2 - k, action)

    def end(self):
        def sent(part):
            self.climb(part).wait_send()

        def fallen(part):
            self.descend(part).wait_send()

        def here(part):
            self.local(part, self.peer)[2].wait()

        for level in range(3):
            self.at_level(level, sent)
        for level in range(1, 4):
            self.at_level(level, fallen)
        if self.split_first:
            self.at_level(3, here)
            for part in range(2):
                self.across(part).wait()


SMALL = 64
WHOLE_FIRST = (1, 3, 5, 7, 9, 11, 13, 15)


def chained(bits):
    return bits == 3


def depths(bits):
    return (4, 4) if chained(bits) else (2, 3)


class Given(NamedTuple):
    part: Any
    feed: Any
    cot: Any
    hidden: Any
    gate_grad: Any
    up_grad: Any
    two: Any
    mid: Any
    rinv_one: Any
    rinv_two: Any
    gains: Any
    near: Any
    out: Any
    proj: Any
    logit: Any
    kern: Any
    kept: Any
    act: Any
    x: Any
    attn_all: Any
    attn_peer: Any
    beta: Any


class Spots(NamedTuple):
    cot: Any
    hidden: Any
    gate_grad: Any
    up_grad: Any
    two: Any
    near: Any
    out_own: Any
    proj: Any
    core_in: Any
    core_own: Any
    sum: Any
    side_in: Any
    mid: Any
    mid_grad: Any
    branch: Any
    heads_grad: Any
    feed_out: Any
    feed_in: Any
    aw: Any
    dproj: Any
    logit: Any
    dlogit: Any
    dkern: Any
    kept: Any
    left_hidden: Any
    left: Any
    small: Any
    small_in: Any
    beta_out: Any
    beta_in: Any
    local_sem: Any
    send_sem: Any
    recv_sem: Any


class Loads:
    def __init__(self, sems):
        self.sems, self.used = sems, 0

    def start(self, source, target):
        copy = pltpu.make_async_copy(source, target, self.sems.at[self.used])
        self.used += 1
        copy.start()
        return [copy]


class Links:
    def __init__(self, send_sems, recv_sems):
        self.send_sems, self.recv_sems, self.used = send_sems, recv_sems, 0

    def start(self, device, source, target):
        copy = pltpu.make_async_remote_copy(
            src_ref=source,
            dst_ref=target,
            send_sem=self.send_sems.at[self.used],
            recv_sem=self.recv_sems.at[self.used],
            device_id=device,
            device_id_type=MESH,
        )
        self.used += 1
        copy.start()
        return copy


def settle(copies):
    for copy in copies:
        copy.wait()
    copies.clear()


def flipped(axis):
    return {axis: 1 - lax.axis_index(axis)}


def group_peer(group, bit_of, bit):
    step = 1 << bit
    return {"dp": group + step - 2 * step * bit_of[bit]}


def back_body(bits, plans, r, outs, out_ref, gin_ref, small_ref, v, rest):
    group, bit_of = own_bits(bits)
    lag, deep = depths(bits)
    count = len(plans)
    core, side = lax.axis_index("tp"), lax.axis_index("wd")
    span, width = r.cot[0].shape
    half = span // 2
    wide = v.aw.shape[-1]
    hw = wide // 4
    heads = r.kern.shape[0]
    model = 2 * width
    hidden_own = r.hidden.shape[1]
    mine = pl.ds(pl.multiple_of(core * half, half), half)
    far = pl.ds(pl.multiple_of((1 - core) * half, half), half)
    loads = Loads(v.local_sem)
    links = Links(v.send_sem, v.recv_sem)
    x_peer, c_peer = flipped("wd"), flipped("tp")

    barrier = pltpu.get_barrier_semaphore()
    for device in [group_peer(group, bit_of, b) for b in range(bits)] + [x_peer, c_peer]:
        pl.semaphore_signal(barrier, inc=1, device_id=device, device_id_type=MESH)
    if chained(bits):
        z = lax.div(group, 2)

        def greet_middle(step):
            device = {"dp": group + step}
            pl.semaphore_signal(barrier, inc=1, device_id=device, device_id_type=MESH)

        pl.when(z == 1)(lambda: greet_middle(2))
        pl.when(z == 2)(lambda: greet_middle(-2))
        inside = (z == 1) | (z == 2)
        pl.when(inside)(lambda: pl.semaphore_wait(barrier, bits + 3))
        pl.when(jnp.logical_not(inside))(lambda: pl.semaphore_wait(barrier, bits + 2))
    else:
        pl.semaphore_wait(barrier, bits + 2)

    first = [links.start(c_peer, r.part[i].at[far], v.core_in.at[i]) for i in range(2)]
    got_hidden = loads.start(r.hidden, v.hidden)
    got_cot = [loads.start(r.cot[i], v.cot[i]) for i in range(2)]
    got_part = [loads.start(r.part[i].at[mine], v.core_own.at[i])[0] for i in range(2)]
    got_ffn = [loads.start(r.two[i], v.two[i])[0] for i in range(2)]
    got_ffn += loads.start(r.gate_grad, v.gate_grad)
    got_ffn += loads.start(r.up_grad, v.up_grad)
    got_mid = [loads.start(r.mid[i].at[mine], v.mid.at[i])[0] for i in range(2)]
    own_rows = pl.ds(pl.multiple_of(side * heads * hw, heads * hw), heads * hw)
    got_out = [loads.start(r.out[i].at[own_rows], v.out_own.at[i])[0] for i in range(2)]
    got_near = loads.start(r.near, v.near)
    got_proj = loads.start(r.proj, v.proj)

    def load_kept(h):
        copies = [loads.start(a.at[pl.ds(h, 1)], b)[0] for a, b in zip(r.kept, v.kept)]
        return copies + loads.start(r.logit.at[pl.ds(h, 1)], v.logit)

    got_kept = load_kept(0)

    pieces = []
    shared, used = {}, {}
    cut_width, cut_hidden = width // 2, hidden_own // 2

    def piece(left, right, view):
        plan = plans[len(pieces)]
        size = len(plan.scratch())
        own = [rest.pop(0) for _ in range(size)]
        pieces.append(plan.bind(group, bit_of, gradient(left, right), view, own))

    def columns(out, start, size):
        cols = pl.ds(pl.multiple_of(start, 128), size)
        return lambda where: out.at[where + (slice(None), cols)]

    def owner(j):
        return side if j == 0 else 1 - side

    for j in range(2):
        for i in range(2):
            cut = slice(i * cut_width, (i + 1) * cut_width)
            piece(
                v.left_hidden,
                lambda j=j, cut=cut: v.cot[j][:, cut],
                lambda where, j=j, cut=cut: outs[0].at[(owner(j),) + where + (slice(None), cut)],
            )
    for n, values in ((1, v.gate_grad), (2, v.up_grad)):
        for j in range(2):
            for i in range(2):
                cut = slice(i * cut_hidden, (i + 1) * cut_hidden)
                piece(
                    v.left.at[j],
                    lambda values=values, cut=cut: values[:, cut],
                    columns(outs[n], owner(j) * hidden_own + i * cut_hidden, cut_hidden),
                )
    for i in range(2):
        cut = slice(i * cut_width, (i + 1) * cut_width)
        piece(
            v.left.at[0],
            lambda cut=cut: v.branch[0, :, cut],
            lambda where, cut=cut: outs[3].at[where + (slice(None), cut)],
        )
    for h in range(heads):
        for j in range(2):
            piece(
                v.left.at[j],
                lambda h=h: v.dproj[h],
                lambda where, h=h, j=j: outs[4].at[(owner(j) * heads + h,) + where],
            )
    for i, plan in enumerate(plans):
        shapes = plan.rotating()
        if shapes:
            key = (plan.rows, plan.columns)
            place = shared.setdefault(key, [])
            at = used.get(key, 0)
            used[key] = at + 1
            if at < deep:
                place.append([rest.pop(0) for _ in shapes])
            pieces[i].send = place[at % deep]

    position = [0]

    def pump(until):
        last = max(i + lag * len(p.stages) for i, p in enumerate(pieces))
        for slot in range(position[0], min(until, last)):
            for i in reversed(range(count)):
                step, off = divmod(slot - i, lag)
                if off == 0 and 0 <= step < len(pieces[i].stages):
                    pieces[i].stages[step]()
        position[0] = max(position[0], until)

    settle(got_hidden)
    turned(v.hidden, v.left_hidden)
    settle(got_cot[0])
    pump(2)
    settle(got_cot[1])
    pump(4)
    settle(got_part)
    settle(first)
    for i in range(2):
        v.sum[i] = (v.core_own[i].astype(F32) + v.core_in[i].astype(F32)).astype(BF16)
    first = [links.start(x_peer, v.sum.at[i], v.side_in.at[1 - i]) for i in range(2)]
    settle(got_ffn)
    for i in range(2):
        turned(v.two[i], v.left.at[i])
    pump(8)
    settle(first)
    settle(got_mid)

    def norm_back(base_of, rinv, gains):
        grads = [v.sum[i].astype(F32) + v.side_in[i].astype(F32) for i in range(2)]
        cross = sum(
            jnp.sum(grads[i] * gains[i] * base_of(i), -1, keepdims=True) for i in range(2)
        )
        cube = rinv * rinv * rinv * cross / model
        backs = [grads[i] * gains[i] * rinv - base_of(i) * cube for i in range(2)]
        return backs, jnp.sum(grads[0] * base_of(0) * rinv, 0, keepdims=True)

    gains = [g[1:2, :] for g in r.gains]
    backs, gain_two = norm_back(lambda i: v.mid[i], r.rinv_two[mine, :], gains)
    for i in range(2):
        value = v.cot[i][mine, :].astype(F32) + backs[i]
        if i == 0:
            v.mid_grad[...] = value
        v.branch[i, mine, :] = value.astype(BF16)
    first = [links.start(c_peer, v.branch.at[i, mine], v.branch.at[i, mine]) for i in range(2)]
    pump(9)
    settle(first)
    settle(got_out)
    grad = dotb(v.branch[0], v.out_own[0], NT) + dotb(v.branch[1], v.out_own[1], NT)
    for h in range(heads):
        v.heads_grad[h] = grad[:, h * hw : (h + 1) * hw].astype(BF16)
    first = [links.start(c_peer, r.feed[i].at[far], v.core_in.at[i]) for i in range(2)]
    got_part = [loads.start(r.feed[i].at[mine], v.core_own.at[i])[0] for i in range(2)]
    pump(10)
    settle(first)
    settle(got_part)
    feed = [v.core_own[i].astype(F32) + v.core_in[i].astype(F32) for i in range(2)]
    v.feed_out[...] = feed[1].astype(BF16)
    v.mid[0] = v.mid[0] + feed[0]
    first = [links.start(x_peer, v.feed_out, v.feed_in)]
    settle(got_proj)
    lanes = lax.broadcasted_iota(jnp.int32, (span, 128), 1)
    grad_beta = jnp.zeros((span, 128), F32)
    got_x = []

    def give_outputs():
        settle(first)
        v.feed_out[...] = (v.mid[0] + v.feed_in[...].astype(F32)).astype(BF16)
        first.append(links.start(c_peer, v.feed_out, out_ref.at[mine]))
        first.extend(loads.start(v.feed_out, out_ref.at[mine]))

    def take_inputs():
        settle(first)
        got_x.extend(loads.start(r.x[i].at[mine], v.core_own.at[i])[0] for i in range(2))

    for h in range(heads):
        settle(got_kept)
        got_aw = loads.start(r.attn_all.at[side * heads + h], v.aw.at[0])
        got_aw += loads.start(r.attn_peer.at[h], v.aw.at[1])
        backward_body(
            v.proj.at[h],
            v.logit,
            r.kern.at[pl.ds(h, 1)],
            v.heads_grad.at[h],
            v.kept[0],
            v.kept[1],
            v.kept[2],
            v.dproj.at[h],
            v.dlogit,
            v.dkern.at[pl.ds(h, 1)],
        )
        grad_beta = grad_beta + jnp.where(lanes == side * heads + h, v.dlogit[0], 0.0)
        if h + 1 < heads:
            got_kept = load_kept(h + 1)
        settle(got_aw)
        for i in range(2):
            value = dotb(v.dproj[h], v.aw[i], NT)
            if h > 0:
                value = value + v.cot[i][...].astype(F32)
            if h == heads - 1:
                low = grad_beta.astype(BF16)
                value = value + dotb(low[:, : 2 * heads], r.beta[i][...])
            v.cot[i][...] = value.astype(BF16)
        pump(10 + h)
        if h == 0:
            give_outputs()
        if h == min(1, heads - 1):
            take_inputs()
    beta_low = grad_beta.astype(BF16)
    first = [links.start(c_peer, v.cot[i].at[far], v.core_in.at[i]) for i in range(2)]
    pump(12)
    settle(got_near)
    turned(v.near, v.left.at[0])
    settle(first)
    for i in range(2):
        total = v.cot[i][mine, :].astype(F32) + v.core_in[i].astype(F32)
        v.sum[i] = total.astype(BF16)
    first = [links.start(x_peer, v.sum.at[i], v.side_in.at[1 - i]) for i in range(2)]
    pump(14)
    got_act = [loads.start(r.act[i], v.two[i])[0] for i in range(2)]
    settle(got_act)
    for i in range(2):
        turned(v.two[i], v.left.at[i])
    pump(15)
    settle(first)
    settle(got_x)
    gains = [g[0:1, :] for g in r.gains]
    backs, gain_one = norm_back(lambda i: v.core_own[i].astype(F32), r.rinv_one[mine, :], gains)
    v.feed_out[...] = (v.mid_grad[...] + backs[0]).astype(BF16)
    first = [links.start(c_peer, v.feed_out, gin_ref.at[mine])]
    first += loads.start(v.feed_out, gin_ref.at[mine])
    rows = width // 128
    small = v.small
    for i in range(rows):
        cut = slice(i * 128, (i + 1) * 128)
        small[0, i : i + 1, :] = gain_one[:, cut]
        small[0, 8 + i : 9 + i, :] = gain_two[:, cut]
    small[0, rows:8, :] = jnp.zeros((8 - rows, 128), F32)
    small[0, 8 + rows : 16, :] = jnp.zeros((8 - rows, 128), F32)
    gain_rows = pl.ds(0, 16)
    first.append(links.start(c_peer, small.at[0, gain_rows], v.small_in.at[bits, gain_rows]))
    for i in range(2):
        value = lax.dot_general(beta_low, v.two[i][...], TN, preferred_element_type=F32)
        v.beta_out[i] = jnp.where(side == 0, value[0:8], value[heads : heads + 8])
    first.append(links.start(x_peer, v.beta_out.at[1], v.beta_in))
    pump(16)
    settle(first)
    small[0, 0:16, :] = small[0, 0:16, :] + v.small_in[bits, 0:16, :]
    for h in range(heads):
        for i in range(rows):
            cut = slice(i * 128, (i + 1) * 128)
            at = 16 + h * rows + i
            small[0, at : at + 1, :] = v.beta_out[0, h : h + 1, cut]
            at = at + heads * rows
            small[0, at : at + 1, :] = v.beta_in[h : h + 1, cut]
    at = 16 + 2 * heads * rows
    taps = KCONV * heads
    small[0, at : at + taps, :] = v.dkern[...].reshape(taps, hw)
    if at + taps < small.shape[1]:
        small[0, at + taps :, :] = jnp.zeros((small.shape[1] - at - taps, 128), F32)
    for bit in range(bits):
        copy = links.start(group_peer(group, bit_of, bit), small.at[bit], v.small_in.at[bit])
        pump(17 + bit)
        copy.wait()
        small[bit + 1] = small[bit] + v.small_in[bit]
    small_ref[...] = small[bits]
    pump(1000)


def backward_all(bits, given):
    span, width = given.cot[0].shape
    hidden_own = given.hidden.shape[1]
    heads, hw = given.kern.shape[0], given.kern.shape[-1]
    wide = 4 * hw
    half = span // 2
    order_a = list(range(bits))
    order_b = [1, 0] + list(range(2, bits)) if bits > 1 else order_a
    shapes = [(hidden_own, width // 2)] * 4
    shapes += [(width, hidden_own // 2)] * 8
    shapes += [(width, width // 2)] * 2
    shapes += [(width, wide)] * (2 * heads)
    peers = [False, False, True, True] * 3 + [False, False] + [False, True] * heads
    plans = []
    for i, ((rows, columns), peer) in enumerate(zip(shapes, peers)):
        if chained(bits):
            plans.append(Chain(rows // 4, columns, peer, i not in WHOLE_FIRST))
        else:
            order = order_b if i % 4 == 2 else order_a
            plans.append(Reduce(order, rows >> bits, columns, peer))
    rows = (span, width)
    part = (2, half, width)
    lefts = (2, 2) if chained(bits) else (2,) * bits
    cuts = 2 ** len(lefts)

    def like(a):
        return pltpu.VMEM(a.shape, a.dtype)

    spots = Spots(
        cot=[like(a) for a in given.cot],
        hidden=like(given.hidden),
        gate_grad=like(given.gate_grad),
        up_grad=like(given.up_grad),
        two=[like(a) for a in given.two],
        near=like(given.near),
        out_own=pltpu.VMEM((2, heads * hw, width), BF16),
        proj=like(given.proj),
        core_in=pltpu.VMEM(part, BF16),
        core_own=pltpu.VMEM(part, BF16),
        sum=pltpu.VMEM(part, BF16),
        side_in=pltpu.VMEM(part, BF16),
        mid=pltpu.VMEM(part, F32),
        mid_grad=pltpu.VMEM(part[1:], F32),
        branch=pltpu.VMEM((2,) + rows, BF16),
        heads_grad=pltpu.VMEM((heads, span, hw), BF16),
        feed_out=pltpu.VMEM(part[1:], BF16),
        feed_in=pltpu.VMEM(part[1:], BF16),
        aw=pltpu.VMEM((2, width, wide), BF16),
        dproj=pltpu.VMEM((heads, span, wide), BF16),
        logit=pltpu.VMEM((1, span, 1), F32),
        dlogit=pltpu.VMEM((1, span, 1), F32),
        dkern=pltpu.VMEM((heads, KCONV, hw), F32),
        kept=[pltpu.VMEM((1,) + a.shape[1:], a.dtype) for a in given.kept],
        left_hidden=pltpu.VMEM(lefts + (hidden_own // cuts, span), BF16),
        left=pltpu.VMEM((2,) + lefts + (width // cuts, span), BF16),
        small=pltpu.VMEM((bits + 1, SMALL, 128), F32),
        small_in=pltpu.VMEM((bits + 1, SMALL, 128), F32),
        beta_out=pltpu.VMEM((2, 8, width), F32),
        beta_in=pltpu.VMEM((8, width), F32),
        local_sem=pltpu.SemaphoreType.DMA((64,)),
        send_sem=pltpu.SemaphoreType.DMA((64,)),
        recv_sem=pltpu.SemaphoreType.DMA((64,)),
    )
    more = [s for plan in plans for s in plan.scratch()]
    seen = {}
    deep = depths(bits)[1]
    for plan in plans:
        key = (plan.rows, plan.columns)
        if plan.rotating():
            seen[key] = seen.get(key, 0) + 1
            if seen[key] <= deep:
                more += plan.rotating()
    out_shapes = [
        (2,) + lefts + (hidden_own // cuts, width),
        lefts + (width // cuts, 2 * hidden_own),
        lefts + (width // cuts, 2 * hidden_own),
        lefts + (width // cuts, width),
        (2 * heads,) + lefts + (width // cuts, wide),
    ]
    any_spec = pl.BlockSpec(memory_space=pl.ANY)
    vmem_spec = pl.BlockSpec(memory_space=pltpu.VMEM)
    specs = jax.tree.map(lambda _: any_spec, given)
    specs = specs._replace(
        rinv_one=vmem_spec,
        rinv_two=vmem_spec,
        gains=[vmem_spec] * 2,
        kern=vmem_spec,
        beta=[vmem_spec] * 2,
    )
    return pl.pallas_call(
        functools.partial(back_body, bits, plans),
        in_specs=[specs],
        out_specs=[[any_spec] * 5, any_spec, any_spec, vmem_spec],
        out_shape=[
            [jax.ShapeDtypeStruct(shape, BF16) for shape in out_shapes],
            jax.ShapeDtypeStruct(rows, BF16),
            jax.ShapeDtypeStruct(rows, BF16),
            jax.ShapeDtypeStruct((SMALL, 128), F32),
        ],
        scratch_shapes=[spots, more],
        compiler_params=pltpu.CompilerParams(
            collective_id=0, has_side_effects=True, vmem_limit_bytes=62 * 2**20
        ),
        name="backward_all",
    )(given)


class Front(NamedTuple):
    inputs: Any
    cot: Any
    attn_all: Any
    out: Any
    gate: Any
    up: Any
    down: Any
    beta: Any
    gains: Any
    kern: Any
    lengths: Any


class Made(NamedTuple):
    part: Any
    feed: Any
    cot: Any
    hidden: Any
    gate_grad: Any
    up_grad: Any
    two: Any
    mid: Any
    rinv_one: Any
    rinv_two: Any
    gains: Any
    near: Any
    proj: Any
    logit: Any
    kept: Any
    act: Any
    x: Any
    out: Any
    attn: Any
    beta: Any


class Rooms(NamedTuple):
    x: Any
    cot: Any
    attn: Any
    out: Any
    out_far: Any
    gate: Any
    up: Any
    down: Any
    act: Any
    two: Any
    mid: Any
    proj: Any
    logit: Any
    attended: Any
    near: Any
    far: Any
    hidden: Any
    gate_grad: Any
    up_grad: Any
    slope: Any
    silu: Any
    part: Any
    feed: Any
    kept: Any
    local_sem: Any
    send_sem: Any
    recv_sem: Any


class Fetch:
    def __init__(self, links, group, bit_of, source, target, rows):
        self.links, self.source, self.target = links, source, target
        self.eighth = rows // 8
        self.bit_of = bit_of
        self.first, self.second = (group_peer(group, bit_of, b) for b in range(2))

    def chunk(self, one, two, which, count=1):
        start = ((one * 2 + two) * 2 + which) * self.eighth
        return pl.ds(pl.multiple_of(start, self.eighth), count * self.eighth)

    def start(self):
        rows = self.chunk(self.bit_of[0], self.bit_of[1], 0, 2)
        self.straight = self.links.start(flipped("wd"), self.source(rows), self.target(rows))
        return self

    def pass_on(self):
        self.straight.wait()
        self.sent = []
        for which in range(2):
            ref = self.target(self.chunk(self.bit_of[0], self.bit_of[1], which))
            for device in (self.first, self.second):
                self.sent.append(self.links.start(device, ref, ref))
        return self

    def pass_far(self):
        self.sent[0].wait()
        ref = self.target(self.chunk(1 - self.bit_of[0], self.bit_of[1], 0))
        self.sent.append(self.links.start(self.second, ref, ref))
        self.sent[3].wait()
        ref = self.target(self.chunk(self.bit_of[0], 1 - self.bit_of[1], 1))
        self.sent.append(self.links.start(self.first, ref, ref))
        return self

    def end(self):
        for i in (1, 2, 4, 5):
            self.sent[i].wait()


def front_body(bits, r, out, v):
    group, bit_of = own_bits(bits)
    core, side = lax.axis_index("tp"), lax.axis_index("wd")
    span, width = r.inputs.shape
    half = span // 2
    heads, hw = r.kern.shape[0], r.kern.shape[-1]
    own_width = heads * hw
    hidden_own = v.hidden.shape[1]
    model = 2 * width
    mine = pl.ds(pl.multiple_of(core * half, half), half)
    loads = Loads(v.local_sem)
    links = Links(v.send_sem, v.recv_sem)
    x_peer, c_peer = flipped("wd"), flipped("tp")
    own_cols = pl.ds(pl.multiple_of(side * hidden_own, hidden_own), hidden_own)
    other_cols = pl.ds(pl.multiple_of((1 - side) * hidden_own, hidden_own), hidden_own)

    barrier = pltpu.get_barrier_semaphore()
    for device in [group_peer(group, bit_of, b) for b in range(2)] + [x_peer, c_peer]:
        pl.semaphore_signal(barrier, inc=1, device_id=device, device_id_type=MESH)
    pl.semaphore_wait(barrier, 4)

    def fetch(source, target, rows):
        return Fetch(links, group, bit_of, source, target, rows)

    def down_rows(rows):
        start = (1 - side) * hidden_own + rows.start
        return r.down.at[pl.ds(pl.multiple_of(start, rows.size), rows.size)]

    attn = [
        fetch(
            lambda rows, h=h: r.attn_all.at[(1 - side) * heads + h, rows],
            lambda rows, h=h: v.attn[1].at[h, rows],
            width,
        )
        for h in range(heads)
    ]
    out_w = fetch(lambda rows: r.out.at[rows], lambda rows: v.out[1].at[rows], width)
    gate_w = fetch(lambda rows: r.gate.at[rows, other_cols], lambda rows: v.gate[1].at[rows], width)
    up_w = fetch(lambda rows: r.up.at[rows, other_cols], lambda rows: v.up[1].at[rows], width)
    down_w = fetch(down_rows, lambda rows: v.down[1].at[rows], hidden_own)

    attn[0].start()
    x_half = links.start(x_peer, r.inputs.at[mine], v.x[1].at[mine])
    tiny = [links.start(x_peer, r.beta, out.beta), links.start(x_peer, r.gains, out.gains)]
    attn[1].start()
    got_x = loads.start(r.inputs, v.x[0])
    got_attn = [loads.start(r.attn_all.at[side * heads + h], v.attn[0].at[h]) for h in range(heads)]
    got_rest = loads.start(r.out, v.out[0])
    got_rest += loads.start(r.gate.at[:, own_cols], v.gate[0])
    got_rest += loads.start(r.up.at[:, own_cols], v.up[0])
    got_rest += loads.start(r.down.at[own_cols], v.down[0])
    got_rest += loads.start(r.cot, v.cot[0])
    out_far = [links.start(c_peer, r.out, v.out_far[0])]
    given = []

    attn[0].pass_on()
    attn[2].start()
    x_half.wait()
    x_rest = links.start(c_peer, v.x[1].at[mine], v.x[1].at[mine])
    settle(tiny)
    settle(got_x)
    x_rest.wait()
    out_w.start()
    attn[0].pass_far()
    given += loads.start(v.x[1], out.x)
    xs = [v.x[i][...].astype(F32) for i in range(2)]
    square = sum(jnp.sum(x * x, -1, keepdims=True) for x in xs)
    rinv = lax.rsqrt(square / model + norm_eps)
    out.rinv_one[...] = rinv
    for i, gains in enumerate((r.gains, out.gains)):
        v.act[i][...] = (xs[i] * rinv * gains[0:1, :]).astype(BF16)
        given += loads.start(v.act[i], out.act[i])
    logits = dotb(v.act[0][...], r.beta[...], NT) + dotb(v.act[1][...], out.beta[...], NT)
    for h in range(heads):
        v.logit[h] = jnp.where(side == 0, logits[:, h : h + 1], logits[:, heads + h : heads + h + 1])
    given += loads.start(v.logit, out.logit)
    attn[1].pass_on()
    gate_w.start()
    cot_half = []
    near_in, far_in = [], []
    saved = [[], []]
    before = [
        [attn[1].pass_far, attn[2].pass_on, up_w.start],
        [out_w.pass_far, gate_w.pass_on, down_w.start],
        [gate_w.pass_far, up_w.pass_on],
    ]
    afterwards = [
        [attn[2].pass_far, out_w.pass_on],
        [lambda: cot_half.append(links.start(x_peer, r.cot.at[mine], v.cot[1].at[mine]))],
        [up_w.pass_far, down_w.pass_on],
    ]
    for h in range(heads):
        attn[h].end()
        given += loads.start(v.attn[1].at[h], out.attn.at[h])
        settle(got_attn[h])
        value = dotb(v.act[0][...], v.attn[0][h]) + dotb(v.act[1][...], v.attn[1][h])
        v.proj[h] = value.astype(BF16)
        for step in before[h]:
            step()
        kept = v.kept[h % 2]
        settle(saved[h % 2])
        forward_body(
            r.lengths,
            v.proj.at[h],
            v.logit.at[pl.ds(h, 1)],
            r.kern.at[pl.ds(h, 1)],
            v.attended.at[h],
            kept[0],
            kept[1],
            kept[2],
        )
        saved[h % 2] += [
            loads.start(a, b.at[pl.ds(h, 1)])[0] for a, b in zip(kept, out.kept)
        ]
        place = pl.ds(pl.multiple_of((side * heads + h) * hw, hw), hw)
        v.near[:, place] = v.attended[h]
        near_in.append(links.start(x_peer, v.near.at[:, place], v.near.at[:, place]))
        far_in.append(links.start(c_peer, v.near.at[:, place], v.far.at[:, place]))
        for step in afterwards[h]:
            step()
    given += loads.start(v.proj, out.proj)
    out_w.end()
    out_far.append(links.start(c_peer, v.out[1], v.out_far[1]))
    given += loads.start(v.out[1], out.out)
    for h in range(heads):
        near_in[h].wait()
        place = pl.ds(pl.multiple_of(((1 - side) * heads + h) * hw, hw), hw)
        far_in.append(links.start(c_peer, v.near.at[:, place], v.far.at[:, place]))
    given += loads.start(v.near, out.near)
    cot_half[0].wait()
    cot_rest = links.start(c_peer, v.cot[1].at[mine], v.cot[1].at[mine])
    settle(far_in)
    settle(out_far)
    settle(got_rest)

    def branch_rows(j, _):
        rows = pl.ds(pl.multiple_of(j * 256, 256), 256)
        near, far = v.near[rows, :], v.far[rows, :]
        mids = [
            v.x[i][rows, :].astype(F32) + dotb(near, v.out[i][...]) + dotb(far, v.out_far[i][...])
            for i in range(2)
        ]
        square = sum(jnp.sum(m * m, -1, keepdims=True) for m in mids)
        rinv = lax.rsqrt(square / model + norm_eps)
        out.rinv_two[rows, :] = rinv
        for i, gains in enumerate((r.gains, out.gains)):
            v.mid[i][rows, :] = mids[i]
            v.two[i][rows, :] = (mids[i] * rinv * gains[1:2, :]).astype(BF16)
        return 0

    lax.fori_loop(0, span // 256, branch_rows, 0)
    for i in range(2):
        given += loads.start(v.mid[i], out.mid[i])
        given += loads.start(v.two[i], out.two[i])
    down_w.pass_far()
    gate_w.end()
    up_w.end()

    def hidden_columns(j, _):
        cols = pl.ds(pl.multiple_of(j * 256, 256), 256)
        two = [t[...] for t in v.two]
        gate = dotb(two[0], v.gate[0][:, cols]) + dotb(two[1], v.gate[1][:, cols])
        up = dotb(two[0], v.up[0][:, cols]) + dotb(two[1], v.up[1][:, cols])
        sigma = jax.nn.sigmoid(gate)
        silu = gate * sigma
        v.hidden[:, cols] = (silu * up).astype(BF16)
        v.slope[:, cols] = up * sigma * (1.0 + gate * (1.0 - sigma))
        v.silu[:, cols] = silu
        return 0

    lax.fori_loop(0, hidden_own // 256, hidden_columns, 0)
    cot_rest.wait()
    given += loads.start(v.cot[1], out.cot)
    down_w.end()

    def grad_columns(j, _):
        cols = pl.ds(pl.multiple_of(j * 256, 256), 256)
        grad = dotb(v.cot[0][...], v.down[0][cols, :], NT)
        grad = grad + dotb(v.cot[1][...], v.down[1][cols, :], NT)
        v.gate_grad[:, cols] = (grad * v.slope[:, cols]).astype(BF16)
        v.up_grad[:, cols] = (grad * v.silu[:, cols]).astype(BF16)
        return 0

    lax.fori_loop(0, hidden_own // 256, grad_columns, 0)
    given += loads.start(v.hidden, out.hidden)
    given += loads.start(v.gate_grad, out.gate_grad)
    given += loads.start(v.up_grad, out.up_grad)
    for i in range(2):

        def model_columns(j, _, i=i):
            cols = pl.ds(pl.multiple_of(j * 256, 256), 256)
            value = dotb(v.gate_grad[...], v.gate[i][cols, :], NT)
            value = value + dotb(v.up_grad[...], v.up[i][cols, :], NT)
            v.part[i][:, cols] = value.astype(BF16)
            v.feed[i][:, cols] = dotb(v.hidden[...], v.down[i][:, cols]).astype(BF16)
            return 0

        lax.fori_loop(0, width // 256, model_columns, 0)
        given += loads.start(v.part[i], out.part[i])
        given += loads.start(v.feed[i], out.feed[i])
    settle(saved[0])
    settle(saved[1])
    settle(given)


def forward_all(bits, front):
    span, width = front.inputs.shape
    heads, hw = front.kern.shape[0], front.kern.shape[-1]
    wide = 4 * hw
    hidden_own = front.gate.shape[1] // 2
    rows = (span, width)
    kept = [(3, 2, HALF, HALF), (3, 2, HALF, HALF), (3, HALF, HALF)]

    def room(shape, dtype=BF16):
        return pltpu.VMEM(shape, dtype)

    def twice(shape, dtype=BF16):
        return [room(shape, dtype) for _ in range(2)]

    rooms = Rooms(
        x=twice(rows),
        cot=twice(rows),
        attn=twice((heads, width, wide)),
        out=twice((2 * heads * hw, width)),
        out_far=twice((2 * heads * hw, width)),
        gate=twice((width, hidden_own)),
        up=twice((width, hidden_own)),
        down=twice((hidden_own, width)),
        act=twice(rows),
        two=twice(rows),
        mid=twice(rows, F32),
        proj=room((heads, span, wide)),
        logit=room((heads, span, 1), F32),
        attended=room((heads, span, hw)),
        near=room((span, 2 * heads * hw)),
        far=room((span, 2 * heads * hw)),
        hidden=room((span, hidden_own)),
        gate_grad=room((span, hidden_own)),
        up_grad=room((span, hidden_own)),
        slope=room((span, hidden_own), F32),
        silu=room((span, hidden_own), F32),
        part=twice(rows),
        feed=twice(rows),
        kept=[[room((1,) + shape) for shape in kept] for _ in range(2)],
        local_sem=pltpu.SemaphoreType.DMA((64,)),
        send_sem=pltpu.SemaphoreType.DMA((96,)),
        recv_sem=pltpu.SemaphoreType.DMA((96,)),
    )

    def give(shape, dtype=BF16):
        return jax.ShapeDtypeStruct(shape, dtype)

    made = Made(
        part=[give(rows)] * 2,
        feed=[give(rows)] * 2,
        cot=give(rows),
        hidden=give((span, hidden_own)),
        gate_grad=give((span, hidden_own)),
        up_grad=give((span, hidden_own)),
        two=[give(rows)] * 2,
        mid=[give(rows, F32)] * 2,
        rinv_one=give((span, 1), F32),
        rinv_two=give((span, 1), F32),
        gains=give((2, width), F32),
        near=give((span, 2 * heads * hw)),
        proj=give((heads, span, wide)),
        logit=give((heads, span, 1), F32),
        kept=[give((heads,) + shape) for shape in kept],
        act=[give(rows)] * 2,
        x=give(rows),
        out=give((2 * heads * hw, width)),
        attn=give((heads, width, wide)),
        beta=give(front.beta.shape),
    )
    any_spec = pl.BlockSpec(memory_space=pl.ANY)
    vmem_spec = pl.BlockSpec(memory_space=pltpu.VMEM)
    specs = jax.tree.map(lambda _: any_spec, front)
    specs = specs._replace(
        beta=vmem_spec,
        gains=vmem_spec,
        kern=vmem_spec,
        lengths=pl.BlockSpec(memory_space=pltpu.SMEM),
    )
    out_specs = jax.tree.map(lambda _: any_spec, made)
    out_specs = out_specs._replace(
        rinv_one=vmem_spec, rinv_two=vmem_spec, gains=vmem_spec, beta=vmem_spec
    )
    return pl.pallas_call(
        functools.partial(front_body, bits),
        in_specs=[specs],
        out_specs=[out_specs],
        out_shape=[made],
        scratch_shapes=[rooms],
        compiler_params=pltpu.CompilerParams(
            collective_id=1, has_side_effects=True, vmem_limit_bytes=62 * 2**20
        ),
        name="forward_all",
    )(front)[0]


def on_device(
    group_count,
    inputs,
    lengths,
    gain_attn,
    attn_proj,
    beta_proj,
    conv_kernel,
    out_proj,
    gain_ffn,
    gate_proj,
    up_proj,
    down_proj,
    cotangent,
):
    width = inputs.shape[1]
    heads, hw = conv_kernel.shape[1], conv_kernel.shape[2]
    bits = group_count.bit_length() - 1
    attn_all = jnp.transpose(attn_proj, (1, 0, 2))
    out_rows = out_proj.reshape(-1, width)
    kern = jnp.transpose(conv_kernel, (1, 0, 2))
    beta_rows = beta_proj.T
    gains = jnp.stack([gain_attn, gain_ffn])
    made = forward_all(
        bits,
        Front(
            inputs=inputs,
            cot=cotangent,
            attn_all=attn_all,
            out=out_rows,
            gate=gate_proj,
            up=up_proj,
            down=down_proj,
            beta=beta_rows,
            gains=gains,
            kern=kern,
            lengths=lengths,
        ),
    )
    given = Given(
        part=made.part,
        feed=made.feed,
        cot=[cotangent, made.cot],
        hidden=made.hidden,
        gate_grad=made.gate_grad,
        up_grad=made.up_grad,
        two=made.two,
        mid=made.mid,
        rinv_one=made.rinv_one,
        rinv_two=made.rinv_two,
        gains=[gains, made.gains],
        near=made.near,
        out=[out_rows, made.out],
        proj=made.proj,
        logit=made.logit,
        kern=kern,
        kept=made.kept,
        act=made.act,
        x=[inputs, made.x],
        attn_all=attn_all,
        attn_peer=made.attn,
        beta=[beta_rows, made.beta],
    )
    (down_sum, gate_sum, up_sum, out_sum, attn_sum), outputs, grad_inputs, small = backward_all(
        bits, given
    )
    rows = width // 128
    gain_one_sum = small[0:rows].reshape(-1)
    gain_two_sum = small[8 : 8 + rows].reshape(-1)
    at = 16 + 2 * heads * rows
    beta_sum = small[16:at].reshape(2, heads, width)
    beta_sum = jnp.where(lax.axis_index("wd") == 0, beta_sum, beta_sum[::-1])
    beta_sum = beta_sum.reshape(2 * heads, width).T
    kern_sum = small[at : at + KCONV * heads].reshape(heads, KCONV, hw)
    attn_sum = attn_sum.reshape(2 * heads, width, -1)
    return (
        outputs,
        grad_inputs,
        gain_one_sum,
        jnp.transpose(attn_sum, (1, 0, 2)).astype(F32),
        beta_sum,
        jnp.transpose(kern_sum, (1, 0, 2)),
        out_sum.astype(F32).reshape(out_proj.shape),
        gain_two_sum,
        gate_sum.astype(F32).reshape(gate_proj.shape),
        up_sum.astype(F32).reshape(up_proj.shape),
        down_sum.astype(F32).reshape(down_proj.shape),
    )


def solution(mesh):
    return jax.shard_map(
        functools.partial(on_device, mesh.shape["dp"]),
        mesh=mesh,
        in_specs=(
            P("dp", "wd"),
            P("dp"),
            P("wd"),
            P("wd", "tp", None),
            P("wd", "tp"),
            P(None, ("tp", "wd"), None),
            P("tp", None, "wd"),
            P("wd"),
            P("wd", "tp"),
            P("wd", "tp"),
            P("tp", "wd"),
            P("dp", "wd"),
        ),
        out_specs=(
            P("dp", "wd"),
            P("dp", "wd"),
            P("wd"),
            P("wd", "tp", None),
            P("wd", "tp"),
            P(None, ("tp", "wd"), None),
            P("tp", None, "wd"),
            P("wd"),
            P("wd", "tp"),
            P("wd", "tp"),
            P("tp", "wd"),
        ),
        check_vma=False,
    )
```

```python
import functools
from typing import Any, NamedTuple

import jax
import jax.numpy as jnp
import numpy as np
from jax import lax
from jax.experimental import pallas as pl
from jax.experimental.pallas import tpu as pltpu
from jax.sharding import PartitionSpec as P

norm_eps = 1e-06
KCONV = 4
HALF = 256
F32 = jnp.float32
BF16 = jnp.bfloat16
NT = (((1,), (1,)), ((), ()))
NN = (((1,), (0,)), ((), ()))


def dotb(a, b, dims=NN):
    return lax.dot_general(a, b, dims, preferred_element_type=F32)


def split(a):
    hi = a.astype(BF16)
    return hi, (a - hi.astype(F32)).astype(BF16)


def dot3(a, b, dims=NN):
    (ah, al), (bh, bl) = a, b
    return dotb(ah, bh, dims) + (dotb(al, bh, dims) + dotb(ah, bl, dims))


def shift_down(a, m):
    if m == 0:
        return a
    rows = lax.broadcasted_iota(jnp.int32, a.shape, 0)
    return jnp.where(rows >= m, pltpu.roll(a, m, 0), 0.0)


def shift_up(a, m):
    if m == 0:
        return a
    n = a.shape[0]
    rows = lax.broadcasted_iota(jnp.int32, a.shape, 0)
    return jnp.where(rows < n - m, pltpu.roll(a, n - m, 0), 0.0)


def house_of(raws, kern):
    conv = kern[0:1] * raws
    for m in range(1, KCONV):
        conv = conv + kern[m : m + 1] * shift_down(raws, m)
    scale = lax.rsqrt(jnp.sum(conv * conv, -1, keepdims=True) + 1e-06)
    return conv * scale, scale


def forward_body(len_ref, proj_ref, logit_ref, kern_ref, o_ref, x_ref, w_ref, p_ref):
    length = len_ref[0]
    hw = o_ref.shape[-1]
    q = proj_ref[:, 0:hw]
    k = proj_ref[:, hw : 2 * hw]
    v = proj_ref[:, 2 * hw : 3 * hw]
    raws = proj_ref[:, 3 * hw : 4 * hw].astype(F32)
    house, _ = house_of(raws, kern_ref[0])
    beta = 2.0 * jax.nn.sigmoid(logit_ref[0])
    hh, hl = split(house)
    top, low = slice(0, HALF), slice(HALF, 2 * HALF)
    ri = lax.broadcasted_iota(jnp.int32, (HALF, HALF), 0)
    ci = lax.broadcasted_iota(jnp.int32, (HALF, HALF), 1)
    strict = ri > ci
    causal = ri >= ci
    h_left = jnp.concatenate([hh, hl, hh], 1)
    h_right = jnp.concatenate([hh, hh, hl], 1)
    h_two = jnp.concatenate([hh, hl], 1)
    k_two = jnp.concatenate([k, k], 1)
    q_two = jnp.concatenate([q, q], 1)

    def gram(a, b):
        return dotb(h_left[a], h_right[b], NT)

    def keyed(a, b):
        return dotb(h_two[a], k_two[b], NT)

    def asked(a, b):
        return dotb(q_two[a], h_two[b], NT)

    n11 = beta[top] * jnp.where(strict, gram(top, top), 0.0)
    n22 = beta[low] * jnp.where(strict, gram(low, low), 0.0)
    n21 = split(beta[low] * gram(low, top))
    inverses = [n11, n22]
    level = 1
    xor = ri ^ ci
    bits = [split(n11), split(n22)]
    current = None
    while level < HALF:
        mask = (xor >= level) & (xor < 2 * level)
        for d in range(2):
            if level == 1:
                eye = jnp.where(ri == ci, 1.0, 0.0)
                inverses[d] = eye - jnp.where(mask, inverses[d], 0.0)
            else:
                t = split(inverses[d])
                zero = jnp.zeros((), BF16)
                c = tuple(jnp.where(mask, part, zero) for part in bits[d])
                inverses[d] = inverses[d] - dot3(t, split(dot3(c, t)))
        level *= 2
    t1, t2 = split(inverses[0]), split(inverses[1])
    b11 = split(beta[top] * jnp.where(strict, keyed(top, top), 0.0))
    b22 = split(beta[low] * jnp.where(strict, keyed(low, low), 0.0))
    b21f = beta[low] * keyed(low, top)
    b21 = split(b21f)
    m11 = split(jnp.where(causal, asked(top, top), 0.0))
    m22 = split(jnp.where(causal, asked(low, low), 0.0))
    m21 = asked(low, top)
    x11 = split(dot3(t1, b11))
    x22 = split(dot3(t2, b22))
    x21 = split(dot3(t2, split(b21f - dot3(n21, x11))))
    w11 = split(dot3(m11, t1))
    w22 = split(dot3(m22, t2))
    w21 = split(dot3(split(m21 - dot3(w22, n21)), t1))
    scale = hw ** (-0.5)

    def soften(scores, allowed):
        scores = jnp.where(allowed, scores, -1e30)
        weights = jnp.exp(scores - jnp.max(scores, -1, keepdims=True))
        return (weights * (1.0 / jnp.sum(weights, -1, keepdims=True))).astype(BF16)

    s11 = (dotb(q[top], k[top], NT) - dot3(w11, b11)) * scale
    s21 = (dotb(q[low], k[top], NT) - (dot3(w21, b11) + dot3(w22, b21))) * scale
    s22 = (dotb(q[low], k[low], NT) - dot3(w22, b22)) * scale
    p1 = soften(s11, causal & (ci < length))
    p2 = soften(
        jnp.concatenate([s21, s22], 1),
        jnp.concatenate([ci < length, causal & (ci + HALF < length)], 1),
    )
    o_ref[top, :] = dotb(p1, v[top]).astype(o_ref.dtype)
    o_ref[low, :] = dotb(p2, v).astype(o_ref.dtype)
    p_ref[0, 0] = p1
    p_ref[0, 1] = p2[:, :HALF]
    p_ref[0, 2] = p2[:, HALF:]
    for i, (xx, ww) in enumerate(((x11, w11), (x21, w21), (x22, w22))):
        for j in range(2):
            x_ref[0, i, j] = xx[j]
            w_ref[0, i, j] = ww[j].T


def backward_body(proj_ref, logit_ref, kern_ref, g_ref, x_ref, w_ref, p_ref, dproj_ref, dlogit_ref, dkern_ref):
    hw = g_ref.shape[-1]
    q = proj_ref[:, 0:hw]
    k = proj_ref[:, hw : 2 * hw]
    v = proj_ref[:, 2 * hw : 3 * hw]
    raws = proj_ref[:, 3 * hw : 4 * hw].astype(F32)
    kern = kern_ref[0]
    house, rs = house_of(raws, kern)
    beta = 2.0 * jax.nn.sigmoid(logit_ref[0])
    g = g_ref[...]
    hh, hl = split(house)
    top, low = slice(0, HALF), slice(HALF, 2 * HALF)
    ri = lax.broadcasted_iota(jnp.int32, (HALF, HALF), 0)
    ci = lax.broadcasted_iota(jnp.int32, (HALF, HALF), 1)
    strict = ri > ci
    causal = ri >= ci
    scale = hw ** (-0.5)
    p11, p21, p22 = (p_ref[0, i] for i in range(3))
    x11, x21, x22 = ((x_ref[0, i, 0], x_ref[0, i, 1]) for i in range(3))
    w11, w21, w22 = ((w_ref[0, i, 0], w_ref[0, i, 1]) for i in range(3))
    q_t, g_t = q.T, g.T
    ht_h, ht_l = hh.T, hl.T

    def soften_back(probs, dprobs):
        pf = probs.astype(F32)
        mixed = pf * dprobs
        return (mixed - pf * jnp.sum(mixed, -1, keepdims=True)) * scale

    z1 = soften_back(p11, dotb(g[top], v[top], NT))
    z2 = soften_back(jnp.concatenate([p21, p22], 1), dotb(g[low], v, NT))
    z11 = split(z1)
    z21 = split(z2[:, :HALF])
    z22 = split(z2[:, HALF:])
    u11 = jnp.where(causal, dot3(z11, x11, NT), 0.0)
    u21 = dot3(z21, x11, NT)
    u22 = jnp.where(causal, dot3(z21, x21, NT) + dot3(z22, x22, NT), 0.0)
    u11, u21, u22 = split(u11), split(u21), split(u22)
    b11 = jnp.where(strict, dot3(w11, z11) + dot3(w21, z21), 0.0)
    b21 = dot3(w22, z21)
    b22 = jnp.where(strict, dot3(w22, z22), 0.0)
    a11 = jnp.where(strict, dot3(w11, u11) + dot3(w21, u21), 0.0)
    a21 = dot3(w22, u21)
    a22 = jnp.where(strict, dot3(w22, u22), 0.0)
    b11s, b21s, b22s = split(b11), split(b21), split(b22)
    a11s, a21s, a22s = split(a11), split(a21), split(a22)

    def rows(c11, c21, c22, mats):
        (mh, ml) = mats
        first = dotb(c11[0], mh[top]) + dotb(c11[1], mh[top])
        second = dotb(c21[0], mh[top]) + dotb(c21[1], mh[top])
        second = second + dotb(c22[0], mh[low]) + dotb(c22[1], mh[low])
        if ml is not None:
            first = first + dotb(c11[0], ml[top])
            second = second + dotb(c21[0], ml[top]) + dotb(c22[0], ml[low])
        return jnp.concatenate([first, second], 0)

    def cols(c11, c21, c22, mats):
        (mh, ml) = mats
        first = dotb(mh[:, top], c11[0]) + dotb(mh[:, top], c11[1])
        first = first + dotb(mh[:, low], c21[0]) + dotb(mh[:, low], c21[1])
        second = dotb(mh[:, low], c22[0]) + dotb(mh[:, low], c22[1])
        if ml is not None:
            first = first + dotb(ml[:, top], c11[0]) + dotb(ml[:, low], c21[0])
            second = second + dotb(ml[:, low], c22[0])
        return jnp.concatenate([first, second], 1)

    dq = rows(z11, z21, z22, (k, None)) - rows(u11, u21, u22, (hh, hl))
    bk = rows(b11s, b21s, b22s, (k, None))
    nh = rows(a11s, a21s, a22s, (hh, hl))
    mixed = nh - bk
    dbeta = jnp.sum(house * mixed, -1, keepdims=True)
    dlogit_ref[0] = dbeta * beta * (1.0 - 0.5 * beta)
    bb = [split(beta[s] * b) for s, b in ((top, b11), (low, b21), (low, b22))]
    ab = [split(beta[s] * a) for s, a in ((top, a11), (low, a21), (low, a22))]
    dk_t = cols(z11, z21, z22, (q_t, None)) - cols(*bb, (ht_h, ht_l))
    dh_t = cols(*ab, (ht_h, ht_l)) - cols(u11, u21, u22, (q_t, None))
    dv_t = jnp.concatenate(
        [dotb(g_t[:, top], p11) + dotb(g_t[:, low], p21), dotb(g_t[:, low], p22)], 1
    )
    dh = beta * mixed + dh_t.T
    dc = rs * (dh - house * jnp.sum(house * dh, -1, keepdims=True))
    dr = kern[0:1] * dc
    taps = [jnp.sum(dc * raws, 0, keepdims=True)]
    for m in range(1, KCONV):
        up = shift_up(dc, m)
        dr = dr + kern[m : m + 1] * up
        taps.append(jnp.sum(up * raws, 0, keepdims=True))
    dkern_ref[0] = jnp.concatenate(taps, 0)
    dproj_ref[:, 0:hw] = dq.astype(BF16)
    dproj_ref[:, hw : 2 * hw] = dk_t.T.astype(BF16)
    dproj_ref[:, 2 * hw : 3 * hw] = dv_t.T.astype(BF16)
    dproj_ref[:, 3 * hw : 4 * hw] = dr.astype(BF16)


MESH = pl.DeviceIdType.MESH
TN = (((0,), (0,)), ((), ()))


def own_bits(bits):
    group = lax.axis_index("dp")
    return group, [lax.rem(lax.div(group, 1 << b), 2) for b in range(bits)]


class Reduce:
    def __init__(self, order, rows, columns, peer):
        self.order, self.rows, self.columns, self.peer = order, rows, columns, peer
        self.bits = len(order)

    def dims(self, taken):
        return (2,) * (self.bits - taken) + (self.rows, self.columns)

    def scratch(self):
        shapes = [pltpu.VMEM(self.dims(1), BF16)]
        shapes += [pltpu.VMEM(self.dims(1 + k), BF16) for k in range(self.bits)]
        shapes += [pltpu.VMEM(self.dims(self.bits), BF16)]
        if self.peer:
            shapes += [pltpu.VMEM(self.dims(self.bits), BF16)]
        count = 2 * self.bits + 1
        return shapes + [pltpu.SemaphoreType.DMA((count,)), pltpu.SemaphoreType.DMA((count + 1,))]

    def rotating(self):
        return [pltpu.VMEM(self.dims(1 + k), BF16) for k in range(self.bits)]

    def bind(self, group, bit_of, compute, out, refs):
        self.group, self.bit_of, self.compute, self.out = group, bit_of, compute, out
        refs = list(refs)
        self.kept = refs.pop(0)
        self.recv = [refs.pop(0) for _ in range(self.bits)]
        self.shard = refs.pop(0)
        self.from_peer = refs.pop(0) if self.peer else None
        self.send_sem, self.recv_sem = refs
        stages = [functools.partial(self.halve, k) for k in range(self.bits)] + [self.finish]
        if self.peer:
            stages.append(self.take_peer)
        stages += [functools.partial(self.double, k) for k in range(1, self.bits)] + [self.end]
        self.stages = stages
        self.copies = {}
        return self

    def at(self, fixed, gone=()):
        return tuple(
            fixed.get(b, slice(None)) for b in range(self.bits - 1, -1, -1) if b not in gone
        )

    def remote(self, slot, source, target, bit=None):
        if bit is None:
            device = {"wd": 1 - lax.axis_index("wd")}
        else:
            step = 1 << bit
            device = {"dp": self.group + step - 2 * step * self.bit_of[bit]}
        copy = pltpu.make_async_remote_copy(
            src_ref=source,
            dst_ref=target,
            send_sem=self.send_sem.at[slot],
            recv_sem=self.recv_sem.at[slot],
            device_id=device,
            device_id_type=MESH,
        )
        copy.start()
        self.copies[slot] = copy

    def total(self, step, fixed, target):
        free = [b for b in range(self.bits - 1, -1, -1) if b not in fixed]
        part = 32 if self.rows % 32 == 0 else self.rows
        for combo in range(1 << len(free)):
            place = {b: (combo >> i) & 1 for i, b in enumerate(reversed(free))}
            where = {**fixed, **place}
            head = tuple(place[b] for b in free)

            def body(i, _):
                rows = pl.ds(pl.multiple_of(i * part, part), part)
                value = self.kept[self.at(where, self.order[:1]) + (rows,)].astype(F32)
                for j in range(step):
                    gone = self.order[: j + 1]
                    value = value + self.recv[j][self.at(where, gone) + (rows,)].astype(F32)
                target[head + (rows,)] = value.astype(BF16)
                return 0

            lax.fori_loop(0, self.rows // part, body, 0)

    def halve(self, k):
        bit = self.order[k]
        if k == 0:
            self.compute(self, self.at({bit: 1 - self.bit_of[bit]}), self.send[0])
        else:
            self.copies[k - 1].wait()
            fixed = {b: self.bit_of[b] for b in self.order[:k]}
            fixed[bit] = 1 - self.bit_of[bit]
            self.total(k, fixed, self.send[k])
        self.remote(k, self.send[k], self.recv[k], bit)
        if k == 0:
            self.compute(self, self.at({bit: self.bit_of[bit]}), self.kept)

    def finish(self):
        self.copies[self.bits - 1].wait()
        mine = {b: self.bit_of[b] for b in range(self.bits)}
        self.total(self.bits, mine, self.shard)
        if self.peer:
            self.remote(self.bits, self.shard, self.from_peer)
        else:
            self.begin(self.shard)

    def take_peer(self):
        self.copies[self.bits].wait()
        self.begin(self.from_peer)

    def begin(self, block):
        mine = self.at({b: self.bit_of[b] for b in range(self.bits)})
        local = pltpu.make_async_copy(block, self.out(mine), self.recv_sem.at[2 * self.bits + 1])
        local.start()
        self.copies[-1] = local
        self.remote(self.bits + 1, block, self.out(mine), self.order[-1])

    def double(self, k):
        if k == 1:
            self.copies[-1].wait()
        self.copies[self.bits + k].wait()
        bit = self.order[self.bits - 1 - k]
        fixed = {b: self.bit_of[b] for b in self.order[: self.bits - k]}
        slab = self.out(self.at(fixed))
        self.remote(self.bits + 1 + k, slab, slab, bit)

    def end(self):
        if self.bits == 1:
            self.copies[-1].wait()
        self.copies[2 * self.bits].wait()


def turned(source, target):
    rows, lead = target.shape[-2], target.shape[:-2]
    if rows % 16 == 0:
        target[...] = source[...].T.reshape(target.shape)
    else:
        value = source[...].astype(F32).T
        for i, place in enumerate(np.ndindex(*lead)):
            target[place] = value[i * rows : (i + 1) * rows].astype(BF16)


def gradient(left, right):
    def compute(piece, where, target):
        values = right()
        if piece.rows % 16 == 0:
            part = left[where]
            part = part.reshape(-1, part.shape[-1])
            target[...] = dotb(part, values).astype(BF16).reshape(target.shape)
        else:
            for place in np.ndindex(*target.shape[:-2]):
                free = iter(place)
                index = tuple(next(free) if isinstance(w, slice) else w for w in where)
                target[place] = dotb(left[index + tuple(free)], values).astype(BF16)

    return compute


class Chain:
    bits = 3
    last_z = 3

    def __init__(self, rows, columns, peer, split_first):
        self.rows, self.columns, self.peer, self.split_first = rows, columns, peer, split_first

    def scratch(self):
        block = (self.rows, self.columns)
        if self.split_first:
            shapes = [pltpu.VMEM((2,) + block, BF16)] * 2 + [pltpu.VMEM(block, BF16)] * 2
        else:
            shapes = [pltpu.VMEM((2, 2) + block, BF16)] + [pltpu.VMEM((2,) + block, BF16)] * 2
        return shapes + [pltpu.SemaphoreType.DMA((8,)), pltpu.SemaphoreType.DMA((9,))]

    def rotating(self):
        return [pltpu.VMEM((2, self.rows, self.columns), BF16)] if self.split_first else []

    def bind(self, group, bit_of, compute, out, refs):
        self.compute, self.out = compute, out
        self.group, self.y, self.z = group, bit_of[0], lax.div(group, 2)
        refs = list(refs)
        self.kept = refs.pop(0)
        if self.split_first:
            self.halved = refs.pop(0)
        self.come = refs[:2]
        self.send_sem, self.recv_sem = refs[2:]
        ends = [self.finish] + ([self.take_peer] if self.peer else [])
        if self.split_first:
            self.stages = [self.first_split, self.climb_first]
            self.stages += [self.climb_second, self.climb_third] + ends
            self.stages += [functools.partial(self.fall, k) for k in range(3)] + [self.end]
        else:
            self.stages = [self.first_whole, self.climb_second, self.climb_third, self.halve_end]
            self.stages += ends + [self.fall_start]
            self.stages += [functools.partial(self.fall, k) for k in range(3)] + [self.end]
        return self

    def hop(self, slot, source, target, step=None, axis=None):
        if axis is not None:
            device = {axis: 1 - lax.axis_index(axis)}
        elif step is None:
            device = {"dp": self.group + 1 - 2 * self.y}
        else:
            device = {"dp": self.group + 2 * step}
        return pltpu.make_async_remote_copy(
            src_ref=source,
            dst_ref=target,
            send_sem=self.send_sem.at[slot],
            recv_sem=self.recv_sem.at[slot],
            device_id=device,
            device_id_type=MESH,
        )

    def climb(self, part):
        return self.hop(part, self.kept.at[part], self.come[part], 1 if part else -1)

    def part_of_out(self, part):
        if self.split_first:
            return self.out((self.y, part))
        return self.out((part, slice(None)))

    def descend(self, part):
        ref = self.part_of_out(part)
        return self.hop(2 + part, ref, ref, -1 if part else 1)

    def across(self, part):
        ref = self.out((self.y, part)) if self.split_first else self.out((part, self.y))
        return self.hop(4 + part, ref, ref)

    def swap(self, part):
        spare = self.come[1 - part] if self.split_first else self.come[1 - part].at[1]
        block = self.kept.at[part] if self.split_first else self.kept.at[part, self.y]
        return self.hop(6, block, spare, axis="wd")

    def end_swap(self, part):
        block = self.kept.at[part, 1 - self.y]
        return self.hop(7, block, self.come[1 - part].at[0])

    def add(self, target, *others):
        part = 32 if self.rows % 32 == 0 else self.rows

        def body(i, _):
            rows = pl.ds(pl.multiple_of(i * part, part), part)
            value = target[rows].astype(F32)
            for other in others:
                value = value + other[rows].astype(F32)
            target[rows] = value.astype(BF16)
            return 0

        lax.fori_loop(0, self.rows // part, body, 0)

    def gather(self, part, first):
        if self.split_first:
            others = [self.halved.at[part]] + ([] if first else [self.come[part]])
            self.add(self.kept.at[part], *others)
        elif not first:
            for y in range(2):
                self.add(self.kept.at[part, y], self.come[part].at[y])

    def at_level(self, level, action):
        pl.when(self.z == level)(lambda: action(1))
        pl.when(self.z == self.last_z - level)(lambda: action(0))

    def first_split(self):
        self.compute(self, (1 - self.y,), self.send[0])
        self.hop(7, self.send[0], self.halved).start()
        self.compute(self, (self.y,), self.kept)

    def climb_first(self):
        self.hop(7, self.send[0], self.halved).wait()

        def action(part):
            self.gather(part, True)
            self.climb(part).start()

        self.at_level(0, action)

    def first_whole(self):
        self.compute(self, (), self.kept)
        self.at_level(0, lambda part: self.climb(part).start())

    def onwards(self, level):
        def action(part):
            self.climb(part).wait_recv()
            self.gather(part, False)
            self.climb(part).start()

        self.at_level(level, action)

    def climb_second(self):
        self.onwards(1)

    def climb_third(self):
        self.onwards(2)

    def halve_end(self):
        def action(part):
            self.climb(part).wait_recv()
            self.add(self.kept.at[part, 1 - self.y], self.come[part].at[1 - self.y])
            self.end_swap(part).start()

        self.at_level(3, action)

    def finish(self):
        def action(part):
            if self.split_first:
                self.climb(part).wait_recv()
                self.gather(part, False)
            else:
                self.end_swap(part).wait()
                self.add(
                    self.kept.at[part, self.y],
                    self.come[part].at[self.y],
                    self.come[1 - part].at[0],
                )
            if self.peer:
                self.swap(part).start()
            else:
                self.begin(part, False)

        self.at_level(3, action)

    def take_peer(self):
        def action(part):
            self.swap(part).wait()
            self.begin(part, True)

        self.at_level(3, action)

    def local(self, part, taken):
        if self.split_first:
            block = self.come[1 - part] if taken else self.kept.at[part]
            ref = self.out((self.y, part))
        else:
            block = self.come[1 - part].at[1] if taken else self.kept.at[part, self.y]
            ref = self.out((part, self.y))
        return block, ref, pltpu.make_async_copy(block, ref, self.recv_sem.at[8])

    def begin(self, part, taken):
        block, ref, copy = self.local(part, taken)
        copy.start()
        self.hop(4 + part, block, ref).start()
        if self.split_first:
            self.hop(2 + part, block, ref, -1 if part else 1).start()

    def fall_start(self):
        def action(part):
            self.local(part, self.peer)[2].wait()
            self.across(part).wait()
            self.descend(part).start()

        self.at_level(3, action)

    def fall(self, k):
        def action(part):
            self.descend(part).wait_recv()
            if k < 2:
                self.descend(part).start()
            if self.split_first:
                self.across(part).start()

        self.at_level(2 - k, action)

    def end(self):
        def sent(part):
            self.climb(part).wait_send()

        def fallen(part):
            self.descend(part).wait_send()

        def here(part):
            self.local(part, self.peer)[2].wait()

        for level in range(3):
            self.at_level(level, sent)
        for level in range(1, 4):
            self.at_level(level, fallen)
        if self.split_first:
            self.at_level(3, here)
            for part in range(2):
                self.across(part).wait()


SMALL = 64
WHOLE_FIRST = (1, 3, 5, 7, 9, 11, 13, 15)


def chained(bits):
    return bits == 3


def depths(bits):
    return (4, 4) if chained(bits) else (2, 3)


class Given(NamedTuple):
    part: Any
    feed: Any
    cot: Any
    hidden: Any
    gate_grad: Any
    up_grad: Any
    two: Any
    mid: Any
    rinv_one: Any
    rinv_two: Any
    gains: Any
    near: Any
    out: Any
    proj: Any
    logit: Any
    kern: Any
    kept: Any
    act: Any
    x: Any
    attn_all: Any
    attn_peer: Any
    beta: Any


class Spots(NamedTuple):
    cot: Any
    hidden: Any
    gate_grad: Any
    up_grad: Any
    two: Any
    near: Any
    out_own: Any
    proj: Any
    core_in: Any
    core_own: Any
    sum: Any
    side_in: Any
    mid: Any
    mid_grad: Any
    branch: Any
    heads_grad: Any
    feed_out: Any
    feed_in: Any
    aw: Any
    dproj: Any
    logit: Any
    dlogit: Any
    dkern: Any
    kept: Any
    left_hidden: Any
    left: Any
    small: Any
    small_in: Any
    beta_out: Any
    beta_in: Any
    local_sem: Any
    send_sem: Any
    recv_sem: Any


class Loads:
    def __init__(self, sems):
        self.sems, self.used = sems, 0

    def start(self, source, target):
        copy = pltpu.make_async_copy(source, target, self.sems.at[self.used])
        self.used += 1
        copy.start()
        return [copy]


class Links:
    def __init__(self, send_sems, recv_sems):
        self.send_sems, self.recv_sems, self.used = send_sems, recv_sems, 0

    def start(self, device, source, target):
        copy = pltpu.make_async_remote_copy(
            src_ref=source,
            dst_ref=target,
            send_sem=self.send_sems.at[self.used],
            recv_sem=self.recv_sems.at[self.used],
            device_id=device,
            device_id_type=MESH,
        )
        self.used += 1
        copy.start()
        return copy


def settle(copies):
    for copy in copies:
        copy.wait()
    copies.clear()


def flipped(axis):
    return {axis: 1 - lax.axis_index(axis)}


def group_peer(group, bit_of, bit):
    step = 1 << bit
    return {"dp": group + step - 2 * step * bit_of[bit]}


def back_body(bits, plans, r, outs, out_ref, gin_ref, small_ref, v, rest):
    group, bit_of = own_bits(bits)
    lag, deep = depths(bits)
    count = len(plans)
    core, side = lax.axis_index("tp"), lax.axis_index("wd")
    span, width = r.cot[0].shape
    half = span // 2
    wide = v.aw.shape[-1]
    hw = wide // 4
    heads = r.kern.shape[0]
    model = 2 * width
    hidden_own = r.hidden.shape[1]
    mine = pl.ds(pl.multiple_of(core * half, half), half)
    far = pl.ds(pl.multiple_of((1 - core) * half, half), half)
    loads = Loads(v.local_sem)
    links = Links(v.send_sem, v.recv_sem)
    x_peer, c_peer = flipped("wd"), flipped("tp")

    barrier = pltpu.get_barrier_semaphore()
    for device in [group_peer(group, bit_of, b) for b in range(bits)] + [x_peer, c_peer]:
        pl.semaphore_signal(barrier, inc=1, device_id=device, device_id_type=MESH)
    if chained(bits):
        z = lax.div(group, 2)

        def greet_middle(step):
            device = {"dp": group + step}
            pl.semaphore_signal(barrier, inc=1, device_id=device, device_id_type=MESH)

        pl.when(z == 1)(lambda: greet_middle(2))
        pl.when(z == 2)(lambda: greet_middle(-2))
        inside = (z == 1) | (z == 2)
        pl.when(inside)(lambda: pl.semaphore_wait(barrier, bits + 3))
        pl.when(jnp.logical_not(inside))(lambda: pl.semaphore_wait(barrier, bits + 2))
    else:
        pl.semaphore_wait(barrier, bits + 2)

    first = [links.start(c_peer, r.part[i].at[far], v.core_in.at[i]) for i in range(2)]
    got_hidden = loads.start(r.hidden, v.hidden)
    got_cot = [loads.start(r.cot[i], v.cot[i]) for i in range(2)]
    got_part = [loads.start(r.part[i].at[mine], v.core_own.at[i])[0] for i in range(2)]
    got_ffn = [loads.start(r.two[i], v.two[i])[0] for i in range(2)]
    got_ffn += loads.start(r.gate_grad, v.gate_grad)
    got_ffn += loads.start(r.up_grad, v.up_grad)
    got_mid = [loads.start(r.mid[i].at[mine], v.mid.at[i])[0] for i in range(2)]
    own_rows = pl.ds(pl.multiple_of(side * heads * hw, heads * hw), heads * hw)
    got_out = [loads.start(r.out[i].at[own_rows], v.out_own.at[i])[0] for i in range(2)]
    got_near = loads.start(r.near, v.near)
    got_proj = loads.start(r.proj, v.proj)

    def load_kept(h):
        copies = [loads.start(a.at[pl.ds(h, 1)], b)[0] for a, b in zip(r.kept, v.kept)]
        return copies + loads.start(r.logit.at[pl.ds(h, 1)], v.logit)

    got_kept = load_kept(0)

    pieces = []
    shared, used = {}, {}
    cut_width, cut_hidden = width // 2, hidden_own // 2

    def piece(left, right, view):
        plan = plans[len(pieces)]
        size = len(plan.scratch())
        own = [rest.pop(0) for _ in range(size)]
        pieces.append(plan.bind(group, bit_of, gradient(left, right), view, own))

    def columns(out, start, size):
        cols = pl.ds(pl.multiple_of(start, 128), size)
        return lambda where: out.at[where + (slice(None), cols)]

    def owner(j):
        return side if j == 0 else 1 - side

    for j in range(2):
        for i in range(2):
            cut = slice(i * cut_width, (i + 1) * cut_width)
            piece(
                v.left_hidden,
                lambda j=j, cut=cut: v.cot[j][:, cut],
                lambda where, j=j, cut=cut: outs[0].at[(owner(j),) + where + (slice(None), cut)],
            )
    for n, values in ((1, v.gate_grad), (2, v.up_grad)):
        for j in range(2):
            for i in range(2):
                cut = slice(i * cut_hidden, (i + 1) * cut_hidden)
                piece(
                    v.left.at[j],
                    lambda values=values, cut=cut: values[:, cut],
                    columns(outs[n], owner(j) * hidden_own + i * cut_hidden, cut_hidden),
                )
    for i in range(2):
        cut = slice(i * cut_width, (i + 1) * cut_width)
        piece(
            v.left.at[0],
            lambda cut=cut: v.branch[0, :, cut],
            lambda where, cut=cut: outs[3].at[where + (slice(None), cut)],
        )
    for h in range(heads):
        for j in range(2):
            piece(
                v.left.at[j],
                lambda h=h: v.dproj[h],
                lambda where, h=h, j=j: outs[4].at[(owner(j) * heads + h,) + where],
            )
    for i, plan in enumerate(plans):
        shapes = plan.rotating()
        if shapes:
            key = (plan.rows, plan.columns)
            place = shared.setdefault(key, [])
            at = used.get(key, 0)
            used[key] = at + 1
            if at < deep:
                place.append([rest.pop(0) for _ in shapes])
            pieces[i].send = place[at % deep]

    position = [0]

    def pump(until):
        last = max(i + lag * len(p.stages) for i, p in enumerate(pieces))
        for slot in range(position[0], min(until, last)):
            for i in reversed(range(count)):
                step, off = divmod(slot - i, lag)
                if off == 0 and 0 <= step < len(pieces[i].stages):
                    pieces[i].stages[step]()
        position[0] = max(position[0], until)

    settle(got_hidden)
    turned(v.hidden, v.left_hidden)
    settle(got_cot[0])
    pump(2)
    settle(got_cot[1])
    pump(4)
    settle(got_part)
    settle(first)
    for i in range(2):
        v.sum[i] = (v.core_own[i].astype(F32) + v.core_in[i].astype(F32)).astype(BF16)
    first = [links.start(x_peer, v.sum.at[i], v.side_in.at[1 - i]) for i in range(2)]
    settle(got_ffn)
    for i in range(2):
        turned(v.two[i], v.left.at[i])
    pump(8)
    settle(first)
    settle(got_mid)

    def norm_back(base_of, rinv, gains):
        grads = [v.sum[i].astype(F32) + v.side_in[i].astype(F32) for i in range(2)]
        cross = sum(
            jnp.sum(grads[i] * gains[i] * base_of(i), -1, keepdims=True) for i in range(2)
        )
        cube = rinv * rinv * rinv * cross / model
        backs = [grads[i] * gains[i] * rinv - base_of(i) * cube for i in range(2)]
        return backs, jnp.sum(grads[0] * base_of(0) * rinv, 0, keepdims=True)

    gains = [g[1:2, :] for g in r.gains]
    backs, gain_two = norm_back(lambda i: v.mid[i], r.rinv_two[mine, :], gains)
    for i in range(2):
        value = v.cot[i][mine, :].astype(F32) + backs[i]
        if i == 0:
            v.mid_grad[...] = value
        v.branch[i, mine, :] = value.astype(BF16)
    first = [links.start(c_peer, v.branch.at[i, mine], v.branch.at[i, mine]) for i in range(2)]
    pump(9)
    settle(first)
    settle(got_out)
    grad = dotb(v.branch[0], v.out_own[0], NT) + dotb(v.branch[1], v.out_own[1], NT)
    for h in range(heads):
        v.heads_grad[h] = grad[:, h * hw : (h + 1) * hw].astype(BF16)
    first = [links.start(c_peer, r.feed[i].at[far], v.core_in.at[i]) for i in range(2)]
    got_part = [loads.start(r.feed[i].at[mine], v.core_own.at[i])[0] for i in range(2)]
    pump(10)
    settle(first)
    settle(got_part)
    feed = [v.core_own[i].astype(F32) + v.core_in[i].astype(F32) for i in range(2)]
    v.feed_out[...] = feed[1].astype(BF16)
    v.mid[0] = v.mid[0] + feed[0]
    first = [links.start(x_peer, v.feed_out, v.feed_in)]
    settle(got_proj)
    lanes = lax.broadcasted_iota(jnp.int32, (span, 128), 1)
    grad_beta = jnp.zeros((span, 128), F32)
    got_x = []

    def give_outputs():
        settle(first)
        v.feed_out[...] = (v.mid[0] + v.feed_in[...].astype(F32)).astype(BF16)
        first.append(links.start(c_peer, v.feed_out, out_ref.at[mine]))
        first.extend(loads.start(v.feed_out, out_ref.at[mine]))

    def take_inputs():
        settle(first)
        got_x.extend(loads.start(r.x[i].at[mine], v.core_own.at[i])[0] for i in range(2))

    for h in range(heads):
        settle(got_kept)
        got_aw = loads.start(r.attn_all.at[side * heads + h], v.aw.at[0])
        got_aw += loads.start(r.attn_peer.at[h], v.aw.at[1])
        backward_body(
            v.proj.at[h],
            v.logit,
            r.kern.at[pl.ds(h, 1)],
            v.heads_grad.at[h],
            v.kept[0],
            v.kept[1],
            v.kept[2],
            v.dproj.at[h],
            v.dlogit,
            v.dkern.at[pl.ds(h, 1)],
        )
        grad_beta = grad_beta + jnp.where(lanes == side * heads + h, v.dlogit[0], 0.0)
        if h + 1 < heads:
            got_kept = load_kept(h + 1)
        pump(10 + h)
        settle(got_aw)
        for i in range(2):
            value = dotb(v.dproj[h], v.aw[i], NT)
            if h > 0:
                value = value + v.cot[i][...].astype(F32)
            if h == heads - 1:
                low = grad_beta.astype(BF16)
                value = value + dotb(low[:, : 2 * heads], r.beta[i][...])
            v.cot[i][...] = value.astype(BF16)
        if h == 0:
            give_outputs()
        if h == min(1, heads - 1):
            take_inputs()
    beta_low = grad_beta.astype(BF16)
    first = [links.start(c_peer, v.cot[i].at[far], v.core_in.at[i]) for i in range(2)]
    pump(12)
    settle(got_near)
    turned(v.near, v.left.at[0])
    settle(first)
    for i in range(2):
        total = v.cot[i][mine, :].astype(F32) + v.core_in[i].astype(F32)
        v.sum[i] = total.astype(BF16)
    first = [links.start(x_peer, v.sum.at[i], v.side_in.at[1 - i]) for i in range(2)]
    pump(14)
    got_act = [loads.start(r.act[i], v.two[i])[0] for i in range(2)]
    settle(got_act)
    for i in range(2):
        turned(v.two[i], v.left.at[i])
    pump(15)
    settle(first)
    settle(got_x)
    gains = [g[0:1, :] for g in r.gains]
    backs, gain_one = norm_back(lambda i: v.core_own[i].astype(F32), r.rinv_one[mine, :], gains)
    v.feed_out[...] = (v.mid_grad[...] + backs[0]).astype(BF16)
    first = [links.start(c_peer, v.feed_out, gin_ref.at[mine])]
    first += loads.start(v.feed_out, gin_ref.at[mine])
    rows = width // 128
    small = v.small
    for i in range(rows):
        cut = slice(i * 128, (i + 1) * 128)
        small[0, i : i + 1, :] = gain_one[:, cut]
        small[0, 8 + i : 9 + i, :] = gain_two[:, cut]
    small[0, rows:8, :] = jnp.zeros((8 - rows, 128), F32)
    small[0, 8 + rows : 16, :] = jnp.zeros((8 - rows, 128), F32)
    gain_rows = pl.ds(0, 16)
    first.append(links.start(c_peer, small.at[0, gain_rows], v.small_in.at[bits, gain_rows]))
    for i in range(2):
        value = lax.dot_general(beta_low, v.two[i][...], TN, preferred_element_type=F32)
        v.beta_out[i] = jnp.where(side == 0, value[0:8], value[heads : heads + 8])
    first.append(links.start(x_peer, v.beta_out.at[1], v.beta_in))
    pump(16)
    settle(first)
    small[0, 0:16, :] = small[0, 0:16, :] + v.small_in[bits, 0:16, :]
    for h in range(heads):
        for i in range(rows):
            cut = slice(i * 128, (i + 1) * 128)
            at = 16 + h * rows + i
            small[0, at : at + 1, :] = v.beta_out[0, h : h + 1, cut]
            at = at + heads * rows
            small[0, at : at + 1, :] = v.beta_in[h : h + 1, cut]
    at = 16 + 2 * heads * rows
    taps = KCONV * heads
    small[0, at : at + taps, :] = v.dkern[...].reshape(taps, hw)
    if at + taps < small.shape[1]:
        small[0, at + taps :, :] = jnp.zeros((small.shape[1] - at - taps, 128), F32)
    for bit in range(bits):
        copy = links.start(group_peer(group, bit_of, bit), small.at[bit], v.small_in.at[bit])
        pump(17 + bit)
        copy.wait()
        small[bit + 1] = small[bit] + v.small_in[bit]
    small_ref[...] = small[bits]
    pump(1000)


def backward_all(bits, given):
    span, width = given.cot[0].shape
    hidden_own = given.hidden.shape[1]
    heads, hw = given.kern.shape[0], given.kern.shape[-1]
    wide = 4 * hw
    half = span // 2
    order_a = list(range(bits))
    order_b = [1, 0] + list(range(2, bits)) if bits > 1 else order_a
    shapes = [(hidden_own, width // 2)] * 4
    shapes += [(width, hidden_own // 2)] * 8
    shapes += [(width, width // 2)] * 2
    shapes += [(width, wide)] * (2 * heads)
    peers = [False, False, True, True] * 3 + [False, False] + [False, True] * heads
    plans = []
    for i, ((rows, columns), peer) in enumerate(zip(shapes, peers)):
        if chained(bits):
            plans.append(Chain(rows // 4, columns, peer, i not in WHOLE_FIRST))
        else:
            order = order_b if i % 4 == 2 else order_a
            plans.append(Reduce(order, rows >> bits, columns, peer))
    rows = (span, width)
    part = (2, half, width)
    lefts = (2, 2) if chained(bits) else (2,) * bits
    cuts = 2 ** len(lefts)

    def like(a):
        return pltpu.VMEM(a.shape, a.dtype)

    spots = Spots(
        cot=[like(a) for a in given.cot],
        hidden=like(given.hidden),
        gate_grad=like(given.gate_grad),
        up_grad=like(given.up_grad),
        two=[like(a) for a in given.two],
        near=like(given.near),
        out_own=pltpu.VMEM((2, heads * hw, width), BF16),
        proj=like(given.proj),
        core_in=pltpu.VMEM(part, BF16),
        core_own=pltpu.VMEM(part, BF16),
        sum=pltpu.VMEM(part, BF16),
        side_in=pltpu.VMEM(part, BF16),
        mid=pltpu.VMEM(part, F32),
        mid_grad=pltpu.VMEM(part[1:], F32),
        branch=pltpu.VMEM((2,) + rows, BF16),
        heads_grad=pltpu.VMEM((heads, span, hw), BF16),
        feed_out=pltpu.VMEM(part[1:], BF16),
        feed_in=pltpu.VMEM(part[1:], BF16),
        aw=pltpu.VMEM((2, width, wide), BF16),
        dproj=pltpu.VMEM((heads, span, wide), BF16),
        logit=pltpu.VMEM((1, span, 1), F32),
        dlogit=pltpu.VMEM((1, span, 1), F32),
        dkern=pltpu.VMEM((heads, KCONV, hw), F32),
        kept=[pltpu.VMEM((1,) + a.shape[1:], a.dtype) for a in given.kept],
        left_hidden=pltpu.VMEM(lefts + (hidden_own // cuts, span), BF16),
        left=pltpu.VMEM((2,) + lefts + (width // cuts, span), BF16),
        small=pltpu.VMEM((bits + 1, SMALL, 128), F32),
        small_in=pltpu.VMEM((bits + 1, SMALL, 128), F32),
        beta_out=pltpu.VMEM((2, 8, width), F32),
        beta_in=pltpu.VMEM((8, width), F32),
        local_sem=pltpu.SemaphoreType.DMA((64,)),
        send_sem=pltpu.SemaphoreType.DMA((64,)),
        recv_sem=pltpu.SemaphoreType.DMA((64,)),
    )
    more = [s for plan in plans for s in plan.scratch()]
    seen = {}
    deep = depths(bits)[1]
    for plan in plans:
        key = (plan.rows, plan.columns)
        if plan.rotating():
            seen[key] = seen.get(key, 0) + 1
            if seen[key] <= deep:
                more += plan.rotating()
    out_shapes = [
        (2,) + lefts + (hidden_own // cuts, width),
        lefts + (width // cuts, 2 * hidden_own),
        lefts + (width // cuts, 2 * hidden_own),
        lefts + (width // cuts, width),
        (2 * heads,) + lefts + (width // cuts, wide),
    ]
    any_spec = pl.BlockSpec(memory_space=pl.ANY)
    vmem_spec = pl.BlockSpec(memory_space=pltpu.VMEM)
    specs = jax.tree.map(lambda _: any_spec, given)
    specs = specs._replace(
        rinv_one=vmem_spec,
        rinv_two=vmem_spec,
        gains=[vmem_spec] * 2,
        kern=vmem_spec,
        beta=[vmem_spec] * 2,
    )
    return pl.pallas_call(
        functools.partial(back_body, bits, plans),
        in_specs=[specs],
        out_specs=[[any_spec] * 5, any_spec, any_spec, vmem_spec],
        out_shape=[
            [jax.ShapeDtypeStruct(shape, BF16) for shape in out_shapes],
            jax.ShapeDtypeStruct(rows, BF16),
            jax.ShapeDtypeStruct(rows, BF16),
            jax.ShapeDtypeStruct((SMALL, 128), F32),
        ],
        scratch_shapes=[spots, more],
        compiler_params=pltpu.CompilerParams(
            collective_id=0, has_side_effects=True, vmem_limit_bytes=62 * 2**20
        ),
        name="backward_all",
    )(given)


class Front(NamedTuple):
    inputs: Any
    cot: Any
    attn_all: Any
    out: Any
    gate: Any
    up: Any
    down: Any
    beta: Any
    gains: Any
    kern: Any
    lengths: Any


class Made(NamedTuple):
    part: Any
    feed: Any
    cot: Any
    hidden: Any
    gate_grad: Any
    up_grad: Any
    two: Any
    mid: Any
    rinv_one: Any
    rinv_two: Any
    gains: Any
    near: Any
    proj: Any
    logit: Any
    kept: Any
    act: Any
    x: Any
    out: Any
    attn: Any
    beta: Any


class Rooms(NamedTuple):
    x: Any
    cot: Any
    attn: Any
    out: Any
    out_far: Any
    gate: Any
    up: Any
    down: Any
    act: Any
    two: Any
    mid: Any
    proj: Any
    logit: Any
    attended: Any
    near: Any
    far: Any
    hidden: Any
    gate_grad: Any
    up_grad: Any
    slope: Any
    silu: Any
    part: Any
    feed: Any
    kept: Any
    local_sem: Any
    send_sem: Any
    recv_sem: Any


class Fetch:
    def __init__(self, links, group, bit_of, source, target, rows):
        self.links, self.source, self.target = links, source, target
        self.eighth = rows // 8
        self.bit_of = bit_of
        self.first, self.second = (group_peer(group, bit_of, b) for b in range(2))

    def chunk(self, one, two, which, count=1):
        start = ((one * 2 + two) * 2 + which) * self.eighth
        return pl.ds(pl.multiple_of(start, self.eighth), count * self.eighth)

    def start(self):
        rows = self.chunk(self.bit_of[0], self.bit_of[1], 0, 2)
        self.straight = self.links.start(flipped("wd"), self.source(rows), self.target(rows))
        return self

    def pass_on(self):
        self.straight.wait()
        self.sent = []
        for which in range(2):
            ref = self.target(self.chunk(self.bit_of[0], self.bit_of[1], which))
            for device in (self.first, self.second):
                self.sent.append(self.links.start(device, ref, ref))
        return self

    def pass_far(self):
        self.sent[0].wait()
        ref = self.target(self.chunk(1 - self.bit_of[0], self.bit_of[1], 0))
        self.sent.append(self.links.start(self.second, ref, ref))
        self.sent[3].wait()
        ref = self.target(self.chunk(self.bit_of[0], 1 - self.bit_of[1], 1))
        self.sent.append(self.links.start(self.first, ref, ref))
        return self

    def end(self):
        for i in (1, 2, 4, 5):
            self.sent[i].wait()


def front_body(bits, r, out, v):
    group, bit_of = own_bits(bits)
    core, side = lax.axis_index("tp"), lax.axis_index("wd")
    span, width = r.inputs.shape
    half = span // 2
    heads, hw = r.kern.shape[0], r.kern.shape[-1]
    own_width = heads * hw
    hidden_own = v.hidden.shape[1]
    model = 2 * width
    mine = pl.ds(pl.multiple_of(core * half, half), half)
    loads = Loads(v.local_sem)
    links = Links(v.send_sem, v.recv_sem)
    x_peer, c_peer = flipped("wd"), flipped("tp")
    own_cols = pl.ds(pl.multiple_of(side * hidden_own, hidden_own), hidden_own)
    other_cols = pl.ds(pl.multiple_of((1 - side) * hidden_own, hidden_own), hidden_own)

    barrier = pltpu.get_barrier_semaphore()
    for device in [group_peer(group, bit_of, b) for b in range(2)] + [x_peer, c_peer]:
        pl.semaphore_signal(barrier, inc=1, device_id=device, device_id_type=MESH)
    pl.semaphore_wait(barrier, 4)

    def fetch(source, target, rows):
        return Fetch(links, group, bit_of, source, target, rows)

    def down_rows(rows):
        start = (1 - side) * hidden_own + rows.start
        return r.down.at[pl.ds(pl.multiple_of(start, rows.size), rows.size)]

    attn = [
        fetch(
            lambda rows, h=h: r.attn_all.at[(1 - side) * heads + h, rows],
            lambda rows, h=h: v.attn[1].at[h, rows],
            width,
        )
        for h in range(heads)
    ]
    out_w = fetch(lambda rows: r.out.at[rows], lambda rows: v.out[1].at[rows], width)
    gate_w = fetch(lambda rows: r.gate.at[rows, other_cols], lambda rows: v.gate[1].at[rows], width)
    up_w = fetch(lambda rows: r.up.at[rows, other_cols], lambda rows: v.up[1].at[rows], width)
    down_w = fetch(down_rows, lambda rows: v.down[1].at[rows], hidden_own)

    attn[0].start()
    x_half = links.start(x_peer, r.inputs.at[mine], v.x[1].at[mine])
    tiny = [links.start(x_peer, r.beta, out.beta), links.start(x_peer, r.gains, out.gains)]
    attn[1].start()
    attn[2].start()
    out_w.start()
    gate_w.start()
    got_x = loads.start(r.inputs, v.x[0])
    got_attn = [loads.start(r.attn_all.at[side * heads + h], v.attn[0].at[h]) for h in range(heads)]
    got_rest = loads.start(r.out, v.out[0])
    got_rest += loads.start(r.gate.at[:, own_cols], v.gate[0])
    got_rest += loads.start(r.up.at[:, own_cols], v.up[0])
    got_rest += loads.start(r.down.at[own_cols], v.down[0])
    got_rest += loads.start(r.cot, v.cot[0])
    out_far = [links.start(c_peer, r.out, v.out_far[0])]
    given = []

    attn[0].pass_on()
    x_half.wait()
    x_rest = links.start(c_peer, v.x[1].at[mine], v.x[1].at[mine])
    settle(tiny)
    settle(got_x)
    x_rest.wait()
    up_w.start()
    attn[0].pass_far()
    given += loads.start(v.x[1], out.x)
    xs = [v.x[i][...].astype(F32) for i in range(2)]
    square = sum(jnp.sum(x * x, -1, keepdims=True) for x in xs)
    rinv = lax.rsqrt(square / model + norm_eps)
    out.rinv_one[...] = rinv
    for i, gains in enumerate((r.gains, out.gains)):
        v.act[i][...] = (xs[i] * rinv * gains[0:1, :]).astype(BF16)
        given += loads.start(v.act[i], out.act[i])
    logits = dotb(v.act[0][...], r.beta[...], NT) + dotb(v.act[1][...], out.beta[...], NT)
    for h in range(heads):
        v.logit[h] = jnp.where(side == 0, logits[:, h : h + 1], logits[:, heads + h : heads + h + 1])
    given += loads.start(v.logit, out.logit)
    attn[1].pass_on()
    cot_half = []
    near_in, far_in = [], []
    saved = [[], []]
    before = [
        [attn[1].pass_far, attn[2].pass_on, down_w.start],
        [out_w.pass_far, gate_w.pass_on],
        [gate_w.pass_far, up_w.pass_on],
    ]
    afterwards = [
        [attn[2].pass_far, out_w.pass_on],
        [lambda: cot_half.append(links.start(x_peer, r.cot.at[mine], v.cot[1].at[mine]))],
        [up_w.pass_far, down_w.pass_on],
    ]
    for h in range(heads):
        attn[h].end()
        given += loads.start(v.attn[1].at[h], out.attn.at[h])
        settle(got_attn[h])
        value = dotb(v.act[0][...], v.attn[0][h]) + dotb(v.act[1][...], v.attn[1][h])
        v.proj[h] = value.astype(BF16)
        for step in before[h]:
            step()
        kept = v.kept[h % 2]
        settle(saved[h % 2])
        forward_body(
            r.lengths,
            v.proj.at[h],
            v.logit.at[pl.ds(h, 1)],
            r.kern.at[pl.ds(h, 1)],
            v.attended.at[h],
            kept[0],
            kept[1],
            kept[2],
        )
        saved[h % 2] += [
            loads.start(a, b.at[pl.ds(h, 1)])[0] for a, b in zip(kept, out.kept)
        ]
        place = pl.ds(pl.multiple_of((side * heads + h) * hw, hw), hw)
        v.near[:, place] = v.attended[h]
        near_in.append(links.start(x_peer, v.near.at[:, place], v.near.at[:, place]))
        far_in.append(links.start(c_peer, v.near.at[:, place], v.far.at[:, place]))
        for step in afterwards[h]:
            step()
    given += loads.start(v.proj, out.proj)
    out_w.end()
    out_far.append(links.start(c_peer, v.out[1], v.out_far[1]))
    given += loads.start(v.out[1], out.out)
    for h in range(heads):
        near_in[h].wait()
        place = pl.ds(pl.multiple_of(((1 - side) * heads + h) * hw, hw), hw)
        far_in.append(links.start(c_peer, v.near.at[:, place], v.far.at[:, place]))
    given += loads.start(v.near, out.near)
    cot_half[0].wait()
    cot_rest = links.start(c_peer, v.cot[1].at[mine], v.cot[1].at[mine])
    settle(far_in)
    settle(out_far)
    settle(got_rest)

    def branch_rows(j, _):
        rows = pl.ds(pl.multiple_of(j * 256, 256), 256)
        near, far = v.near[rows, :], v.far[rows, :]
        mids = [
            v.x[i][rows, :].astype(F32) + dotb(near, v.out[i][...]) + dotb(far, v.out_far[i][...])
            for i in range(2)
        ]
        square = sum(jnp.sum(m * m, -1, keepdims=True) for m in mids)
        rinv = lax.rsqrt(square / model + norm_eps)
        out.rinv_two[rows, :] = rinv
        for i, gains in enumerate((r.gains, out.gains)):
            v.mid[i][rows, :] = mids[i]
            v.two[i][rows, :] = (mids[i] * rinv * gains[1:2, :]).astype(BF16)
        return 0

    lax.fori_loop(0, span // 256, branch_rows, 0)
    for i in range(2):
        given += loads.start(v.mid[i], out.mid[i])
        given += loads.start(v.two[i], out.two[i])
    down_w.pass_far()
    gate_w.end()
    up_w.end()

    def hidden_columns(j, _):
        cols = pl.ds(pl.multiple_of(j * 256, 256), 256)
        two = [t[...] for t in v.two]
        gate = dotb(two[0], v.gate[0][:, cols]) + dotb(two[1], v.gate[1][:, cols])
        up = dotb(two[0], v.up[0][:, cols]) + dotb(two[1], v.up[1][:, cols])
        sigma = jax.nn.sigmoid(gate)
        silu = gate * sigma
        v.hidden[:, cols] = (silu * up).astype(BF16)
        v.slope[:, cols] = up * sigma * (1.0 + gate * (1.0 - sigma))
        v.silu[:, cols] = silu
        return 0

    lax.fori_loop(0, hidden_own // 256, hidden_columns, 0)
    def feed_columns(i):
        def columns(j, _):
            cols = pl.ds(pl.multiple_of(j * 256, 256), 256)
            v.feed[i][:, cols] = dotb(v.hidden[...], v.down[i][:, cols]).astype(BF16)
            return 0

        lax.fori_loop(0, width // 256, columns, 0)

    feed_columns(0)
    given += loads.start(v.feed[0], out.feed[0])
    cot_rest.wait()
    given += loads.start(v.cot[1], out.cot)
    down_w.end()

    def grad_columns(j, _):
        cols = pl.ds(pl.multiple_of(j * 256, 256), 256)
        grad = dotb(v.cot[0][...], v.down[0][cols, :], NT)
        grad = grad + dotb(v.cot[1][...], v.down[1][cols, :], NT)
        v.gate_grad[:, cols] = (grad * v.slope[:, cols]).astype(BF16)
        v.up_grad[:, cols] = (grad * v.silu[:, cols]).astype(BF16)
        return 0

    lax.fori_loop(0, hidden_own // 256, grad_columns, 0)
    given += loads.start(v.hidden, out.hidden)
    given += loads.start(v.gate_grad, out.gate_grad)
    given += loads.start(v.up_grad, out.up_grad)
    for i in range(2):

        def model_columns(j, _, i=i):
            cols = pl.ds(pl.multiple_of(j * 256, 256), 256)
            value = dotb(v.gate_grad[...], v.gate[i][cols, :], NT)
            value = value + dotb(v.up_grad[...], v.up[i][cols, :], NT)
            v.part[i][:, cols] = value.astype(BF16)
            return 0

        lax.fori_loop(0, width // 256, model_columns, 0)
        given += loads.start(v.part[i], out.part[i])
    feed_columns(1)
    given += loads.start(v.feed[1], out.feed[1])
    settle(saved[0])
    settle(saved[1])
    settle(given)


def forward_all(bits, front):
    span, width = front.inputs.shape
    heads, hw = front.kern.shape[0], front.kern.shape[-1]
    wide = 4 * hw
    hidden_own = front.gate.shape[1] // 2
    rows = (span, width)
    kept = [(3, 2, HALF, HALF), (3, 2, HALF, HALF), (3, HALF, HALF)]

    def room(shape, dtype=BF16):
        return pltpu.VMEM(shape, dtype)

    def twice(shape, dtype=BF16):
        return [room(shape, dtype) for _ in range(2)]

    rooms = Rooms(
        x=twice(rows),
        cot=twice(rows),
        attn=twice((heads, width, wide)),
        out=twice((2 * heads * hw, width)),
        out_far=twice((2 * heads * hw, width)),
        gate=twice((width, hidden_own)),
        up=twice((width, hidden_own)),
        down=twice((hidden_own, width)),
        act=twice(rows),
        two=twice(rows),
        mid=twice(rows, F32),
        proj=room((heads, span, wide)),
        logit=room((heads, span, 1), F32),
        attended=room((heads, span, hw)),
        near=room((span, 2 * heads * hw)),
        far=room((span, 2 * heads * hw)),
        hidden=room((span, hidden_own)),
        gate_grad=room((span, hidden_own)),
        up_grad=room((span, hidden_own)),
        slope=room((span, hidden_own), F32),
        silu=room((span, hidden_own), F32),
        part=twice(rows),
        feed=twice(rows),
        kept=[[room((1,) + shape) for shape in kept] for _ in range(2)],
        local_sem=pltpu.SemaphoreType.DMA((64,)),
        send_sem=pltpu.SemaphoreType.DMA((96,)),
        recv_sem=pltpu.SemaphoreType.DMA((96,)),
    )

    def give(shape, dtype=BF16):
        return jax.ShapeDtypeStruct(shape, dtype)

    made = Made(
        part=[give(rows)] * 2,
        feed=[give(rows)] * 2,
        cot=give(rows),
        hidden=give((span, hidden_own)),
        gate_grad=give((span, hidden_own)),
        up_grad=give((span, hidden_own)),
        two=[give(rows)] * 2,
        mid=[give(rows, F32)] * 2,
        rinv_one=give((span, 1), F32),
        rinv_two=give((span, 1), F32),
        gains=give((2, width), F32),
        near=give((span, 2 * heads * hw)),
        proj=give((heads, span, wide)),
        logit=give((heads, span, 1), F32),
        kept=[give((heads,) + shape) for shape in kept],
        act=[give(rows)] * 2,
        x=give(rows),
        out=give((2 * heads * hw, width)),
        attn=give((heads, width, wide)),
        beta=give(front.beta.shape),
    )
    any_spec = pl.BlockSpec(memory_space=pl.ANY)
    vmem_spec = pl.BlockSpec(memory_space=pltpu.VMEM)
    specs = jax.tree.map(lambda _: any_spec, front)
    specs = specs._replace(
        beta=vmem_spec,
        gains=vmem_spec,
        kern=vmem_spec,
        lengths=pl.BlockSpec(memory_space=pltpu.SMEM),
    )
    out_specs = jax.tree.map(lambda _: any_spec, made)
    out_specs = out_specs._replace(
        rinv_one=vmem_spec, rinv_two=vmem_spec, gains=vmem_spec, beta=vmem_spec
    )
    return pl.pallas_call(
        functools.partial(front_body, bits),
        in_specs=[specs],
        out_specs=[out_specs],
        out_shape=[made],
        scratch_shapes=[rooms],
        compiler_params=pltpu.CompilerParams(
            collective_id=1, has_side_effects=True, vmem_limit_bytes=62 * 2**20
        ),
        name="forward_all",
    )(front)[0]


def on_device(
    group_count,
    inputs,
    lengths,
    gain_attn,
    attn_proj,
    beta_proj,
    conv_kernel,
    out_proj,
    gain_ffn,
    gate_proj,
    up_proj,
    down_proj,
    cotangent,
):
    width = inputs.shape[1]
    heads, hw = conv_kernel.shape[1], conv_kernel.shape[2]
    bits = group_count.bit_length() - 1
    attn_all = jnp.transpose(attn_proj, (1, 0, 2))
    out_rows = out_proj.reshape(-1, width)
    kern = jnp.transpose(conv_kernel, (1, 0, 2))
    beta_rows = beta_proj.T
    gains = jnp.stack([gain_attn, gain_ffn])
    made = forward_all(
        bits,
        Front(
            inputs=inputs,
            cot=cotangent,
            attn_all=attn_all,
            out=out_rows,
            gate=gate_proj,
            up=up_proj,
            down=down_proj,
            beta=beta_rows,
            gains=gains,
            kern=kern,
            lengths=lengths,
        ),
    )
    given = Given(
        part=made.part,
        feed=made.feed,
        cot=[cotangent, made.cot],
        hidden=made.hidden,
        gate_grad=made.gate_grad,
        up_grad=made.up_grad,
        two=made.two,
        mid=made.mid,
        rinv_one=made.rinv_one,
        rinv_two=made.rinv_two,
        gains=[gains, made.gains],
        near=made.near,
        out=[out_rows, made.out],
        proj=made.proj,
        logit=made.logit,
        kern=kern,
        kept=made.kept,
        act=made.act,
        x=[inputs, made.x],
        attn_all=attn_all,
        attn_peer=made.attn,
        beta=[beta_rows, made.beta],
    )
    (down_sum, gate_sum, up_sum, out_sum, attn_sum), outputs, grad_inputs, small = backward_all(
        bits, given
    )
    rows = width // 128
    gain_one_sum = small[0:rows].reshape(-1)
    gain_two_sum = small[8 : 8 + rows].reshape(-1)
    at = 16 + 2 * heads * rows
    beta_sum = small[16:at].reshape(2, heads, width)
    beta_sum = jnp.where(lax.axis_index("wd") == 0, beta_sum, beta_sum[::-1])
    beta_sum = beta_sum.reshape(2 * heads, width).T
    kern_sum = small[at : at + KCONV * heads].reshape(heads, KCONV, hw)
    attn_sum = attn_sum.reshape(2 * heads, width, -1)
    return (
        outputs,
        grad_inputs,
        gain_one_sum,
        jnp.transpose(attn_sum, (1, 0, 2)).astype(F32),
        beta_sum,
        jnp.transpose(kern_sum, (1, 0, 2)),
        out_sum.astype(F32).reshape(out_proj.shape),
        gain_two_sum,
        gate_sum.astype(F32).reshape(gate_proj.shape),
        up_sum.astype(F32).reshape(up_proj.shape),
        down_sum.astype(F32).reshape(down_proj.shape),
    )


def solution(mesh):
    return jax.shard_map(
        functools.partial(on_device, mesh.shape["dp"]),
        mesh=mesh,
        in_specs=(
            P("dp", "wd"),
            P("dp"),
            P("wd"),
            P("wd", "tp", None),
            P("wd", "tp"),
            P(None, ("tp", "wd"), None),
            P("tp", None, "wd"),
            P("wd"),
            P("wd", "tp"),
            P("wd", "tp"),
            P("tp", "wd"),
            P("dp", "wd"),
        ),
        out_specs=(
            P("dp", "wd"),
            P("dp", "wd"),
            P("wd"),
            P("wd", "tp", None),
            P("wd", "tp"),
            P(None, ("tp", "wd"), None),
            P("tp", None, "wd"),
            P("wd"),
            P("wd", "tp"),
            P("wd", "tp"),
            P("tp", "wd"),
        ),
        check_vma=False,
    )
```
